32 devices in a mesh: rep: 4 (over x, core), shard: 8 (over z, y).
Axes of the slice: x: 2, y: 2, z: 4, core: 2. Of those that a mesh axis runs over, the one named last changes fastest.
Arguments:
- tokens: bfloat16 [8192, 1024], P(('rep', 'shard')), may hold values from -6 to 6
- norm_attn: bfloat16 [1024], P('shard'), may hold values from 0.099609375 to 1.8984375
- w_query: bfloat16 [1024, 1024], P('shard'), may hold values from -0.375 to 0.375
- w_latent: bfloat16 [1024, 512], P('shard'), may hold values from -0.1875 to 0.1875
- w_key_up: bfloat16 [2, 256, 512], P(None, 'shard'), may hold values from -0.375 to 0.375
- w_value_up: bfloat16 [2, 256, 512], P(None, 'shard'), may hold values from -0.375 to 0.375
- w_out: bfloat16 [1024, 1024], P(None, 'shard'), may hold values from -0.75 to 0.75
- norm_ffn: bfloat16 [1024], P('shard'), may hold values from 0.099609375 to 1.8984375
- w_gate: bfloat16 [1024, 2816], P('shard'), may hold values from -0.1875 to 0.1875
- w_up: bfloat16 [1024, 2816], P('shard'), may hold values from -0.1875 to 0.1875
- w_down: bfloat16 [2816, 1024], P('shard'), may hold values from -0.109375 to 0.109375
- cotangent: bfloat16 [8192, 1024], P(('rep', 'shard')), may hold values from -6 to 6
Outputs:
- output: bfloat16 [8192, 1024], P(('rep', 'shard'))
- grad_tokens: bfloat16 [8192, 1024], P(('rep', 'shard'))
- grad_norm_attn: float32 [1024], P('shard')
- grad_w_query: float32 [1024, 1024], P('shard')
- grad_w_latent: float32 [1024, 512], P('shard')
- grad_w_key_up: float32 [2, 256, 512], P(None, 'shard')
- grad_w_value_up: float32 [2, 256, 512], P(None, 'shard')
- grad_w_out: float32 [1024, 1024], P(None, 'shard')
- grad_norm_ffn: float32 [1024], P('shard')
- grad_w_gate: float32 [1024, 2816], P('shard')
- grad_w_up: float32 [1024, 2816], P('shard')
- grad_w_down: float32 [2816, 1024], P('shard')
The draws below stay inside these ranges and needn't reach their ends.
All inputs are finite; a program needn't handle non-finite values.
Results may differ from the reference program's by a relative error of at most 0.018.
Values may be sent and summed in bfloat16 or wider, within the bound.
No kernel may reach another device: no remote copies, remote signals or barrier semaphores. Data moves between devices by JAX's collectives and lax.ppermute only.
A program may use at most 192 MiB of HBM per device.

```python
import math
import jax
import jax.numpy as jnp
from jax import lax

D = 1024
HQ = 16
HD = 64
LG = 2
LAT = 256
FF = 2816
SEQ_LEN = 256
TOKENS = 8192


def with_spikes(entries, key, source, target, blocks, factor):
    owner, partner = [(jnp.arange(entries.shape[dim]) // (entries.shape[dim] // blocks)).reshape([-1 if axis == dim else 1 for axis in range(entries.ndim)]) for dim in (source, target)]
    chosen = jax.random.permutation(key, blocks)[partner]
    strong = (owner == chosen) | (owner == (partner + blocks // 2) % blocks)
    return jnp.where(strong, factor * entries, entries)


def block_levels(stream_key, shape, cuts, low, high):
    loudness = 1.0
    for axis_at, blocks in cuts:
        heights = jax.random.uniform(jax.random.fold_in(jax.random.fold_in(stream_key, 6), axis_at), (blocks,), jnp.float32, low / len(cuts), high / len(cuts))
        loudness = loudness * jnp.repeat(jnp.exp(heights), shape[axis_at] // blocks).reshape((-1,) + (1,) * (len(shape) - 1 - axis_at))
    return loudness


def centred(key, dims, deviation, limit, pieces=(), dtype=jnp.bfloat16):
    gain = block_levels(key, dims, pieces, -0.22, 0.18) if pieces else 1.0
    values = jax.random.normal(key, dims, jnp.float32) * deviation * gain
    return jnp.minimum(jnp.maximum(values, -limit), limit).astype(dtype)


def gaussian_with(own_key, dims, scale, reach, pieces, heavy, dtype=jnp.bfloat16):
    array = scale * jax.random.normal(own_key, dims, jnp.float32)
    if pieces:
        array = array * block_levels(own_key, dims, pieces, -0.22, 0.18)
    return jnp.clip(with_spikes(array, jax.random.fold_in(own_key, 3), *heavy), -reach, reach).astype(dtype)


def setup_inputs(seed: int = 0) -> dict:
    splits = jax.random.split(jax.random.key(seed), 13)
    return {
        "tokens": centred(splits[0], (TOKENS, D), 1.0, 6.0, ((0, 32),)),
        "norm_attn": jnp.clip(1.0 + 0.18 * jax.random.normal(splits[1], (D,), jnp.float32), 0.099609375, 1.8984375).astype(jnp.bfloat16),
        "w_query": centred(splits[2], (D, HQ * HD), (D // 4) ** -0.5, 0.375, ((0, 8),)),
        "w_latent": centred(splits[3], (D, LG * LAT), D ** -0.5, 0.1875, ((0, 8),)),
        "w_key_up": centred(splits[4], (LG, LAT, HQ * HD // LG), LAT ** -0.5, 0.375, ((1, 8),)),
        "w_value_up": centred(splits[5], (LG, LAT, HQ * HD // LG), LAT ** -0.5, 0.375, ((1, 8),)),
        "w_out": centred(splits[6], (HQ * HD, D), (HQ * HD // 16) ** -0.5, 0.75, ((1, 8),)),
        "norm_ffn": jnp.clip(1.0 + 0.18 * jax.random.normal(splits[7], (D,), jnp.float32), 0.099609375, 1.8984375).astype(jnp.bfloat16),
        "w_gate": centred(splits[8], (D, FF), D ** -0.5, 0.1875, ((0, 8),)),
        "w_up": centred(splits[9], (D, FF), D ** -0.5, 0.1875, ((0, 8),)),
        "w_down": centred(splits[10], (FF, D), FF ** -0.5, 0.109375, ((0, 8),)),
        "cotangent": gaussian_with(splits[11], (TOKENS, D), 1.0, 6.0, ((0, 32),), (0, 1, 32, 2.75)),
    }


@jax.custom_vjp
def low(v):
    return lax.optimization_barrier(v.astype(jnp.bfloat16)).astype(jnp.float32)

@jax.custom_vjp
def low_back(v):
    return v

def low_keep(v):
    return (low(v), None)

def low_pass(kept, grad):
    return (grad,)

def back_keep(v):
    return (v, None)

def back_low(kept, grad):
    return (low(grad),)
low.defvjp(low_keep, low_pass)
low_back.defvjp(back_keep, back_low)
epsilon = 1e-05
highest = lax.Precision.HIGHEST

def rms_scale(rows_in):
    return lax.rsqrt(lax.optimization_barrier(jnp.mean(rows_in * rows_in, axis=-1, keepdims=True)) + epsilon)

def attention(queries, latents, w_key_up, w_value_up):
    length = queries.shape[0]
    grouped = latents.reshape(length, LG, LAT)
    key_heads = low_back(low(jnp.einsum('tgl,glk->tgk', grouped, w_key_up, precision=highest))).reshape(length, HQ, HD)
    value_heads = low_back(low(jnp.einsum('tgl,glk->tgk', grouped, w_value_up, precision=highest))).reshape(length, HQ, HD)
    query_heads = queries.reshape(length, HQ, HD)
    scores = low_back(jnp.einsum('qhd,khd->hqk', query_heads, key_heads, precision=highest) * HD ** (-0.5))
    row_ids = lax.broadcasted_iota(jnp.int32, (length, length), 0)
    col_ids = lax.broadcasted_iota(jnp.int32, (length, length), 1)
    scores = jnp.where(col_ids <= row_ids, scores, -1e+30)
    attn_probs = jax.nn.softmax(scores, axis=-1)
    mixed_heads = jnp.einsum('hqk,khd->qhd', low(attn_probs), value_heads, precision=highest)
    return mixed_heads.reshape(length, HQ * HD)

def layer_block(rows_in, params):
    norm_attn, w_query, w_latent, w_key_up, w_value_up, w_out, norm_ffn, w_gate, w_up, w_down = params
    normed_attn = low(rows_in * rms_scale(rows_in) * norm_attn)
    queries = low_back(low(jnp.dot(normed_attn, w_query, precision=highest)))
    latents = low_back(low(jnp.dot(normed_attn, w_latent, precision=highest)))
    seq_count = rows_in.shape[0] // SEQ_LEN
    mixed_heads = jax.vmap(attention, in_axes=(0, 0, None, None))(queries.reshape(seq_count, SEQ_LEN, HQ * HD), latents.reshape(seq_count, SEQ_LEN, LG * LAT), w_key_up, w_value_up)
    mixed_heads = low_back(low(mixed_heads.reshape(rows_in.shape[0], HQ * HD)))
    attn_out = low_back(jnp.dot(mixed_heads, w_out, precision=highest))
    residual = rows_in + attn_out
    normed_ffn = low(residual * rms_scale(residual) * norm_ffn)
    gate_proj = low_back(jnp.dot(normed_ffn, w_gate, precision=highest))
    up_proj = low_back(jnp.dot(normed_ffn, w_up, precision=highest))
    activated = low(jax.nn.silu(gate_proj) * up_proj)
    ffn_out = low_back(jnp.dot(activated, w_down, precision=highest))
    return residual + ffn_out

def layer(inputs, params):
    seq_total = TOKENS // SEQ_LEN
    per_block = math.gcd(seq_total, max(1, 4096 // SEQ_LEN))
    block_count = seq_total // per_block
    blocks = inputs.reshape(block_count, per_block * SEQ_LEN, D)
    results = lax.map(jax.checkpoint(lambda block_rows: layer_block(block_rows, params)), blocks)
    return results.reshape(TOKENS, D)

def reference(tokens, norm_attn, w_query, w_latent, w_key_up, w_value_up, w_out, norm_ffn, w_gate, w_up, w_down, cotangent):
    params = tuple((item.astype(jnp.float32) for item in (norm_attn, w_query, w_latent, w_key_up, w_value_up, w_out, norm_ffn, w_gate, w_up, w_down)))
    inputs = tokens.astype(jnp.float32)
    result, pullback = jax.vjp(layer, inputs, params)
    grad_inputs, grad_params = pullback(cotangent.astype(jnp.float32))
    return (result.astype(jnp.bfloat16), grad_inputs.astype(jnp.bfloat16), grad_params[0], grad_params[1], grad_params[2], grad_params[3], grad_params[4], grad_params[5], grad_params[6], grad_params[7], grad_params[8], grad_params[9])
```

```python
import jax
import jax.numpy as jnp
from jax import lax
from jax.sharding import PartitionSpec as P

HQ = 16
HD = 64
LG = 2
LAT = 256
SEQ = 256
R = 4
f32 = jnp.float32
bf16 = jnp.bfloat16
epsilon = 1e-05


def rms_scale(rows_in):
    return lax.rsqrt(jnp.mean(rows_in * rows_in, axis=-1, keepdims=True) + epsilon)


def dot_nn(a, b):
    return lax.dot_general(a, b, (((1,), (0,)), ((), ())), preferred_element_type=f32)


def dot_nt(a, b):
    return lax.dot_general(a, b, (((1,), (1,)), ((), ())), preferred_element_type=f32)


def dot_tn(a, b):
    return lax.dot_general(a, b, (((0,), (0,)), ((), ())), preferred_element_type=f32)


def make_layer(mesh):
    S = mesh.shape["shard"]
    Z = S // 2
    assert mesh.shape["rep"] == R

    def flip_core(v):
        return lax.ppermute(v, "rep", [(i, i ^ 1) for i in range(R)])

    def flip_x(v):
        return lax.ppermute(v, "rep", [(i, i ^ 2) for i in range(R)])

    def flip_y(v):
        return lax.ppermute(v, "shard", [(i, i ^ 1) for i in range(S)])

    def rot_z(v, k):
        return lax.ppermute(v, "shard", [(i, (i + 2 * k) % S) for i in range(S)])

    def layer(
        tokens,
        norm_attn,
        w_query,
        w_latent,
        w_key_up,
        w_value_up,
        w_out,
        norm_ffn,
        w_gate,
        w_up,
        w_down,
        cotangent,
    ):
        r = lax.axis_index("rep")
        s = lax.axis_index("shard")
        x, c, z, y = r // 2, r % 2, s // 2, s % 2
        T, D = tokens.shape
        n_d = w_query.shape[0]
        n_l = w_key_up.shape[1]
        n_f = w_down.shape[0] // R
        q_c = w_query.shape[1] // R
        FFq = n_f * S

        def gather_rep(v):
            far = flip_x(v)
            near = flip_core(jnp.stack([v, far]))
            return jnp.stack([v, near[0], far, near[1]])

        def scatter_rep(v):
            near = flip_core(v[1::2].astype(bf16))
            chip = v[0::2] + near
            far = flip_x(chip[1].astype(bf16))
            return chip[0] + far

        def absolute(v):
            v = jnp.where(c == 1, v[jnp.array([1, 0, 3, 2])], v)
            return jnp.where(x == 1, v[jnp.array([2, 3, 0, 1])], v)

        def gather_shard(v):
            full = jnp.zeros((Z, 2) + v.shape, v.dtype)
            zeros = (0,) * v.ndim
            for k in range(Z):
                piece = v if k == 0 else rot_z(v, k)
                other = flip_y(piece)
                at = lax.rem(z - k + Z, Z)
                full = lax.dynamic_update_slice(full, piece[None, None], (at, y) + zeros)
                full = lax.dynamic_update_slice(full, other[None, None], (at, 1 - y) + zeros)
            return full.reshape((S,) + v.shape)

        def scatter_shard(v):
            v = v.reshape((Z, 2) + v.shape[1:])
            mine = lax.dynamic_index_in_dim(v, y, 1, False)
            give = lax.dynamic_index_in_dim(v, 1 - y, 1, False)
            half = (mine.astype(f32) + flip_y(give).astype(f32)).astype(bf16)
            total = lax.dynamic_index_in_dim(half, z, 0, False).astype(f32)
            for k in range(1, Z):
                piece = lax.dynamic_index_in_dim(half, lax.rem(z + k, Z), 0, False)
                total = total + rot_z(piece, k).astype(f32)
            return absolute(gather_rep(total.astype(bf16)))

        my_query = lax.dynamic_slice_in_dim(w_query, r * q_c, q_c, 1)
        my_latent = lax.dynamic_slice_in_dim(w_latent, x * LAT, LAT, 1)
        my_key = lax.dynamic_slice_in_dim(
            lax.dynamic_index_in_dim(w_key_up, x, 0, False), c * q_c, q_c, 1
        )
        my_value = lax.dynamic_slice_in_dim(
            lax.dynamic_index_in_dim(w_value_up, x, 0, False), c * q_c, q_c, 1
        )
        my_out = lax.dynamic_slice_in_dim(w_out, r * q_c, q_c, 0).T
        gains = jnp.zeros((16, q_c), bf16)
        gains = gains.at[0, :n_d].set(norm_attn).at[1, :n_d].set(norm_ffn)
        pack = jnp.concatenate([my_query, my_latent, my_key, my_value, my_out, gains], 0)
        cuts = [n_d, 2 * n_d, 2 * n_d + n_l, 2 * n_d + 2 * n_l, 3 * n_d + 2 * n_l]

        col = lax.broadcasted_iota(jnp.int32, (S * R * n_f, FFq), 1)
        row = lax.broadcasted_iota(jnp.int32, (S * R * n_f, FFq), 0)
        pick = (row == (col // n_f) * (R * n_f) + r * n_f + col % n_f).astype(bf16)
        my_gate_up = dot_nn(jnp.concatenate([w_gate, w_up], 0), pick).astype(bf16)
        my_down = lax.dynamic_slice_in_dim(w_down, r * n_f, n_f, 0)

        all_tokens = gather_rep(tokens).reshape(R * T, D)
        packs = gather_shard(pack)
        all_cot = gather_rep(cotangent).reshape(R * T, D)
        gate_up = gather_shard(my_gate_up)
        down = gather_shard(my_down).reshape(FFq, D)

        query_w = packs[:, : cuts[0]].reshape(D, q_c)
        latent_w = packs[:, cuts[0] : cuts[1]].reshape(D, LAT)
        key_w = packs[:, cuts[1] : cuts[2]].reshape(LAT, q_c)
        value_w = packs[:, cuts[2] : cuts[3]].reshape(LAT, q_c)
        out_w = packs[:, cuts[3] : cuts[4]].reshape(D, q_c)
        gain_attn = packs[:, cuts[4], :n_d].reshape(D).astype(f32)
        gain_ffn = packs[:, cuts[4] + 1, :n_d].reshape(D).astype(f32)
        gate_w = gate_up[:, :n_d].reshape(D, FFq)
        up_w = gate_up[:, n_d:].reshape(D, FFq)

        heads = q_c // HD
        group_in = all_tokens.astype(f32)
        scale_attn = rms_scale(group_in)
        normed_attn = (group_in * scale_attn * gain_attn).astype(bf16)
        queries = dot_nn(normed_attn, query_w).astype(bf16)
        latents = dot_nn(normed_attn, latent_w).astype(bf16)
        keys = dot_nn(latents, key_w).astype(bf16)
        values = dot_nn(latents, value_w).astype(bf16)
        qh = queries.reshape(R, T, heads, HD)
        kh = keys.reshape(R, T, heads, HD)
        vh = values.reshape(R, T, heads, HD)
        row_ids = lax.broadcasted_iota(jnp.int32, (SEQ, SEQ), 0)
        col_ids = lax.broadcasted_iota(jnp.int32, (SEQ, SEQ), 1)
        scores = jnp.einsum("bqhd,bkhd->bhqk", qh, kh, preferred_element_type=f32) * HD**-0.5
        scores = jnp.where(col_ids <= row_ids, scores, -1e30)
        maxima = jnp.max(scores, axis=-1, keepdims=True)
        exps = jnp.exp(scores - maxima)
        probs = exps / jnp.sum(exps, axis=-1, keepdims=True)
        low_probs = probs.astype(bf16)
        mixed = jnp.einsum("bhqk,bkhd->bqhd", low_probs, vh, preferred_element_type=f32)
        mixed = mixed.astype(bf16).reshape(R * T, q_c)
        attn_part = dot_nt(mixed, out_w).reshape(R, T, D)
        inputs = tokens.astype(f32)
        residual = inputs + scatter_rep(attn_part)
        scale_ffn = rms_scale(residual)
        normed_own = (residual * scale_ffn * gain_ffn).astype(bf16)
        normed_ffn = gather_rep(normed_own).reshape(R * T, D)

        gate_proj = dot_nn(normed_ffn, gate_w)
        up_proj = dot_nn(normed_ffn, up_w)
        sig = jax.nn.sigmoid(gate_proj)
        silu = gate_proj * sig
        activated = (silu * up_proj).astype(bf16)
        grad_down = dot_tn(activated, all_cot).astype(bf16).reshape(S, n_f, D)
        grad_act = dot_nt(all_cot, down)
        grad_gate = (grad_act * up_proj * sig * (1.0 + gate_proj * (1.0 - sig))).astype(bf16)
        grad_up = (grad_act * silu).astype(bf16)
        grad_gate_w = dot_tn(normed_ffn, grad_gate).astype(bf16).reshape(S, n_d, FFq)
        grad_up_w = dot_tn(normed_ffn, grad_up).astype(bf16).reshape(S, n_d, FFq)
        ffn_back = dot_nt(grad_gate, gate_w) + dot_nt(grad_up, up_w)
        grad_normed_ffn = scatter_rep(ffn_back.reshape(R, T, D))
        ffn_part = dot_nn(activated, down).reshape(R, T, D)
        output = (residual + scatter_rep(ffn_part)).astype(bf16)

        weighted = grad_normed_ffn * gain_ffn
        grad_residual = (
            cotangent.astype(f32)
            + scale_ffn * weighted
            - residual * scale_ffn**3 * jnp.mean(weighted * residual, axis=-1, keepdims=True)
        )
        grad_attn = gather_rep(grad_residual.astype(bf16)).reshape(R * T, D)

        grad_out_w = dot_tn(grad_attn, mixed).astype(bf16)
        grad_mixed = dot_nn(grad_attn, out_w).astype(bf16).reshape(R, T, heads, HD)
        grad_probs = jnp.einsum("bqhd,bkhd->bhqk", grad_mixed, vh, preferred_element_type=f32)
        grad_scores = (
            probs * (grad_probs - jnp.sum(probs * grad_probs, axis=-1, keepdims=True))
        ).astype(bf16)
        grad_q = jnp.einsum("bhqk,bkhd->bqhd", grad_scores, kh, preferred_element_type=f32)
        grad_k = jnp.einsum("bhqk,bqhd->bkhd", grad_scores, qh, preferred_element_type=f32)
        grad_v = jnp.einsum("bhqk,bqhd->bkhd", low_probs, grad_mixed, preferred_element_type=f32)
        grad_q = (grad_q * HD**-0.5).astype(bf16).reshape(R * T, q_c)
        grad_k = (grad_k * HD**-0.5).astype(bf16).reshape(R * T, q_c)
        grad_v = grad_v.astype(bf16).reshape(R * T, q_c)
        grad_key_w = dot_tn(latents, grad_k).astype(bf16)
        grad_value_w = dot_tn(latents, grad_v).astype(bf16)
        grad_query_w = dot_tn(normed_attn, grad_q).astype(bf16)
        lat_part = (dot_nt(grad_k, key_w) + dot_nt(grad_v, value_w)).reshape(R, T, LAT)
        near = flip_core(lat_part[1::2])
        grad_lat = (lat_part[0::2] + near).astype(bf16).reshape(2 * T, LAT)
        half_normed = normed_attn.reshape(R, T, D)[0::2].reshape(2 * T, D)
        grad_latent_w = dot_tn(half_normed, grad_lat).astype(bf16)
        attn_back = dot_nt(grad_q, query_w).reshape(R, T, D)
        lat_back = dot_nt(grad_lat, latent_w).reshape(2, T, D)
        attn_back = jnp.stack(
            [attn_back[0] + lat_back[0], attn_back[1], attn_back[2] + lat_back[1], attn_back[3]]
        )
        grad_normed_attn = scatter_rep(attn_back)
        weighted = grad_normed_attn * gain_attn
        scale_own = rms_scale(inputs)
        grad_tokens = (
            grad_residual
            + scale_own * weighted
            - inputs * scale_own**3 * jnp.mean(weighted * inputs, axis=-1, keepdims=True)
        ).astype(bf16)

        sum_down = scatter_shard(grad_down)
        sum_gate = scatter_shard(grad_gate_w)
        sum_up = scatter_shard(grad_up_w)
        grad_pack = jnp.concatenate(
            [
                grad_query_w.reshape(S, n_d, q_c),
                grad_latent_w.reshape(S, n_d, LAT),
                grad_key_w.reshape(S, n_l, q_c),
                grad_value_w.reshape(S, n_l, q_c),
                grad_out_w.reshape(S, n_d, q_c),
            ],
            1,
        )
        sum_pack = scatter_shard(grad_pack).astype(f32)
        g_query = sum_pack[:, : cuts[0]].transpose(1, 0, 2).reshape(n_d, R * q_c)
        g_latent = sum_pack[:, cuts[0] : cuts[1]]
        g_latent = jnp.concatenate([g_latent[0] + g_latent[1], g_latent[2] + g_latent[3]], 1)
        g_key = sum_pack[:, cuts[1] : cuts[2]].reshape(LG, 2, n_l, q_c)
        g_key = g_key.transpose(0, 2, 1, 3).reshape(LG, n_l, 2 * q_c)
        g_value = sum_pack[:, cuts[2] : cuts[3]].reshape(LG, 2, n_l, q_c)
        g_value = g_value.transpose(0, 2, 1, 3).reshape(LG, n_l, 2 * q_c)
        g_out = sum_pack[:, cuts[3] : cuts[4]].transpose(0, 2, 1).reshape(R * q_c, n_d)
        g_down = sum_down.reshape(R * n_f, D).astype(f32)

        def spread(v):
            v = v.reshape(R, n_d, S, n_f).transpose(1, 2, 0, 3)
            return v.reshape(n_d, S * R * n_f).astype(f32)

        g_gate = spread(sum_gate)
        g_up = spread(sum_up)
        g_norm_attn = (
            jnp.sum(g_query * w_query.astype(f32), axis=1)
            + jnp.sum(g_latent * w_latent.astype(f32), axis=1)
        ) / norm_attn.astype(f32)
        g_norm_ffn = (
            jnp.sum(g_gate * w_gate.astype(f32), axis=1) + jnp.sum(g_up * w_up.astype(f32), axis=1)
        ) / norm_ffn.astype(f32)
        return (
            output,
            grad_tokens,
            g_norm_attn,
            g_query,
            g_latent,
            g_key,
            g_value,
            g_out,
            g_norm_ffn,
            g_gate,
            g_up,
            g_down,
        )

    return layer


def solution(mesh):
    return jax.shard_map(
        make_layer(mesh),
        mesh=mesh,
        in_specs=(
            P(("rep", "shard"), None),
            P("shard"),
            P("shard", None),
            P("shard", None),
            P(None, "shard", None),
            P(None, "shard", None),
            P(None, "shard"),
            P("shard"),
            P("shard", None),
            P("shard", None),
            P("shard", None),
            P(("rep", "shard"), None),
        ),
        out_specs=(
            P(("rep", "shard"), None),
            P(("rep", "shard"), None),
            P("shard"),
            P("shard", None),
            P("shard", None),
            P(None, "shard", None),
            P(None, "shard", None),
            P(None, "shard"),
            P("shard"),
            P("shard", None),
            P("shard", None),
            P("shard", None),
        ),
        check_vma=False,
    )
```

```python
import jax
import jax.numpy as jnp
from jax import lax
from jax.experimental import pallas as pl
from jax.experimental.pallas import tpu as pltpu
from jax.sharding import PartitionSpec as P

HQ = 16
HD = 64
LG = 2
LAT = 256
SEQ = 256
R = 4
f32 = jnp.float32
bf16 = jnp.bfloat16
epsilon = 1e-05


def rms_scale(rows_in):
    return lax.rsqrt(jnp.mean(rows_in * rows_in, axis=-1, keepdims=True) + epsilon)


def dot_nn(a, b):
    return lax.dot_general(a, b, (((1,), (0,)), ((), ())), preferred_element_type=f32)


def dot_nt(a, b):
    return lax.dot_general(a, b, (((1,), (1,)), ((), ())), preferred_element_type=f32)


def dot_tn(a, b):
    return lax.dot_general(a, b, (((0,), (0,)), ((), ())), preferred_element_type=f32)


def make_plain(mesh):
    S = mesh.shape["shard"]
    Z = S // 2
    assert mesh.shape["rep"] == R

    def flip_core(v):
        return lax.ppermute(v, "rep", [(i, i ^ 1) for i in range(R)])

    def flip_x(v):
        return lax.ppermute(v, "rep", [(i, i ^ 2) for i in range(R)])

    def flip_y(v):
        return lax.ppermute(v, "shard", [(i, i ^ 1) for i in range(S)])

    def rot_z(v, k):
        return lax.ppermute(v, "shard", [(i, (i + 2 * k) % S) for i in range(S)])

    def layer(
        tokens,
        norm_attn,
        w_query,
        w_latent,
        w_key_up,
        w_value_up,
        w_out,
        norm_ffn,
        w_gate,
        w_up,
        w_down,
        cotangent,
    ):
        r = lax.axis_index("rep")
        s = lax.axis_index("shard")
        x, c, z, y = r // 2, r % 2, s // 2, s % 2
        T, D = tokens.shape
        n_d = w_query.shape[0]
        n_l = w_key_up.shape[1]
        n_f = w_down.shape[0] // R
        q_c = w_query.shape[1] // R
        FFq = n_f * S

        def gather_rep(v):
            far = flip_x(v)
            near = flip_core(jnp.stack([v, far]))
            return jnp.stack([v, near[0], far, near[1]])

        def scatter_rep(v):
            near = flip_core(v[1::2].astype(bf16))
            chip = v[0::2] + near
            far = flip_x(chip[1].astype(bf16))
            return chip[0] + far

        def absolute(v):
            v = jnp.where(c == 1, v[jnp.array([1, 0, 3, 2])], v)
            return jnp.where(x == 1, v[jnp.array([2, 3, 0, 1])], v)

        def gather_shard(v):
            full = jnp.zeros((Z, 2) + v.shape, v.dtype)
            zeros = (0,) * v.ndim
            for k in range(Z):
                piece = v if k == 0 else rot_z(v, k)
                other = flip_y(piece)
                at = lax.rem(z - k + Z, Z)
                full = lax.dynamic_update_slice(full, piece[None, None], (at, y) + zeros)
                full = lax.dynamic_update_slice(full, other[None, None], (at, 1 - y) + zeros)
            return full.reshape((S,) + v.shape)

        def scatter_shard(v):
            v = v.reshape((Z, 2) + v.shape[1:])
            mine = lax.dynamic_index_in_dim(v, y, 1, False)
            give = lax.dynamic_index_in_dim(v, 1 - y, 1, False)
            half = (mine.astype(f32) + flip_y(give).astype(f32)).astype(bf16)
            total = lax.dynamic_index_in_dim(half, z, 0, False).astype(f32)
            for k in range(1, Z):
                piece = lax.dynamic_index_in_dim(half, lax.rem(z + k, Z), 0, False)
                total = total + rot_z(piece, k).astype(f32)
            return absolute(gather_rep(total.astype(bf16)))

        my_query = lax.dynamic_slice_in_dim(w_query, r * q_c, q_c, 1)
        my_latent = lax.dynamic_slice_in_dim(w_latent, x * LAT, LAT, 1)
        my_key = lax.dynamic_slice_in_dim(
            lax.dynamic_index_in_dim(w_key_up, x, 0, False), c * q_c, q_c, 1
        )
        my_value = lax.dynamic_slice_in_dim(
            lax.dynamic_index_in_dim(w_value_up, x, 0, False), c * q_c, q_c, 1
        )
        my_out = lax.dynamic_slice_in_dim(w_out, r * q_c, q_c, 0).T
        gains = jnp.zeros((16, q_c), bf16)
        gains = gains.at[0, :n_d].set(norm_attn).at[1, :n_d].set(norm_ffn)
        pack = jnp.concatenate([my_query, my_latent, my_key, my_value, my_out, gains], 0)
        cuts = [n_d, 2 * n_d, 2 * n_d + n_l, 2 * n_d + 2 * n_l, 3 * n_d + 2 * n_l]

        col = lax.broadcasted_iota(jnp.int32, (S * R * n_f, FFq), 1)
        row = lax.broadcasted_iota(jnp.int32, (S * R * n_f, FFq), 0)
        pick = (row == (col // n_f) * (R * n_f) + r * n_f + col % n_f).astype(bf16)
        my_gate_up = dot_nn(jnp.concatenate([w_gate, w_up], 0), pick).astype(bf16)
        my_down = lax.dynamic_slice_in_dim(w_down, r * n_f, n_f, 0)

        all_tokens = gather_rep(tokens).reshape(R * T, D)
        packs = gather_shard(pack)
        all_cot = gather_rep(cotangent).reshape(R * T, D)
        gate_up = gather_shard(my_gate_up)
        down = gather_shard(my_down).reshape(FFq, D)

        query_w = packs[:, : cuts[0]].reshape(D, q_c)
        latent_w = packs[:, cuts[0] : cuts[1]].reshape(D, LAT)
        key_w = packs[:, cuts[1] : cuts[2]].reshape(LAT, q_c)
        value_w = packs[:, cuts[2] : cuts[3]].reshape(LAT, q_c)
        out_w = packs[:, cuts[3] : cuts[4]].reshape(D, q_c)
        gain_attn = packs[:, cuts[4], :n_d].reshape(D).astype(f32)
        gain_ffn = packs[:, cuts[4] + 1, :n_d].reshape(D).astype(f32)
        gate_w = gate_up[:, :n_d].reshape(D, FFq)
        up_w = gate_up[:, n_d:].reshape(D, FFq)

        heads = q_c // HD
        group_in = all_tokens.astype(f32)
        scale_attn = rms_scale(group_in)
        normed_attn = (group_in * scale_attn * gain_attn).astype(bf16)
        queries = dot_nn(normed_attn, query_w).astype(bf16)
        latents = dot_nn(normed_attn, latent_w).astype(bf16)
        keys = dot_nn(latents, key_w).astype(bf16)
        values = dot_nn(latents, value_w).astype(bf16)
        qh = queries.reshape(R, T, heads, HD)
        kh = keys.reshape(R, T, heads, HD)
        vh = values.reshape(R, T, heads, HD)
        row_ids = lax.broadcasted_iota(jnp.int32, (SEQ, SEQ), 0)
        col_ids = lax.broadcasted_iota(jnp.int32, (SEQ, SEQ), 1)
        scores = jnp.einsum("bqhd,bkhd->bhqk", qh, kh, preferred_element_type=f32) * HD**-0.5
        scores = jnp.where(col_ids <= row_ids, scores, -1e30)
        maxima = jnp.max(scores, axis=-1, keepdims=True)
        exps = jnp.exp(scores - maxima)
        probs = exps / jnp.sum(exps, axis=-1, keepdims=True)
        low_probs = probs.astype(bf16)
        mixed = jnp.einsum("bhqk,bkhd->bqhd", low_probs, vh, preferred_element_type=f32)
        mixed = mixed.astype(bf16).reshape(R * T, q_c)
        attn_part = dot_nt(mixed, out_w).reshape(R, T, D)
        inputs = tokens.astype(f32)
        residual = inputs + scatter_rep(attn_part)
        scale_ffn = rms_scale(residual)
        normed_own = (residual * scale_ffn * gain_ffn).astype(bf16)
        normed_ffn = gather_rep(normed_own).reshape(R * T, D)

        gate_proj = dot_nn(normed_ffn, gate_w)
        up_proj = dot_nn(normed_ffn, up_w)
        sig = jax.nn.sigmoid(gate_proj)
        silu = gate_proj * sig
        activated = (silu * up_proj).astype(bf16)
        grad_down = dot_tn(activated, all_cot).astype(bf16).reshape(S, n_f, D)
        grad_act = dot_nt(all_cot, down)
        grad_gate = (grad_act * up_proj * sig * (1.0 + gate_proj * (1.0 - sig))).astype(bf16)
        grad_up = (grad_act * silu).astype(bf16)
        grad_gate_w = dot_tn(normed_ffn, grad_gate).astype(bf16).reshape(S, n_d, FFq)
        grad_up_w = dot_tn(normed_ffn, grad_up).astype(bf16).reshape(S, n_d, FFq)
        ffn_back = dot_nt(grad_gate, gate_w) + dot_nt(grad_up, up_w)
        grad_normed_ffn = scatter_rep(ffn_back.reshape(R, T, D))
        ffn_part = dot_nn(activated, down).reshape(R, T, D)
        output = (residual + scatter_rep(ffn_part)).astype(bf16)

        weighted = grad_normed_ffn * gain_ffn
        grad_residual = (
            cotangent.astype(f32)
            + scale_ffn * weighted
            - residual * scale_ffn**3 * jnp.mean(weighted * residual, axis=-1, keepdims=True)
        )
        grad_attn = gather_rep(grad_residual.astype(bf16)).reshape(R * T, D)

        grad_out_w = dot_tn(grad_attn, mixed).astype(bf16)
        grad_mixed = dot_nn(grad_attn, out_w).astype(bf16).reshape(R, T, heads, HD)
        grad_probs = jnp.einsum("bqhd,bkhd->bhqk", grad_mixed, vh, preferred_element_type=f32)
        grad_scores = (
            probs * (grad_probs - jnp.sum(probs * grad_probs, axis=-1, keepdims=True))
        ).astype(bf16)
        grad_q = jnp.einsum("bhqk,bkhd->bqhd", grad_scores, kh, preferred_element_type=f32)
        grad_k = jnp.einsum("bhqk,bqhd->bkhd", grad_scores, qh, preferred_element_type=f32)
        grad_v = jnp.einsum("bhqk,bqhd->bkhd", low_probs, grad_mixed, preferred_element_type=f32)
        grad_q = (grad_q * HD**-0.5).astype(bf16).reshape(R * T, q_c)
        grad_k = (grad_k * HD**-0.5).astype(bf16).reshape(R * T, q_c)
        grad_v = grad_v.astype(bf16).reshape(R * T, q_c)
        grad_key_w = dot_tn(latents, grad_k).astype(bf16)
        grad_value_w = dot_tn(latents, grad_v).astype(bf16)
        grad_query_w = dot_tn(normed_attn, grad_q).astype(bf16)
        lat_part = (dot_nt(grad_k, key_w) + dot_nt(grad_v, value_w)).reshape(R, T, LAT)
        near = flip_core(lat_part[1::2])
        grad_lat = (lat_part[0::2] + near).astype(bf16).reshape(2 * T, LAT)
        half_normed = normed_attn.reshape(R, T, D)[0::2].reshape(2 * T, D)
        grad_latent_w = dot_tn(half_normed, grad_lat).astype(bf16)
        attn_back = dot_nt(grad_q, query_w).reshape(R, T, D)
        lat_back = dot_nt(grad_lat, latent_w).reshape(2, T, D)
        attn_back = jnp.stack(
            [attn_back[0] + lat_back[0], attn_back[1], attn_back[2] + lat_back[1], attn_back[3]]
        )
        grad_normed_attn = scatter_rep(attn_back)
        weighted = grad_normed_attn * gain_attn
        scale_own = rms_scale(inputs)
        grad_tokens = (
            grad_residual
            + scale_own * weighted
            - inputs * scale_own**3 * jnp.mean(weighted * inputs, axis=-1, keepdims=True)
        ).astype(bf16)

        sum_down = scatter_shard(grad_down)
        sum_gate = scatter_shard(grad_gate_w)
        sum_up = scatter_shard(grad_up_w)
        grad_pack = jnp.concatenate(
            [
                grad_query_w.reshape(S, n_d, q_c),
                grad_latent_w.reshape(S, n_d, LAT),
                grad_key_w.reshape(S, n_l, q_c),
                grad_value_w.reshape(S, n_l, q_c),
                grad_out_w.reshape(S, n_d, q_c),
            ],
            1,
        )
        sum_pack = scatter_shard(grad_pack).astype(f32)
        g_query = sum_pack[:, : cuts[0]].transpose(1, 0, 2).reshape(n_d, R * q_c)
        g_latent = sum_pack[:, cuts[0] : cuts[1]]
        g_latent = jnp.concatenate([g_latent[0] + g_latent[1], g_latent[2] + g_latent[3]], 1)
        g_key = sum_pack[:, cuts[1] : cuts[2]].reshape(LG, 2, n_l, q_c)
        g_key = g_key.transpose(0, 2, 1, 3).reshape(LG, n_l, 2 * q_c)
        g_value = sum_pack[:, cuts[2] : cuts[3]].reshape(LG, 2, n_l, q_c)
        g_value = g_value.transpose(0, 2, 1, 3).reshape(LG, n_l, 2 * q_c)
        g_out = sum_pack[:, cuts[3] : cuts[4]].transpose(0, 2, 1).reshape(R * q_c, n_d)
        g_down = sum_down.reshape(R * n_f, D).astype(f32)

        def spread(v):
            v = v.reshape(R, n_d, S, n_f).transpose(1, 2, 0, 3)
            return v.reshape(n_d, S * R * n_f).astype(f32)

        g_gate = spread(sum_gate)
        g_up = spread(sum_up)
        g_norm_attn = (
            jnp.sum(g_query * w_query.astype(f32), axis=1)
            + jnp.sum(g_latent * w_latent.astype(f32), axis=1)
        ) / norm_attn.astype(f32)
        g_norm_ffn = (
            jnp.sum(g_gate * w_gate.astype(f32), axis=1) + jnp.sum(g_up * w_up.astype(f32), axis=1)
        ) / norm_ffn.astype(f32)
        return (
            output,
            grad_tokens,
            g_norm_attn,
            g_query,
            g_latent,
            g_key,
            g_value,
            g_out,
            g_norm_ffn,
            g_gate,
            g_up,
            g_down,
        )

    return layer


HBM = pl.BlockSpec(memory_space=pl.ANY)
VMEM = pl.BlockSpec(memory_space=pltpu.VMEM)


def sds(shape, dtype=bf16):
    return jax.ShapeDtypeStruct(shape, dtype)


def call(body, outs, in_specs, scratch=(), name=None, after=()):
    n = len(in_specs)

    def run(*refs):
        body(*refs[:n], *refs[n + len(after) :])

    kernel = pl.pallas_call(
        run,
        out_shape=outs,
        in_specs=list(in_specs) + [HBM] * len(after),
        out_specs=jax.tree.map(lambda _: VMEM, outs),
        scratch_shapes=list(scratch),
        compiler_params=pltpu.CompilerParams(vmem_limit_bytes=56 * 1024 * 1024),
        cost_estimate=pl.CostEstimate(flops=1000, bytes_accessed=1000, transcendentals=0),
        name=name,
    )
    return lambda *args: kernel(*args, *after)


def run_copies(pairs, sems):
    copies = [pltpu.make_async_copy(a, b, sems.at[i]) for i, (a, b) in enumerate(pairs)]
    for copy in copies:
        copy.start()
    for copy in copies:
        copy.wait()


def halves(v):
    low = lax.broadcasted_iota(jnp.int32, v.shape, 1) < HD
    zero = jnp.zeros_like(v)
    return jnp.where(low, v, zero), jnp.where(low, zero, v)


def join(a, b):
    return jnp.where(lax.broadcasted_iota(jnp.int32, a.shape, 1) < HD, a, b)


def softmax_block(qm, k):
    scores = dot_nt(qm, k) * HD**-0.5
    row_ids = lax.broadcasted_iota(jnp.int32, scores.shape, 0)
    col_ids = lax.broadcasted_iota(jnp.int32, scores.shape, 1)
    scores = jnp.where(col_ids <= row_ids, scores, -1e30)
    exps = jnp.exp(scores - jnp.max(scores, axis=-1, keepdims=True))
    return exps / jnp.sum(exps, axis=-1, keepdims=True)


def make_fast(mesh):
    S = mesh.shape["shard"]
    Z = S // 2

    def flip_core(v):
        return lax.ppermute(v, "rep", [(i, i ^ 1) for i in range(R)])

    def flip_x(v):
        return lax.ppermute(v, "rep", [(i, i ^ 2) for i in range(R)])

    def flip_y(v):
        return lax.ppermute(v, "shard", [(i, i ^ 1) for i in range(S)])

    def rot_z(v, k):
        return lax.ppermute(v, "shard", [(i, (i + 2 * k) % S) for i in range(S)])

    def place():
        r = lax.axis_index("rep")
        s = lax.axis_index("shard")
        return r, r // 2, r % 2, s // 2, s % 2

    def gather_rep(v):
        far = flip_x(v)
        return v, flip_core(v), far, flip_core(far)

    def gather_shard(v):
        out = []
        for k in range(Z):
            piece = v if k == 0 else rot_z(v, k)
            out += [piece, flip_y(piece)]
        return out

    def from_shard(p, z, y):
        return 2 * lax.rem(z - p // 2 + Z, Z) + (y if p % 2 == 0 else 1 - y)

    def ring_shard(v):
        out = []
        for k in range(Z):
            piece = v if k == 0 else rot_z(piece, 1)
            out += [piece, flip_y(piece)]
        return out

    def to_shard(k, b, z, y):
        return 2 * lax.rem(z + k, Z) + (y if b == 0 else 1 - y)

    def swap_z(v):
        groups = [[2 * i + j for i in range(Z)] for j in range(2)]
        return lax.all_to_all(v, "shard", 0, 0, axis_index_groups=groups, tiled=True)

    def add_body(mine, got, *outs):
        for k in range(Z):
            total = (mine[k].astype(f32) + got[k].astype(f32)).astype(bf16)
            if len(outs) == 1:
                outs[0][k] = total
            else:
                outs[k][...] = total

    def sum_body(*refs):
        parts = [refs[0][k] for k in range(Z)] if len(refs) == 2 else [r[...] for r in refs[:-1]]
        total = parts[0].astype(f32)
        for part in parts[1:]:
            total = total + part.astype(f32)
        refs[-1][...] = total.astype(bf16)

    def scatter_swap(mine, give, name, after=()):
        got = flip_y(give)
        half = call(add_body, sds(mine.shape), [VMEM] * 2, name=name + "_add", after=after)(mine, got)
        total = call(sum_body, sds(mine.shape[1:]), [VMEM], name=name + "_sum")(swap_z(half))
        return gather_rep(total)

    def scatter_turn(mine, give, name, after=()):
        got = flip_y(give)
        shape = sds(mine.shape[1:])
        parts = call(add_body, (shape,) * Z, [VMEM] * 2, name=name + "_add", after=after)(mine, got)
        moved = [parts[0]] + [rot_z(parts[k], k) for k in range(1, Z)]
        return gather_rep(call(sum_body, shape, [VMEM] * Z, name=name + "_sum")(*moved))

    def layer(
        tokens,
        norm_attn,
        w_query,
        w_latent,
        w_key_up,
        w_value_up,
        w_out,
        norm_ffn,
        w_gate,
        w_up,
        w_down,
        cotangent,
    ):
        T, D = tokens.shape
        n_d = w_query.shape[0]
        n_l = w_key_up.shape[1]
        n_f = w_down.shape[0] // R
        p_f = -(-n_f // 16) * 16
        F = S * p_f
        q_c = w_query.shape[1] // R
        FF = S * R * n_f
        cuts = [0]
        for rows in (n_d, n_d, n_l, n_l, n_d, 16):
            cuts.append(cuts[-1] + rows)

        def pack_body(wq, wl, wk, wv, wo, na, nf, out):
            r, x, c, _, _ = place()
            wide = pl.ds(pl.multiple_of(r * q_c, q_c), q_c)
            group = pl.ds(pl.multiple_of(x * LAT, LAT), LAT)
            part = pl.ds(pl.multiple_of(c * q_c, q_c), q_c)
            out[cuts[0] : cuts[1]] = wq[:, wide]
            out[cuts[1] : cuts[2]] = wl[:, group]
            out[cuts[2] : cuts[3]] = wk[x, :, part]
            out[cuts[3] : cuts[4]] = wv[x, :, part]
            out[cuts[4] : cuts[5]] = wo[wide, :].astype(f32).T.astype(bf16)
            gains = jnp.concatenate([na[...], nf[...]], 1)
            out[cuts[5] : cuts[6]] = jnp.broadcast_to(gains, (16, 2 * n_d))

        pack = call(pack_body, sds((cuts[6], q_c)), [VMEM] * 7, name="pack")(
            w_query,
            w_latent,
            w_key_up,
            w_value_up,
            w_out,
            norm_attn.reshape(1, n_d),
            norm_ffn.reshape(1, n_d),
        )

        w_f = D - F
        u_f = F // w_f
        f_rows = [0, n_d, 2 * n_d, 2 * n_d + p_f, 2 * n_d + p_f + p_f // u_f]

        def prep_body(wg, wu, wd, out):
            r = place()[0]
            for j0 in range(0, F, 128):
                s_lo, s_hi = j0 // p_f, (j0 + 127) // p_f
                a = s_lo * R * n_f // 128 * 128
                b = min(-(-(s_hi + 1) * R * n_f // 128) * 128, FF)
                col = j0 + lax.broadcasted_iota(jnp.int32, (b - a, 128), 1)
                row = a + lax.broadcasted_iota(jnp.int32, (b - a, 128), 0)
                pick = jnp.zeros((b - a, 128), jnp.bool_)
                for s in range(s_lo, s_hi + 1):
                    i = col - s * p_f
                    hit = (i >= 0) & (i < n_f) & (row == s * R * n_f + r * n_f + i)
                    pick = pick | hit
                pick = pick.astype(f32).astype(bf16)
                cols = slice(j0, j0 + 128)
                out[f_rows[0] : f_rows[1], cols] = dot_nn(wg[:, a:b], pick).astype(bf16)
                out[f_rows[1] : f_rows[2], cols] = dot_nn(wu[:, a:b], pick).astype(bf16)
            i = lax.broadcasted_iota(jnp.int32, (p_f, R * n_f), 0)
            m = lax.broadcasted_iota(jnp.int32, (p_f, R * n_f), 1)
            pick = ((i < n_f) & (m == r * n_f + i)).astype(f32).astype(bf16)
            down = dot_nn(pick, wd[...])
            out[f_rows[2] : f_rows[3]] = down[:, :F].astype(bf16)
            for u in range(u_f):
                block = down[u * p_f // u_f : (u + 1) * p_f // u_f, F:]
                out[f_rows[3] : f_rows[4], u * w_f : (u + 1) * w_f] = block.astype(bf16)


        toks = gather_rep(tokens)
        packs = gather_shard(pack)
        my_ffn = call(
            prep_body, sds((f_rows[4], F)), [VMEM] * 3, name="prep", after=packs[2:3]
        )(w_gate, w_up, w_down)
        ffns = ring_shard(my_ffn)
        cots = gather_rep(cotangent)

        def attn_body(*refs):
            tok, pieces = refs[:R], refs[R : R + S]
            (normed, q_o, k_o, v_o, lat_o, mixed, keep, give, wq, wl, wk, wv, wo, gains) = refs[
                R + S : R + S + 14
            ]
            rows, sems = refs[R + S + 14 :]
            _, _, _, z, y = place()
            pairs = []
            for p, piece in enumerate(pieces):
                s = from_shard(p, z, y)
                at_d = pl.ds(pl.multiple_of(s * n_d, n_d), n_d)
                at_l = pl.ds(pl.multiple_of(s * n_l, n_l), n_l)
                spots = (wq.at[at_d], wl.at[at_d], wk.at[at_l], wv.at[at_l], wo.at[at_d], rows.at[s])
                for i, spot in enumerate(spots):
                    pairs.append((piece.at[pl.ds(cuts[i], cuts[i + 1] - cuts[i])], spot))
            run_copies(pairs, sems)
            for s in range(S):
                both = rows[s][0:1].astype(f32)
                gains[0:1, s * n_d : (s + 1) * n_d] = both[:, :n_d]
                gains[1:2, s * n_d : (s + 1) * n_d] = both[:, n_d : 2 * n_d]
            for j in range(R):
                ins = tok[j][...].astype(f32)
                nrm = (ins * rms_scale(ins) * gains[0:1, :]).astype(bf16)
                normed[j] = nrm
                q = dot_nn(nrm, wq[...]).astype(bf16)
                lat = dot_nn(nrm, wl[...]).astype(bf16)
                k = dot_nn(lat, wk[...]).astype(bf16)
                v = dot_nn(lat, wv[...]).astype(bf16)
                q_o[j], lat_o[j], k_o[j], v_o[j] = q, lat, k, v
                for h in range(0, q_c, 2 * HD):
                    kk, vv = k[:, h : h + 2 * HD], v[:, h : h + 2 * HD]
                    both = []
                    for qm in halves(q[:, h : h + 2 * HD]):
                        both.append(dot_nn(softmax_block(qm, kk).astype(bf16), vv))
                    mixed[j, :, h : h + 2 * HD] = join(*both).astype(bf16)
                part = dot_nt(mixed[j], wo[...]).astype(bf16)
                (keep if j % 2 == 0 else give)[j // 2] = part

        small = sds((R, T, q_c))
        (normed, q_s, k_s, v_s, lat_s, mixed, keep, give, wq, wl, wk, wv, wo, gains) = call(
            attn_body,
            (
                sds((R, T, D)),
                small,
                small,
                small,
                small,
                small,
                sds((2, T, D)),
                sds((2, T, D)),
                sds((D, q_c)),
                sds((D, LAT)),
                sds((LAT, q_c)),
                sds((LAT, q_c)),
                sds((D, q_c)),
                sds((8, D), f32),
            ),
            [VMEM] * R + [HBM] * S,
            [pltpu.VMEM((S, 16, q_c), bf16), pltpu.SemaphoreType.DMA((6 * S,))],
            name="attn",
            after=(cots[2], ffns[1], ffns[2]),
        )(*toks, *packs)

        def scatter_rep(keep, give):
            near = flip_core(give)
            chip = (keep[1].astype(f32) + near[1].astype(f32)).astype(bf16)
            return keep, near, flip_x(chip)

        def own_sum(keep, near, far):
            return keep[0].astype(f32) + near[0].astype(f32) + far[...].astype(f32)

        def norm_body(tok, gains, keep, near, far, residual, normed):
            res = tok[...].astype(f32) + own_sum(keep, near, far)
            residual[...] = res
            normed[...] = (res * rms_scale(res) * gains[1:2, :]).astype(bf16)

        residual, normed_own = call(
            norm_body, (sds((T, D), f32), sds((T, D))), [VMEM] * 5, name="norm"
        )(tokens, gains, *scatter_rep(keep, give))
        nffn = gather_rep(normed_own)

        def ffn_body(*refs):
            n_in, cot, pieces = refs[:4], refs[4:8], refs[8 : 8 + S]
            act_o, gg_o, gu_o, keep, give, wd_o, wg, wu, sems = refs[8 + S :]
            _, _, _, z, y = place()
            pairs = []
            for p, piece in enumerate(pieces):
                s = from_shard(p, z, y)
                at = pl.ds(pl.multiple_of(s * n_d, n_d), n_d)
                at_f = pl.ds(pl.multiple_of(s * p_f, p_f), p_f)
                pairs.append((piece.at[pl.ds(f_rows[0], n_d)], wg.at[at]))
                pairs.append((piece.at[pl.ds(f_rows[1], n_d)], wu.at[at]))
                left = wd_o.at[at_f, pl.ds(0, F)]
                pairs.append((piece.at[pl.ds(f_rows[2], p_f)], left))
                for u in range(u_f):
                    block = piece.at[pl.ds(f_rows[3], p_f // u_f), pl.ds(u * w_f, w_f)]
                    n_u = p_f // u_f
                    at_u = pl.ds(pl.multiple_of(s * p_f + u * n_u, n_u), n_u)
                    pairs.append((block, wd_o.at[at_u, pl.ds(F, w_f)]))
            run_copies(pairs, sems)
            for j in range(R):
                n = n_in[j][...]
                gate = dot_nn(n, wg[...])
                up = dot_nn(n, wu[...])
                g_act = dot_nt(cot[j][...], wd_o[...])
                sig = jax.nn.sigmoid(gate)
                silu = gate * sig
                act_o[j] = (silu * up).astype(bf16)
                gg = (g_act * up * sig * (1.0 + gate * (1.0 - sig))).astype(bf16)
                gu = (g_act * silu).astype(bf16)
                gg_o[j], gu_o[j] = gg, gu
                back = dot_nt(gg, wg[...]) + dot_nt(gu, wu[...])
                (keep if j % 2 == 0 else give)[j // 2] = back.astype(bf16)

        hid = sds((R, T, F))
        two = sds((2, T, D))
        act, g_gate, g_up, keep, give, wd = call(
            ffn_body,
            (hid, hid, hid, two, two, sds((F, D))),
            [VMEM] * 8 + [HBM] * S,
            [
                pltpu.VMEM((D, F), bf16),
                pltpu.VMEM((D, F), bf16),
                pltpu.SemaphoreType.DMA(((3 + u_f) * S,)),
            ],
            name="ffn",
        )(*nffn, *cots, *ffns)
        back = scatter_rep(keep, give)

        def down_body(act, c0, c1, c2, c3, out):
            cot = jnp.concatenate([c0[...], c1[...], c2[...], c3[...]], 0)
            out[...] = dot_tn(act[...].reshape(R * T, F), cot).astype(bf16)

        def hidden_body(n0, n1, n2, n3, gg, gu, mine, give, full):
            y = place()[4]
            n_all = jnp.concatenate([n0[...], n1[...], n2[...], n3[...]], 0)
            for i, grad in enumerate((gg, gu)):
                full[...] = dot_tn(n_all, grad[...].reshape(R * T, F)).astype(bf16)
                for k in range(Z):
                    for b, out in enumerate((mine, give)):
                        s = 2 * k + (y if b == 0 else 1 - y)
                        rows = full[pl.ds(pl.multiple_of(s * n_d, n_d), n_d), :]
                        out[k, i * n_d : (i + 1) * n_d] = rows

        g_down = call(down_body, sds((F, D)), [VMEM] * 5, name="gdown")(act, *cots)
        sum_dn = gather_rep(lax.psum_scatter(g_down, "shard", scatter_dimension=0, tiled=True))
        piece = sds((Z, 2 * n_d, F))
        m_h, e_h = call(
            hidden_body, (piece, piece), [VMEM] * 6, [pltpu.VMEM((D, F), bf16)], name="ghid"
        )(*nffn, g_gate, g_up)

        def part_body(act, wd, keep, give):
            for j in range(R):
                (keep if j % 2 == 0 else give)[j // 2] = dot_nn(act[j], wd[...]).astype(bf16)

        def out_body(res, keep, near, far, out):
            out[...] = (res[...] + own_sum(keep, near, far)).astype(bf16)

        def back_norm(ins, grad, gain):
            scale = rms_scale(ins)
            u = grad * gain
            return scale * u - ins * scale**3 * jnp.mean(u * ins, axis=-1, keepdims=True)

        def res_body(cot, res, gains, keep, near, far, g_res, g_attn):
            grad = back_norm(res[...], own_sum(keep, near, far), gains[1:2, :])
            grad = cot[...].astype(f32) + grad
            g_res[...] = grad
            g_attn[...] = grad.astype(bf16)

        grad_res, g_attn = call(
            res_body, (sds((T, D), f32), sds((T, D))), [VMEM] * 6, name="gres"
        )(cotangent, residual, gains, *back)
        g_attns = gather_rep(g_attn)
        part = call(part_body, (two, two), [VMEM] * 2, name="part", after=(g_attn,))(act, wd)
        output = call(out_body, sds((T, D)), [VMEM] * 4, name="outsum")(
            residual, *scatter_rep(*part)
        )

        def attn_back_body(*refs):
            ga = refs[:R]
            q_s, k_s, v_s, lat_s, mixed, normed, wk, wv, wo = refs[R : R + 9]
            gq_o, gl_o, mine, give, gk_o, gv_o, f_wide, f_low = refs[R + 9 :]
            _, _, _, z, y = place()
            for j in range(R):
                gm = dot_nn(ga[j][...], wo[...]).astype(bf16)
                q, k, v = q_s[j], k_s[j], v_s[j]
                for h in range(0, q_c, 2 * HD):
                    cols = slice(h, h + 2 * HD)
                    qq, kk, vv, gg = q[:, cols], k[:, cols], v[:, cols], gm[:, cols]
                    gqs, gks, gvs = [], [], []
                    for qm, gmm in zip(halves(qq), halves(gg)):
                        probs = softmax_block(qm, kk)
                        gp = dot_nt(gmm, vv)
                        gs = probs * (gp - jnp.sum(probs * gp, axis=-1, keepdims=True))
                        gs = gs.astype(bf16)
                        gqs.append(dot_nn(gs, kk))
                        gks.append(dot_tn(gs, qq))
                        gvs.append(dot_tn(probs.astype(bf16), gg))
                    gq_o[j, :, cols] = (join(*gqs) * HD**-0.5).astype(bf16)
                    gk_o[j, :, cols] = (join(*gks) * HD**-0.5).astype(bf16)
                    gv_o[j, :, cols] = join(*gvs).astype(bf16)
                gl_o[j] = (dot_nt(gk_o[j], wk[...]) + dot_nt(gv_o[j], wv[...])).astype(bf16)
            n_all = normed[...].reshape(R * T, D)
            lat = lat_s[...].reshape(R * T, LAT)
            g_all = jnp.concatenate([g[...] for g in ga], 0)
            f_wide[0] = dot_tn(n_all, gq_o[...].reshape(R * T, q_c)).astype(bf16)
            f_wide[1] = dot_tn(n_all, gl_o[...].reshape(R * T, LAT)).astype(bf16)
            f_wide[2] = dot_tn(g_all, mixed[...].reshape(R * T, q_c)).astype(bf16)
            f_low[0] = dot_tn(lat, gk_o[...].reshape(R * T, q_c)).astype(bf16)
            f_low[1] = dot_tn(lat, gv_o[...].reshape(R * T, q_c)).astype(bf16)
            for k in range(Z):
                for b, out in enumerate((mine, give)):
                    s = to_shard(k, b, z, y)
                    at_d = pl.ds(pl.multiple_of(s * n_d, n_d), n_d)
                    at_l = pl.ds(pl.multiple_of(s * n_l, n_l), n_l)
                    out[k, cuts[0] : cuts[1]] = f_wide[0, at_d, :]
                    out[k, cuts[1] : cuts[2]] = f_wide[1, at_d, :]
                    out[k, cuts[2] : cuts[3]] = f_low[0, at_l, :]
                    out[k, cuts[3] : cuts[4]] = f_low[1, at_l, :]
                    out[k, cuts[4] : cuts[5]] = f_wide[2, at_d, :]

        piece = sds((Z, cuts[5], q_c))
        gq, gl, m_p, e_p = call(
            attn_back_body,
            (small, small, piece, piece),
            [VMEM] * (R + 9),
            [
                pltpu.VMEM((R, T, q_c), bf16),
                pltpu.VMEM((R, T, q_c), bf16),
                pltpu.VMEM((3, D, q_c), bf16),
                pltpu.VMEM((2, LAT, q_c), bf16),
            ],
            name="attnback",
        )(*g_attns, q_s, k_s, v_s, lat_s, mixed, normed, wk, wv, wo)

        def in_body(gq, gl, wq, wl, keep, give):
            for j in range(R):
                back = dot_nt(gq[j], wq[...]) + dot_nt(gl[j], wl[...])
                (keep if j % 2 == 0 else give)[j // 2] = back.astype(bf16)

        ins_back = scatter_rep(*call(in_body, (two, two), [VMEM] * 4, name="inback")(gq, gl, wq, wl))

        def tok_body(tok, g_res, gains, keep, near, far, out):
            grad = back_norm(tok[...].astype(f32), own_sum(keep, near, far), gains[0:1, :])
            out[...] = (g_res[...] + grad).astype(bf16)

        grad_tokens = call(tok_body, sds((T, D)), [VMEM] * 6, name="gtok")(
            tokens, grad_res, gains, *ins_back
        )

        sum_p = scatter_turn(m_p, e_p, "pack")
        sum_h = scatter_swap(m_h, e_h, "hid", after=(gq,))

        def final_down_body(v0, v1, v2, v3, out):
            r = place()[0]
            for k, v in enumerate((v0, v1, v2, v3)):
                q = lax.bitwise_xor(r, k)
                out[pl.ds(pl.multiple_of(q * n_f, 8), n_f), :] = v[...].astype(f32)[:n_f]

        g_down = call(final_down_body, sds((R * n_f, D), f32), [VMEM] * 4, name="fdown")(*sum_dn)

        def lane_sum(v):
            total = v[:, :128]
            for j in range(128, v.shape[1], 128):
                total = total + v[:, j : j + 128]
            return jnp.sum(total.T, axis=0, keepdims=True)

        def final_hidden_body(v0, v1, v2, v3, w_g, w_u, nf, out_g, out_u, dots):
            r, x, c, _, _ = place()
            total = 0.0
            for i, (w, out) in enumerate(((w_g, out_g), (w_u, out_u))):
                vs = [v[i * n_d : (i + 1) * n_d].astype(f32) for v in (v0, v1, v2, v3)]
                vs = [jnp.where(c == 1, vs[k ^ 1], vs[k]) for k in range(R)]
                vs = [jnp.where(x == 1, vs[k ^ 2], vs[k]) for k in range(R)]
                for q in range(R):
                    for s in range(S):
                        at = s * R * n_f + q * n_f
                        out[:, at : at + n_f] = vs[q][:, s * p_f : s * p_f + n_f]
                total = total + lane_sum(out[...] * w[...].astype(f32))
            dots[...] = total / nf[...].astype(f32)

        row = sds((1, n_d), f32)
        wide = sds((n_d, FF), f32)
        g_gate_w, g_up_w, g_nf = call(
            final_hidden_body, (wide, wide, row), [VMEM] * 7, name="fhid"
        )(*sum_h, w_gate, w_up, norm_ffn.reshape(1, n_d))

        def final_pack_body(v0, v1, v2, v3, w_q, w_l, na, gq, gl, gk, gv, go, gna):
            r, x, _, _, _ = place()
            vs = (v0, v1, v2, v3)
            for k, v in enumerate(vs):
                q = lax.bitwise_xor(r, k)
                wide = pl.ds(pl.multiple_of(q * q_c, q_c), q_c)
                part = pl.ds(pl.multiple_of((q % 2) * q_c, q_c), q_c)
                gq[:, wide] = v[cuts[0] : cuts[1]].astype(f32)
                gk[q // 2, :, part] = v[cuts[2] : cuts[3]].astype(f32)
                gv[q // 2, :, part] = v[cuts[3] : cuts[4]].astype(f32)
                go[wide, :] = v[cuts[4] : cuts[5]].astype(f32).T
            for k in (0, 2):
                g = lax.bitwise_xor(x, k // 2)
                both = vs[k][cuts[1] : cuts[2]].astype(f32) + vs[k + 1][cuts[1] : cuts[2]].astype(f32)
                gl[:, pl.ds(pl.multiple_of(g * LAT, LAT), LAT)] = both
            dots = lane_sum(gq[...] * w_q[...].astype(f32)) + lane_sum(gl[...] * w_l[...].astype(f32))
            gna[...] = dots / na[...].astype(f32)

        g_query, g_latent, g_key, g_value, g_out, g_na = call(
            final_pack_body,
            (
                sds((n_d, R * q_c), f32),
                sds((n_d, LG * LAT), f32),
                sds((LG, n_l, 2 * q_c), f32),
                sds((LG, n_l, 2 * q_c), f32),
                sds((R * q_c, n_d), f32),
                row,
            ),
            [VMEM] * 7,
            name="fpack",
        )(*sum_p, w_query, w_latent, norm_attn.reshape(1, n_d))
        return (
            output,
            grad_tokens,
            g_na.reshape(n_d),
            g_query,
            g_latent,
            g_key,
            g_value,
            g_out,
            g_nf.reshape(n_d),
            g_gate_w,
            g_up_w,
            g_down,
        )

    return layer


def make_layer(mesh):
    aligned = (LAT // mesh.shape["shard"]) % 16 == 0
    return make_fast(mesh) if aligned else make_plain(mesh)


def solution(mesh):
    return jax.shard_map(
        make_layer(mesh),
        mesh=mesh,
        in_specs=(
            P(("rep", "shard"), None),
            P("shard"),
            P("shard", None),
            P("shard", None),
            P(None, "shard", None),
            P(None, "shard", None),
            P(None, "shard"),
            P("shard"),
            P("shard", None),
            P("shard", None),
            P("shard", None),
            P(("rep", "shard"), None),
        ),
        out_specs=(
            P(("rep", "shard"), None),
            P(("rep", "shard"), None),
            P("shard"),
            P("shard", None),
            P("shard", None),
            P(None, "shard", None),
            P(None, "shard", None),
            P(None, "shard"),
            P("shard"),
            P("shard", None),
            P("shard", None),
            P("shard", None),
        ),
        check_vma=False,
    )
```

```python
import jax
import jax.numpy as jnp
from jax import lax
from jax.experimental import pallas as pl
from jax.experimental.pallas import tpu as pltpu
from jax.sharding import PartitionSpec as P

HQ = 16
HD = 64
LG = 2
LAT = 256
SEQ = 256
R = 4
f32 = jnp.float32
bf16 = jnp.bfloat16
epsilon = 1e-05


def rms_scale(rows_in):
    return lax.rsqrt(jnp.mean(rows_in * rows_in, axis=-1, keepdims=True) + epsilon)


def dot_nn(a, b):
    return lax.dot_general(a, b, (((1,), (0,)), ((), ())), preferred_element_type=f32)


def dot_nt(a, b):
    return lax.dot_general(a, b, (((1,), (1,)), ((), ())), preferred_element_type=f32)


def dot_tn(a, b):
    return lax.dot_general(a, b, (((0,), (0,)), ((), ())), preferred_element_type=f32)


def make_plain(mesh):
    S = mesh.shape["shard"]
    Z = S // 2
    assert mesh.shape["rep"] == R

    def flip_core(v):
        return lax.ppermute(v, "rep", [(i, i ^ 1) for i in range(R)])

    def flip_x(v):
        return lax.ppermute(v, "rep", [(i, i ^ 2) for i in range(R)])

    def flip_y(v):
        return lax.ppermute(v, "shard", [(i, i ^ 1) for i in range(S)])

    def rot_z(v, k):
        return lax.ppermute(v, "shard", [(i, (i + 2 * k) % S) for i in range(S)])

    def layer(
        tokens,
        norm_attn,
        w_query,
        w_latent,
        w_key_up,
        w_value_up,
        w_out,
        norm_ffn,
        w_gate,
        w_up,
        w_down,
        cotangent,
    ):
        r = lax.axis_index("rep")
        s = lax.axis_index("shard")
        x, c, z, y = r // 2, r % 2, s // 2, s % 2
        T, D = tokens.shape
        n_d = w_query.shape[0]
        n_l = w_key_up.shape[1]
        n_f = w_down.shape[0] // R
        q_c = w_query.shape[1] // R
        FFq = n_f * S

        def gather_rep(v):
            far = flip_x(v)
            near = flip_core(jnp.stack([v, far]))
            return jnp.stack([v, near[0], far, near[1]])

        def scatter_rep(v):
            near = flip_core(v[1::2].astype(bf16))
            chip = v[0::2] + near
            far = flip_x(chip[1].astype(bf16))
            return chip[0] + far

        def absolute(v):
            v = jnp.where(c == 1, v[jnp.array([1, 0, 3, 2])], v)
            return jnp.where(x == 1, v[jnp.array([2, 3, 0, 1])], v)

        def gather_shard(v):
            full = jnp.zeros((Z, 2) + v.shape, v.dtype)
            zeros = (0,) * v.ndim
            for k in range(Z):
                piece = v if k == 0 else rot_z(v, k)
                other = flip_y(piece)
                at = lax.rem(z - k + Z, Z)
                full = lax.dynamic_update_slice(full, piece[None, None], (at, y) + zeros)
                full = lax.dynamic_update_slice(full, other[None, None], (at, 1 - y) + zeros)
            return full.reshape((S,) + v.shape)

        def scatter_shard(v):
            v = v.reshape((Z, 2) + v.shape[1:])
            mine = lax.dynamic_index_in_dim(v, y, 1, False)
            give = lax.dynamic_index_in_dim(v, 1 - y, 1, False)
            half = (mine.astype(f32) + flip_y(give).astype(f32)).astype(bf16)
            total = lax.dynamic_index_in_dim(half, z, 0, False).astype(f32)
            for k in range(1, Z):
                piece = lax.dynamic_index_in_dim(half, lax.rem(z + k, Z), 0, False)
                total = total + rot_z(piece, k).astype(f32)
            return absolute(gather_rep(total.astype(bf16)))

        my_query = lax.dynamic_slice_in_dim(w_query, r * q_c, q_c, 1)
        my_latent = lax.dynamic_slice_in_dim(w_latent, x * LAT, LAT, 1)
        my_key = lax.dynamic_slice_in_dim(
            lax.dynamic_index_in_dim(w_key_up, x, 0, False), c * q_c, q_c, 1
        )
        my_value = lax.dynamic_slice_in_dim(
            lax.dynamic_index_in_dim(w_value_up, x, 0, False), c * q_c, q_c, 1
        )
        my_out = lax.dynamic_slice_in_dim(w_out, r * q_c, q_c, 0).T
        gains = jnp.zeros((16, q_c), bf16)
        gains = gains.at[0, :n_d].set(norm_attn).at[1, :n_d].set(norm_ffn)
        pack = jnp.concatenate([my_query, my_latent, my_key, my_value, my_out, gains], 0)
        cuts = [n_d, 2 * n_d, 2 * n_d + n_l, 2 * n_d + 2 * n_l, 3 * n_d + 2 * n_l]

        col = lax.broadcasted_iota(jnp.int32, (S * R * n_f, FFq), 1)
        row = lax.broadcasted_iota(jnp.int32, (S * R * n_f, FFq), 0)
        pick = (row == (col // n_f) * (R * n_f) + r * n_f + col % n_f).astype(bf16)
        my_gate_up = dot_nn(jnp.concatenate([w_gate, w_up], 0), pick).astype(bf16)
        my_down = lax.dynamic_slice_in_dim(w_down, r * n_f, n_f, 0)

        all_tokens = gather_rep(tokens).reshape(R * T, D)
        packs = gather_shard(pack)
        all_cot = gather_rep(cotangent).reshape(R * T, D)
        gate_up = gather_shard(my_gate_up)
        down = gather_shard(my_down).reshape(FFq, D)

        query_w = packs[:, : cuts[0]].reshape(D, q_c)
        latent_w = packs[:, cuts[0] : cuts[1]].reshape(D, LAT)
        key_w = packs[:, cuts[1] : cuts[2]].reshape(LAT, q_c)
        value_w = packs[:, cuts[2] : cuts[3]].reshape(LAT, q_c)
        out_w = packs[:, cuts[3] : cuts[4]].reshape(D, q_c)
        gain_attn = packs[:, cuts[4], :n_d].reshape(D).astype(f32)
        gain_ffn = packs[:, cuts[4] + 1, :n_d].reshape(D).astype(f32)
        gate_w = gate_up[:, :n_d].reshape(D, FFq)
        up_w = gate_up[:, n_d:].reshape(D, FFq)

        heads = q_c // HD
        group_in = all_tokens.astype(f32)
        scale_attn = rms_scale(group_in)
        normed_attn = (group_in * scale_attn * gain_attn).astype(bf16)
        queries = dot_nn(normed_attn, query_w).astype(bf16)
        latents = dot_nn(normed_attn, latent_w).astype(bf16)
        keys = dot_nn(latents, key_w).astype(bf16)
        values = dot_nn(latents, value_w).astype(bf16)
        qh = queries.reshape(R, T, heads, HD)
        kh = keys.reshape(R, T, heads, HD)
        vh = values.reshape(R, T, heads, HD)
        row_ids = lax.broadcasted_iota(jnp.int32, (SEQ, SEQ), 0)
        col_ids = lax.broadcasted_iota(jnp.int32, (SEQ, SEQ), 1)
        scores = jnp.einsum("bqhd,bkhd->bhqk", qh, kh, preferred_element_type=f32) * HD**-0.5
        scores = jnp.where(col_ids <= row_ids, scores, -1e30)
        maxima = jnp.max(scores, axis=-1, keepdims=True)
        exps = jnp.exp(scores - maxima)
        probs = exps / jnp.sum(exps, axis=-1, keepdims=True)
        low_probs = probs.astype(bf16)
        mixed = jnp.einsum("bhqk,bkhd->bqhd", low_probs, vh, preferred_element_type=f32)
        mixed = mixed.astype(bf16).reshape(R * T, q_c)
        attn_part = dot_nt(mixed, out_w).reshape(R, T, D)
        inputs = tokens.astype(f32)
        residual = inputs + scatter_rep(attn_part)
        scale_ffn = rms_scale(residual)
        normed_own = (residual * scale_ffn * gain_ffn).astype(bf16)
        normed_ffn = gather_rep(normed_own).reshape(R * T, D)

        gate_proj = dot_nn(normed_ffn, gate_w)
        up_proj = dot_nn(normed_ffn, up_w)
        sig = jax.nn.sigmoid(gate_proj)
        silu = gate_proj * sig
        activated = (silu * up_proj).astype(bf16)
        grad_down = dot_tn(activated, all_cot).astype(bf16).reshape(S, n_f, D)
        grad_act = dot_nt(all_cot, down)
        grad_gate = (grad_act * up_proj * sig * (1.0 + gate_proj * (1.0 - sig))).astype(bf16)
        grad_up = (grad_act * silu).astype(bf16)
        grad_gate_w = dot_tn(normed_ffn, grad_gate).astype(bf16).reshape(S, n_d, FFq)
        grad_up_w = dot_tn(normed_ffn, grad_up).astype(bf16).reshape(S, n_d, FFq)
        ffn_back = dot_nt(grad_gate, gate_w) + dot_nt(grad_up, up_w)
        grad_normed_ffn = scatter_rep(ffn_back.reshape(R, T, D))
        ffn_part = dot_nn(activated, down).reshape(R, T, D)
        output = (residual + scatter_rep(ffn_part)).astype(bf16)

        weighted = grad_normed_ffn * gain_ffn
        grad_residual = (
            cotangent.astype(f32)
            + scale_ffn * weighted
            - residual * scale_ffn**3 * jnp.mean(weighted * residual, axis=-1, keepdims=True)
        )
        grad_attn = gather_rep(grad_residual.astype(bf16)).reshape(R * T, D)

        grad_out_w = dot_tn(grad_attn, mixed).astype(bf16)
        grad_mixed = dot_nn(grad_attn, out_w).astype(bf16).reshape(R, T, heads, HD)
        grad_probs = jnp.einsum("bqhd,bkhd->bhqk", grad_mixed, vh, preferred_element_type=f32)
        grad_scores = (
            probs * (grad_probs - jnp.sum(probs * grad_probs, axis=-1, keepdims=True))
        ).astype(bf16)
        grad_q = jnp.einsum("bhqk,bkhd->bqhd", grad_scores, kh, preferred_element_type=f32)
        grad_k = jnp.einsum("bhqk,bqhd->bkhd", grad_scores, qh, preferred_element_type=f32)
        grad_v = jnp.einsum("bhqk,bqhd->bkhd", low_probs, grad_mixed, preferred_element_type=f32)
        grad_q = (grad_q * HD**-0.5).astype(bf16).reshape(R * T, q_c)
        grad_k = (grad_k * HD**-0.5).astype(bf16).reshape(R * T, q_c)
        grad_v = grad_v.astype(bf16).reshape(R * T, q_c)
        grad_key_w = dot_tn(latents, grad_k).astype(bf16)
        grad_value_w = dot_tn(latents, grad_v).astype(bf16)
        grad_query_w = dot_tn(normed_attn, grad_q).astype(bf16)
        lat_part = (dot_nt(grad_k, key_w) + dot_nt(grad_v, value_w)).reshape(R, T, LAT)
        near = flip_core(lat_part[1::2])
        grad_lat = (lat_part[0::2] + near).astype(bf16).reshape(2 * T, LAT)
        half_normed = normed_attn.reshape(R, T, D)[0::2].reshape(2 * T, D)
        grad_latent_w = dot_tn(half_normed, grad_lat).astype(bf16)
        attn_back = dot_nt(grad_q, query_w).reshape(R, T, D)
        lat_back = dot_nt(grad_lat, latent_w).reshape(2, T, D)
        attn_back = jnp.stack(
            [attn_back[0] + lat_back[0], attn_back[1], attn_back[2] + lat_back[1], attn_back[3]]
        )
        grad_normed_attn = scatter_rep(attn_back)
        weighted = grad_normed_attn * gain_attn
        scale_own = rms_scale(inputs)
        grad_tokens = (
            grad_residual
            + scale_own * weighted
            - inputs * scale_own**3 * jnp.mean(weighted * inputs, axis=-1, keepdims=True)
        ).astype(bf16)

        sum_down = scatter_shard(grad_down)
        sum_gate = scatter_shard(grad_gate_w)
        sum_up = scatter_shard(grad_up_w)
        grad_pack = jnp.concatenate(
            [
                grad_query_w.reshape(S, n_d, q_c),
                grad_latent_w.reshape(S, n_d, LAT),
                grad_key_w.reshape(S, n_l, q_c),
                grad_value_w.reshape(S, n_l, q_c),
                grad_out_w.reshape(S, n_d, q_c),
            ],
            1,
        )
        sum_pack = scatter_shard(grad_pack).astype(f32)
        g_query = sum_pack[:, : cuts[0]].transpose(1, 0, 2).reshape(n_d, R * q_c)
        g_latent = sum_pack[:, cuts[0] : cuts[1]]
        g_latent = jnp.concatenate([g_latent[0] + g_latent[1], g_latent[2] + g_latent[3]], 1)
        g_key = sum_pack[:, cuts[1] : cuts[2]].reshape(LG, 2, n_l, q_c)
        g_key = g_key.transpose(0, 2, 1, 3).reshape(LG, n_l, 2 * q_c)
        g_value = sum_pack[:, cuts[2] : cuts[3]].reshape(LG, 2, n_l, q_c)
        g_value = g_value.transpose(0, 2, 1, 3).reshape(LG, n_l, 2 * q_c)
        g_out = sum_pack[:, cuts[3] : cuts[4]].transpose(0, 2, 1).reshape(R * q_c, n_d)
        g_down = sum_down.reshape(R * n_f, D).astype(f32)

        def spread(v):
            v = v.reshape(R, n_d, S, n_f).transpose(1, 2, 0, 3)
            return v.reshape(n_d, S * R * n_f).astype(f32)

        g_gate = spread(sum_gate)
        g_up = spread(sum_up)
        g_norm_attn = (
            jnp.sum(g_query * w_query.astype(f32), axis=1)
            + jnp.sum(g_latent * w_latent.astype(f32), axis=1)
        ) / norm_attn.astype(f32)
        g_norm_ffn = (
            jnp.sum(g_gate * w_gate.astype(f32), axis=1) + jnp.sum(g_up * w_up.astype(f32), axis=1)
        ) / norm_ffn.astype(f32)
        return (
            output,
            grad_tokens,
            g_norm_attn,
            g_query,
            g_latent,
            g_key,
            g_value,
            g_out,
            g_norm_ffn,
            g_gate,
            g_up,
            g_down,
        )

    return layer


HBM = pl.BlockSpec(memory_space=pl.ANY)
VMEM = pl.BlockSpec(memory_space=pltpu.VMEM)


def sds(shape, dtype=bf16):
    return jax.ShapeDtypeStruct(shape, dtype)


def call(body, outs, in_specs, scratch=(), name=None, after=()):
    n = len(in_specs)

    def run(*refs):
        body(*refs[:n], *refs[n + len(after) :])

    kernel = pl.pallas_call(
        run,
        out_shape=outs,
        in_specs=list(in_specs) + [HBM] * len(after),
        out_specs=jax.tree.map(lambda _: VMEM, outs),
        scratch_shapes=list(scratch),
        compiler_params=pltpu.CompilerParams(vmem_limit_bytes=(24 if name in WIDE else 8) * 1024 * 1024),
        cost_estimate=pl.CostEstimate(
            flops=0, bytes_accessed=COSTS.get(name, 2500) * 3000, transcendentals=0
        ),
        name=name,
    )
    return lambda *args: kernel(*args, *after)


WIDE = ("attn", "ffn", "attnback", "ghid", "gdown", "part", "inback", "fhid")
COSTS = {
    "pack": 2000,
    "prep": 4500,
    "attn": 11300,
    "norm": 3300,
    "ffn": 15300,
    "ghid": 8500,
    "gdown": 5000,
    "part": 4700,
    "gres": 3900,
    "attnback": 16500,
    "inback": 4000,
}


def run_copies(pairs, sems):
    copies = [pltpu.make_async_copy(a, b, sems.at[i]) for i, (a, b) in enumerate(pairs)]
    for copy in copies:
        copy.start()
    for copy in copies:
        copy.wait()


def halves(v):
    low = lax.broadcasted_iota(jnp.int32, v.shape, 1) < HD
    zero = jnp.zeros_like(v)
    return jnp.where(low, v, zero), jnp.where(low, zero, v)


def join(a, b):
    return jnp.where(lax.broadcasted_iota(jnp.int32, a.shape, 1) < HD, a, b)


def softmax_block(qm, k):
    scores = dot_nt(qm, k) * HD**-0.5
    row_ids = lax.broadcasted_iota(jnp.int32, scores.shape, 0)
    col_ids = lax.broadcasted_iota(jnp.int32, scores.shape, 1)
    scores = jnp.where(col_ids <= row_ids, scores, -1e30)
    exps = jnp.exp(scores - jnp.max(scores, axis=-1, keepdims=True))
    return exps / jnp.sum(exps, axis=-1, keepdims=True)


def make_fast(mesh):
    S = mesh.shape["shard"]
    Z = S // 2

    def flip_core(v):
        return lax.ppermute(v, "rep", [(i, i ^ 1) for i in range(R)])

    def flip_x(v):
        return lax.ppermute(v, "rep", [(i, i ^ 2) for i in range(R)])

    def flip_y(v):
        return lax.ppermute(v, "shard", [(i, i ^ 1) for i in range(S)])

    def rot_z(v, k):
        return lax.ppermute(v, "shard", [(i, (i + 2 * k) % S) for i in range(S)])

    def place():
        r = lax.axis_index("rep")
        s = lax.axis_index("shard")
        return r, r // 2, r % 2, s // 2, s % 2

    def gather_rep(v):
        far = flip_x(v)
        return v, flip_core(v), far, flip_core(far)

    def gather_shard(v):
        out = []
        for k in range(Z):
            piece = v if k == 0 else rot_z(v, k)
            out += [piece, flip_y(piece)]
        return out

    def from_shard(p, z, y):
        return 2 * lax.rem(z - p // 2 + Z, Z) + (y if p % 2 == 0 else 1 - y)

    def ring_shard(v):
        out = []
        for k in range(Z):
            piece = v if k == 0 else rot_z(piece, 1)
            out += [piece, flip_y(piece)]
        return out

    def to_shard(k, b, z, y):
        return 2 * lax.rem(z + k, Z) + (y if b == 0 else 1 - y)

    def swap_z(v):
        groups = [[2 * i + j for i in range(Z)] for j in range(2)]
        return lax.all_to_all(v, "shard", 0, 0, axis_index_groups=groups, tiled=True)

    def add_body(mine, got, *outs):
        for k in range(Z):
            total = (mine[k].astype(f32) + got[k].astype(f32)).astype(bf16)
            if len(outs) == 1:
                outs[0][k] = total
            else:
                outs[k][...] = total

    def sum_body(*refs):
        parts = [refs[0][k] for k in range(Z)] if len(refs) == 2 else [r[...] for r in refs[:-1]]
        total = parts[0].astype(f32)
        for part in parts[1:]:
            total = total + part.astype(f32)
        refs[-1][...] = total.astype(bf16)

    def half_sum(mine, got, name, split, after=()):
        shape = sds(mine.shape[1:])
        outs = (shape,) * Z if split else sds(mine.shape)
        return call(add_body, outs, [VMEM] * 2, name=name + "_add", after=after)(mine, got)

    def turn_z(parts):
        return [parts[0]] + [rot_z(parts[k], k) for k in range(1, Z)]

    def part_sum(parts, name, after=()):
        shape = parts[0].shape if len(parts) > 1 else parts[0].shape[1:]
        return call(sum_body, sds(shape), [VMEM] * len(parts), name=name + "_sum", after=after)(*parts)

    def layer(
        tokens,
        norm_attn,
        w_query,
        w_latent,
        w_key_up,
        w_value_up,
        w_out,
        norm_ffn,
        w_gate,
        w_up,
        w_down,
        cotangent,
    ):
        T, D = tokens.shape
        n_d = w_query.shape[0]
        n_l = w_key_up.shape[1]
        n_f = w_down.shape[0] // R
        p_f = -(-n_f // 16) * 16
        F = S * p_f
        q_c = w_query.shape[1] // R
        FF = S * R * n_f
        cuts = [0]
        for rows in (n_d, n_d, n_l, n_l, n_d, 16):
            cuts.append(cuts[-1] + rows)

        def pack_body(wq, wl, wk, wv, wo, na, nf, out):
            r, x, c, _, _ = place()
            wide = pl.ds(pl.multiple_of(r * q_c, q_c), q_c)
            group = pl.ds(pl.multiple_of(x * LAT, LAT), LAT)
            part = pl.ds(pl.multiple_of(c * q_c, q_c), q_c)
            out[cuts[0] : cuts[1]] = wq[:, wide]
            out[cuts[1] : cuts[2]] = wl[:, group]
            out[cuts[2] : cuts[3]] = wk[x, :, part]
            out[cuts[3] : cuts[4]] = wv[x, :, part]
            out[cuts[4] : cuts[5]] = wo[wide, :].astype(f32).T.astype(bf16)
            gains = jnp.concatenate([na[...], nf[...]], 1)
            out[cuts[5] : cuts[6]] = jnp.broadcast_to(gains, (16, 2 * n_d))

        pack = call(pack_body, sds((cuts[6], q_c)), [VMEM] * 7, name="pack")(
            w_query,
            w_latent,
            w_key_up,
            w_value_up,
            w_out,
            norm_attn.reshape(1, n_d),
            norm_ffn.reshape(1, n_d),
        )

        w_f = D - F
        u_f = F // w_f
        f_rows = [0, n_d, 2 * n_d, 2 * n_d + p_f, 2 * n_d + p_f + p_f // u_f]

        def prep_body(wg, wu, wd, out):
            r = place()[0]
            for j0 in range(0, F, 128):
                s_lo, s_hi = j0 // p_f, (j0 + 127) // p_f
                a = s_lo * R * n_f // 128 * 128
                b = min(-(-(s_hi + 1) * R * n_f // 128) * 128, FF)
                col = j0 + lax.broadcasted_iota(jnp.int32, (b - a, 128), 1)
                row = a + lax.broadcasted_iota(jnp.int32, (b - a, 128), 0)
                pick = jnp.zeros((b - a, 128), jnp.bool_)
                for s in range(s_lo, s_hi + 1):
                    i = col - s * p_f
                    hit = (i >= 0) & (i < n_f) & (row == s * R * n_f + r * n_f + i)
                    pick = pick | hit
                pick = pick.astype(f32).astype(bf16)
                cols = slice(j0, j0 + 128)
                out[f_rows[0] : f_rows[1], cols] = dot_nn(wg[:, a:b], pick).astype(bf16)
                out[f_rows[1] : f_rows[2], cols] = dot_nn(wu[:, a:b], pick).astype(bf16)
            i = lax.broadcasted_iota(jnp.int32, (p_f, R * n_f), 0)
            m = lax.broadcasted_iota(jnp.int32, (p_f, R * n_f), 1)
            pick = ((i < n_f) & (m == r * n_f + i)).astype(f32).astype(bf16)
            down = dot_nn(pick, wd[...])
            out[f_rows[2] : f_rows[3]] = down[:, :F].astype(bf16)
            for u in range(u_f):
                block = down[u * p_f // u_f : (u + 1) * p_f // u_f, F:]
                out[f_rows[3] : f_rows[4], u * w_f : (u + 1) * w_f] = block.astype(bf16)


        toks = gather_rep(tokens)
        packs = gather_shard(pack)
        my_ffn = call(
            prep_body, sds((f_rows[4], F)), [VMEM] * 3, name="prep", after=packs[1:2]
        )(w_gate, w_up, w_down)
        ffns = ring_shard(my_ffn)
        cots = gather_rep(cotangent)

        def attn_body(*refs):
            tok, pieces = refs[:R], refs[R : R + S]
            normed, q_o, k_o, v_o, lat_o, mixed = refs[R + S : R + S + 6]
            parts, (wq, wl, wk, wv, wo, gains) = refs[R + S + 6 : R + S + 10], refs[R + S + 10 : R + S + 16]
            rows, sems = refs[R + S + 16 :]
            _, _, _, z, y = place()
            pairs = []
            for p, piece in enumerate(pieces):
                s = from_shard(p, z, y)
                at_d = pl.ds(pl.multiple_of(s * n_d, n_d), n_d)
                at_l = pl.ds(pl.multiple_of(s * n_l, n_l), n_l)
                spots = (wq.at[at_d], wl.at[at_d], wk.at[at_l], wv.at[at_l], wo.at[at_d], rows.at[s])
                for i, spot in enumerate(spots):
                    pairs.append((piece.at[pl.ds(cuts[i], cuts[i + 1] - cuts[i])], spot))
            run_copies(pairs, sems)
            for s in range(S):
                both = rows[s][0:1].astype(f32)
                gains[0:1, s * n_d : (s + 1) * n_d] = both[:, :n_d]
                gains[1:2, s * n_d : (s + 1) * n_d] = both[:, n_d : 2 * n_d]
            for j in range(R):
                ins = tok[j][...].astype(f32)
                nrm = (ins * rms_scale(ins) * gains[0:1, :]).astype(bf16)
                normed[j] = nrm
                q = dot_nn(nrm, wq[...]).astype(bf16)
                lat = dot_nn(nrm, wl[...]).astype(bf16)
                k = dot_nn(lat, wk[...]).astype(bf16)
                v = dot_nn(lat, wv[...]).astype(bf16)
                q_o[j], lat_o[j], k_o[j], v_o[j] = q, lat, k, v
                for h in range(0, q_c, 2 * HD):
                    kk, vv = k[:, h : h + 2 * HD], v[:, h : h + 2 * HD]
                    both = []
                    for qm in halves(q[:, h : h + 2 * HD]):
                        both.append(dot_nn(softmax_block(qm, kk).astype(bf16), vv))
                    mixed[j, :, h : h + 2 * HD] = join(*both).astype(bf16)
                parts[j][...] = dot_nt(mixed[j], wo[...]).astype(bf16)

        small = sds((R, T, q_c))
        flat = sds((T, D))
        (normed, q_s, k_s, v_s, lat_s, mixed, *parts, wq, wl, wk, wv, wo, gains) = call(
            attn_body,
            (
                sds((R, T, D)),
                small,
                small,
                small,
                small,
                small,
                flat,
                flat,
                flat,
                flat,
                sds((D, q_c)),
                sds((D, LAT)),
                sds((LAT, q_c)),
                sds((LAT, q_c)),
                sds((D, q_c)),
                sds((8, D), f32),
            ),
            [VMEM] * R + [HBM] * S,
            [pltpu.VMEM((S, 16, q_c), bf16), pltpu.SemaphoreType.DMA((6 * S,))],
            name="attn",
            after=(cots[2], ffns[1]),
        )(*toks, *packs)

        def chip_body(keep, near, out):
            out[...] = (keep[...].astype(f32) + near[...].astype(f32)).astype(bf16)

        def scatter_rep(parts, after=()):
            near_far = flip_core(parts[3])
            near = flip_core(parts[1])
            if after:
                chip = call(chip_body, flat, [VMEM] * 2, name="chip", after=after)(parts[2], near_far)
            else:
                chip = (parts[2].astype(f32) + near_far.astype(f32)).astype(bf16)
            return (parts[0], near, flip_x(chip)), chip

        def own_sum(keep, near, far):
            return keep[...].astype(f32) + near[...].astype(f32) + far[...].astype(f32)

        def norm_body(tok, gains, keep, near, far, residual, normed):
            res = tok[...].astype(f32) + own_sum(keep, near, far)
            residual[...] = res
            normed[...] = (res * rms_scale(res) * gains[1:2, :]).astype(bf16)

        residual, normed_own = call(
            norm_body,
            (sds((T, D), f32), sds((T, D))),
            [VMEM] * 5,
            name="norm",
            after=(ffns[5], ffns[6]),
        )(tokens, gains, *scatter_rep(parts, after=(ffns[3], ffns[4]))[0])
        nffn = gather_rep(normed_own)

        def ffn_body(*refs):
            n_in, cot, pieces = refs[:4], refs[4:8], refs[8 : 8 + S]
            act_o, gg_o, gu_o, *parts, wd_o, wg, wu, sems = refs[8 + S :]
            _, _, _, z, y = place()
            pairs = []
            for p, piece in enumerate(pieces):
                s = from_shard(p, z, y)
                at = pl.ds(pl.multiple_of(s * n_d, n_d), n_d)
                at_f = pl.ds(pl.multiple_of(s * p_f, p_f), p_f)
                pairs.append((piece.at[pl.ds(f_rows[0], n_d)], wg.at[at]))
                pairs.append((piece.at[pl.ds(f_rows[1], n_d)], wu.at[at]))
                left = wd_o.at[at_f, pl.ds(0, F)]
                pairs.append((piece.at[pl.ds(f_rows[2], p_f)], left))
                for u in range(u_f):
                    block = piece.at[pl.ds(f_rows[3], p_f // u_f), pl.ds(u * w_f, w_f)]
                    n_u = p_f // u_f
                    at_u = pl.ds(pl.multiple_of(s * p_f + u * n_u, n_u), n_u)
                    pairs.append((block, wd_o.at[at_u, pl.ds(F, w_f)]))
            run_copies(pairs, sems)
            for j in range(R):
                n = n_in[j][...]
                gate = dot_nn(n, wg[...])
                up = dot_nn(n, wu[...])
                g_act = dot_nt(cot[j][...], wd_o[...])
                sig = jax.nn.sigmoid(gate)
                silu = gate * sig
                act_o[j] = (silu * up).astype(bf16)
                gg = (g_act * up * sig * (1.0 + gate * (1.0 - sig))).astype(bf16)
                gu = (g_act * silu).astype(bf16)
                gg_o[j], gu_o[j] = gg, gu
                back = dot_nt(gg, wg[...]) + dot_nt(gu, wu[...])
                parts[j][...] = back.astype(bf16)

        hid = sds((R, T, F))
        act, g_gate, g_up, *parts, wd = call(
            ffn_body,
            (hid, hid, hid, flat, flat, flat, flat, sds((F, D))),
            [VMEM] * 8 + [HBM] * S,
            [
                pltpu.VMEM((D, F), bf16),
                pltpu.VMEM((D, F), bf16),
                pltpu.SemaphoreType.DMA(((3 + u_f) * S,)),
            ],
            name="ffn",
        )(*nffn, *cots, *ffns)
        back, chip = scatter_rep(parts)

        def down_body(act, c0, c1, c2, c3, out):
            cot = jnp.concatenate([c0[...], c1[...], c2[...], c3[...]], 0)
            out[...] = dot_tn(act[...].reshape(R * T, F), cot).astype(bf16)

        def hidden_body(n0, n1, n2, n3, gg, gu, mine, give, full):
            y = place()[4]
            n_all = jnp.concatenate([n0[...], n1[...], n2[...], n3[...]], 0)
            for i, grad in enumerate((gg, gu)):
                full[...] = dot_tn(n_all, grad[...].reshape(R * T, F)).astype(bf16)
                for k in range(Z):
                    for b, out in enumerate((mine, give)):
                        s = 2 * k + (y if b == 0 else 1 - y)
                        rows = full[pl.ds(pl.multiple_of(s * n_d, n_d), n_d), :]
                        out[k, i * n_d : (i + 1) * n_d] = rows

        piece = sds((Z, 2 * n_d, F))
        m_h, e_h = call(
            hidden_body, (piece, piece), [VMEM] * 6, [pltpu.VMEM((D, F), bf16)], name="ghid", after=(chip,)
        )(*nffn, g_gate, g_up)
        g_down = call(down_body, sds((F, D)), [VMEM] * 5, name="gdown", after=(m_h,))(act, *cots)
        sum_dn = gather_rep(lax.psum_scatter(g_down, "shard", scatter_dimension=0, tiled=True))

        def part_body(act, wd, *parts):
            for j in range(R):
                parts[j][...] = dot_nn(act[j], wd[...]).astype(bf16)

        def back_norm(ins, grad, gain):
            scale = rms_scale(ins)
            u = grad * gain
            return scale * u - ins * scale**3 * jnp.mean(u * ins, axis=-1, keepdims=True)

        def res_body(cot, res, gains, keep, near, far, g_res, g_attn):
            grad = back_norm(res[...], own_sum(keep, near, far), gains[1:2, :])
            grad = cot[...].astype(f32) + grad
            g_res[...] = grad
            g_attn[...] = grad.astype(bf16)

        grad_res, g_attn = call(
            res_body, (sds((T, D), f32), sds((T, D))), [VMEM] * 6, name="gres", after=(g_down, m_h)
        )(cotangent, residual, gains, *back)
        g_attns = gather_rep(g_attn)
        part = call(part_body, (flat,) * R, [VMEM] * 2, name="part", after=(g_attn,))(act, wd)
        out_back, out_chip = scatter_rep(part, after=(g_attn,))

        def out_body(res, keep, near, far, out):
            out[...] = (res[...] + own_sum(keep, near, far)).astype(bf16)

        output = call(out_body, flat, [VMEM] * 4, name="outsum")(residual, *out_back)

        def attn_back_body(*refs):
            ga = refs[:R]
            q_s, k_s, v_s, lat_s, mixed, normed, wk, wv, wo = refs[R : R + 9]
            gq_o, gl_o, mine, give, gk_o, gv_o, f_wide, f_low = refs[R + 9 :]
            _, _, _, z, y = place()
            for j in range(R):
                gm = dot_nn(ga[j][...], wo[...]).astype(bf16)
                q, k, v = q_s[j], k_s[j], v_s[j]
                for h in range(0, q_c, 2 * HD):
                    cols = slice(h, h + 2 * HD)
                    qq, kk, vv, gg = q[:, cols], k[:, cols], v[:, cols], gm[:, cols]
                    gqs, gks, gvs = [], [], []
                    for qm, gmm in zip(halves(qq), halves(gg)):
                        probs = softmax_block(qm, kk)
                        gp = dot_nt(gmm, vv)
                        gs = probs * (gp - jnp.sum(probs * gp, axis=-1, keepdims=True))
                        gs = gs.astype(bf16)
                        gqs.append(dot_nn(gs, kk))
                        gks.append(dot_tn(gs, qq))
                        gvs.append(dot_tn(probs.astype(bf16), gg))
                    gq_o[j, :, cols] = (join(*gqs) * HD**-0.5).astype(bf16)
                    gk_o[j, :, cols] = (join(*gks) * HD**-0.5).astype(bf16)
                    gv_o[j, :, cols] = join(*gvs).astype(bf16)
                gl_o[j] = (dot_nt(gk_o[j], wk[...]) + dot_nt(gv_o[j], wv[...])).astype(bf16)
            n_all = normed[...].reshape(R * T, D)
            lat = lat_s[...].reshape(R * T, LAT)
            g_all = jnp.concatenate([g[...] for g in ga], 0)
            f_wide[0] = dot_tn(n_all, gq_o[...].reshape(R * T, q_c)).astype(bf16)
            f_wide[1] = dot_tn(n_all, gl_o[...].reshape(R * T, LAT)).astype(bf16)
            f_wide[2] = dot_tn(g_all, mixed[...].reshape(R * T, q_c)).astype(bf16)
            f_low[0] = dot_tn(lat, gk_o[...].reshape(R * T, q_c)).astype(bf16)
            f_low[1] = dot_tn(lat, gv_o[...].reshape(R * T, q_c)).astype(bf16)
            for k in range(Z):
                for b, out in enumerate((mine, give)):
                    s = to_shard(k, b, z, y)
                    at_d = pl.ds(pl.multiple_of(s * n_d, n_d), n_d)
                    at_l = pl.ds(pl.multiple_of(s * n_l, n_l), n_l)
                    out[k, cuts[0] : cuts[1]] = f_wide[0, at_d, :]
                    out[k, cuts[1] : cuts[2]] = f_wide[1, at_d, :]
                    out[k, cuts[2] : cuts[3]] = f_low[0, at_l, :]
                    out[k, cuts[3] : cuts[4]] = f_low[1, at_l, :]
                    out[k, cuts[4] : cuts[5]] = f_wide[2, at_d, :]

        piece = sds((Z, cuts[5], q_c))
        gq, gl, m_p, e_p = call(
            attn_back_body,
            (small, small, piece, piece),
            [VMEM] * (R + 9),
            [
                pltpu.VMEM((R, T, q_c), bf16),
                pltpu.VMEM((R, T, q_c), bf16),
                pltpu.VMEM((3, D, q_c), bf16),
                pltpu.VMEM((2, LAT, q_c), bf16),
            ],
            name="attnback",
            after=(out_chip,),
        )(*g_attns, q_s, k_s, v_s, lat_s, mixed, normed, wk, wv, wo)

        def in_body(gq, gl, wq, wl, *parts):
            for j in range(R):
                back = dot_nt(gq[j], wq[...]) + dot_nt(gl[j], wl[...])
                parts[j][...] = back.astype(bf16)

        got_h = flip_y(e_h)
        got_p = flip_y(e_p)
        half_h = half_sum(m_h, got_h, "hid", False, after=(gq,))
        ins_part = call(in_body, (flat,) * R, [VMEM] * 4, name="inback")(gq, gl, wq, wl)
        half_p = half_sum(m_p, got_p, "pack", True, after=(half_h, ins_part[0], output))
        ins_back = scatter_rep(ins_part, after=half_p[:1])[0]

        def tok_body(tok, g_res, gains, keep, near, far, out):
            grad = back_norm(tok[...].astype(f32), own_sum(keep, near, far), gains[0:1, :])
            out[...] = (g_res[...] + grad).astype(bf16)

        grad_tokens = call(tok_body, flat, [VMEM] * 6, name="gtok")(
            tokens, grad_res, gains, *ins_back
        )

        own_h = part_sum([swap_z(half_h)], "hid", after=(half_p[0], sum_dn[0]))
        own_p = part_sum(turn_z(half_p), "pack", after=(own_h,))
        sum_h = gather_rep(own_h)
        sum_p = gather_rep(own_p)

        def lane_sum(v):
            total = v[:, :128]
            for j in range(128, v.shape[1], 128):
                total = total + v[:, j : j + 128]
            return jnp.sum(total.T, axis=0, keepdims=True)

        def final_hidden_body(*refs):
            d_in, (v0, v1, v2, v3, w_g, w_u, nf, out_d, out_g, out_u, dots) = refs[:R], refs[R:]
            r, x, c, _, _ = place()
            for k, d in enumerate(d_in):
                q = lax.bitwise_xor(r, k)
                out_d[pl.ds(pl.multiple_of(q * n_f, 8), n_f), :] = d[...].astype(f32)[:n_f]
            total = 0.0
            for i, (w, out) in enumerate(((w_g, out_g), (w_u, out_u))):
                vs = [v[i * n_d : (i + 1) * n_d].astype(f32) for v in (v0, v1, v2, v3)]
                vs = [jnp.where(c == 1, vs[k ^ 1], vs[k]) for k in range(R)]
                vs = [jnp.where(x == 1, vs[k ^ 2], vs[k]) for k in range(R)]
                for q in range(R):
                    for s in range(S):
                        at = s * R * n_f + q * n_f
                        out[:, at : at + n_f] = vs[q][:, s * p_f : s * p_f + n_f]
                total = total + lane_sum(out[...] * w[...].astype(f32))
            dots[...] = total / nf[...].astype(f32)

        row = sds((1, n_d), f32)
        wide = sds((n_d, FF), f32)
        g_down, g_gate_w, g_up_w, g_nf = call(
            final_hidden_body,
            (sds((R * n_f, D), f32), wide, wide, row),
            [VMEM] * (R + 7),
            name="fhid",
        )(*sum_dn, *sum_h, w_gate, w_up, norm_ffn.reshape(1, n_d))

        def final_pack_body(v0, v1, v2, v3, w_q, w_l, na, gq, gl, gk, gv, go, gna):
            r, x, _, _, _ = place()
            vs = (v0, v1, v2, v3)
            for k, v in enumerate(vs):
                q = lax.bitwise_xor(r, k)
                wide = pl.ds(pl.multiple_of(q * q_c, q_c), q_c)
                part = pl.ds(pl.multiple_of((q % 2) * q_c, q_c), q_c)
                gq[:, wide] = v[cuts[0] : cuts[1]].astype(f32)
                gk[q // 2, :, part] = v[cuts[2] : cuts[3]].astype(f32)
                gv[q // 2, :, part] = v[cuts[3] : cuts[4]].astype(f32)
                go[wide, :] = v[cuts[4] : cuts[5]].astype(f32).T
            for k in (0, 2):
                g = lax.bitwise_xor(x, k // 2)
                both = vs[k][cuts[1] : cuts[2]].astype(f32) + vs[k + 1][cuts[1] : cuts[2]].astype(f32)
                gl[:, pl.ds(pl.multiple_of(g * LAT, LAT), LAT)] = both
            dots = lane_sum(gq[...] * w_q[...].astype(f32)) + lane_sum(gl[...] * w_l[...].astype(f32))
            gna[...] = dots / na[...].astype(f32)

        g_query, g_latent, g_key, g_value, g_out, g_na = call(
            final_pack_body,
            (
                sds((n_d, R * q_c), f32),
                sds((n_d, LG * LAT), f32),
                sds((LG, n_l, 2 * q_c), f32),
                sds((LG, n_l, 2 * q_c), f32),
                sds((R * q_c, n_d), f32),
                row,
            ),
            [VMEM] * 7,
            name="fpack",
            after=(g_down, output, grad_tokens),
        )(*sum_p, w_query, w_latent, norm_attn.reshape(1, n_d))
        return (
            output,
            grad_tokens,
            g_na.reshape(n_d),
            g_query,
            g_latent,
            g_key,
            g_value,
            g_out,
            g_nf.reshape(n_d),
            g_gate_w,
            g_up_w,
            g_down,
        )

    return layer


def make_layer(mesh):
    aligned = (LAT // mesh.shape["shard"]) % 16 == 0
    return make_fast(mesh) if aligned else make_plain(mesh)


def solution(mesh):
    return jax.shard_map(
        make_layer(mesh),
        mesh=mesh,
        in_specs=(
            P(("rep", "shard"), None),
            P("shard"),
            P("shard", None),
            P("shard", None),
            P(None, "shard", None),
            P(None, "shard", None),
            P(None, "shard"),
            P("shard"),
            P("shard", None),
            P("shard", None),
            P("shard", None),
            P(("rep", "shard"), None),
        ),
        out_specs=(
            P(("rep", "shard"), None),
            P(("rep", "shard"), None),
            P("shard"),
            P("shard", None),
            P("shard", None),
            P(None, "shard", None),
            P(None, "shard", None),
            P(None, "shard"),
            P("shard"),
            P("shard", None),
            P("shard", None),
            P("shard", None),
        ),
        check_vma=False,
    )
```

```python
import functools

import jax
import jax.numpy as jnp
from jax import lax
from jax.experimental import pallas as pl
from jax.experimental.pallas import tpu as pltpu
from jax.sharding import PartitionSpec as P

HQ = 16
HD = 64
LG = 2
LAT = 256
SEQ = 256
R = 4
f32 = jnp.float32
bf16 = jnp.bfloat16
epsilon = 1e-05


def rms_scale(rows_in):
    return lax.rsqrt(jnp.mean(rows_in * rows_in, axis=-1, keepdims=True) + epsilon)


def dot_nn(a, b):
    return lax.dot_general(a, b, (((1,), (0,)), ((), ())), preferred_element_type=f32)


def dot_nt(a, b):
    return lax.dot_general(a, b, (((1,), (1,)), ((), ())), preferred_element_type=f32)


def dot_tn(a, b):
    return lax.dot_general(a, b, (((0,), (0,)), ((), ())), preferred_element_type=f32)


def make_plain(mesh):
    S = mesh.shape["shard"]
    Z = S // 2
    assert mesh.shape["rep"] == R

    def flip_core(v):
        return lax.ppermute(v, "rep", [(i, i ^ 1) for i in range(R)])

    def flip_x(v):
        return lax.ppermute(v, "rep", [(i, i ^ 2) for i in range(R)])

    def flip_y(v):
        return lax.ppermute(v, "shard", [(i, i ^ 1) for i in range(S)])

    def rot_z(v, k):
        return lax.ppermute(v, "shard", [(i, (i + 2 * k) % S) for i in range(S)])

    def layer(
        tokens,
        norm_attn,
        w_query,
        w_latent,
        w_key_up,
        w_value_up,
        w_out,
        norm_ffn,
        w_gate,
        w_up,
        w_down,
        cotangent,
    ):
        r = lax.axis_index("rep")
        s = lax.axis_index("shard")
        x, c, z, y = r // 2, r % 2, s // 2, s % 2
        T, D = tokens.shape
        n_d = w_query.shape[0]
        n_l = w_key_up.shape[1]
        n_f = w_down.shape[0] // R
        q_c = w_query.shape[1] // R
        FFq = n_f * S

        def gather_rep(v):
            far = flip_x(v)
            near = flip_core(jnp.stack([v, far]))
            return jnp.stack([v, near[0], far, near[1]])

        def scatter_rep(v):
            near = flip_core(v[1::2].astype(bf16))
            chip = v[0::2] + near
            far = flip_x(chip[1].astype(bf16))
            return chip[0] + far

        def absolute(v):
            v = jnp.where(c == 1, v[jnp.array([1, 0, 3, 2])], v)
            return jnp.where(x == 1, v[jnp.array([2, 3, 0, 1])], v)

        def gather_shard(v):
            full = jnp.zeros((Z, 2) + v.shape, v.dtype)
            zeros = (0,) * v.ndim
            for k in range(Z):
                piece = v if k == 0 else rot_z(v, k)
                other = flip_y(piece)
                at = lax.rem(z - k + Z, Z)
                full = lax.dynamic_update_slice(full, piece[None, None], (at, y) + zeros)
                full = lax.dynamic_update_slice(full, other[None, None], (at, 1 - y) + zeros)
            return full.reshape((S,) + v.shape)

        def scatter_shard(v):
            v = v.reshape((Z, 2) + v.shape[1:])
            mine = lax.dynamic_index_in_dim(v, y, 1, False)
            give = lax.dynamic_index_in_dim(v, 1 - y, 1, False)
            half = (mine.astype(f32) + flip_y(give).astype(f32)).astype(bf16)
            total = lax.dynamic_index_in_dim(half, z, 0, False).astype(f32)
            for k in range(1, Z):
                piece = lax.dynamic_index_in_dim(half, lax.rem(z + k, Z), 0, False)
                total = total + rot_z(piece, k).astype(f32)
            return absolute(gather_rep(total.astype(bf16)))

        my_query = lax.dynamic_slice_in_dim(w_query, r * q_c, q_c, 1)
        my_latent = lax.dynamic_slice_in_dim(w_latent, x * LAT, LAT, 1)
        my_key = lax.dynamic_slice_in_dim(
            lax.dynamic_index_in_dim(w_key_up, x, 0, False), c * q_c, q_c, 1
        )
        my_value = lax.dynamic_slice_in_dim(
            lax.dynamic_index_in_dim(w_value_up, x, 0, False), c * q_c, q_c, 1
        )
        my_out = lax.dynamic_slice_in_dim(w_out, r * q_c, q_c, 0).T
        gains = jnp.zeros((16, q_c), bf16)
        gains = gains.at[0, :n_d].set(norm_attn).at[1, :n_d].set(norm_ffn)
        pack = jnp.concatenate([my_query, my_latent, my_key, my_value, my_out, gains], 0)
        cuts = [n_d, 2 * n_d, 2 * n_d + n_l, 2 * n_d + 2 * n_l, 3 * n_d + 2 * n_l]

        col = lax.broadcasted_iota(jnp.int32, (S * R * n_f, FFq), 1)
        row = lax.broadcasted_iota(jnp.int32, (S * R * n_f, FFq), 0)
        pick = (row == (col // n_f) * (R * n_f) + r * n_f + col % n_f).astype(bf16)
        my_gate_up = dot_nn(jnp.concatenate([w_gate, w_up], 0), pick).astype(bf16)
        my_down = lax.dynamic_slice_in_dim(w_down, r * n_f, n_f, 0)

        all_tokens = gather_rep(tokens).reshape(R * T, D)
        packs = gather_shard(pack)
        all_cot = gather_rep(cotangent).reshape(R * T, D)
        gate_up = gather_shard(my_gate_up)
        down = gather_shard(my_down).reshape(FFq, D)

        query_w = packs[:, : cuts[0]].reshape(D, q_c)
        latent_w = packs[:, cuts[0] : cuts[1]].reshape(D, LAT)
        key_w = packs[:, cuts[1] : cuts[2]].reshape(LAT, q_c)
        value_w = packs[:, cuts[2] : cuts[3]].reshape(LAT, q_c)
        out_w = packs[:, cuts[3] : cuts[4]].reshape(D, q_c)
        gain_attn = packs[:, cuts[4], :n_d].reshape(D).astype(f32)
        gain_ffn = packs[:, cuts[4] + 1, :n_d].reshape(D).astype(f32)
        gate_w = gate_up[:, :n_d].reshape(D, FFq)
        up_w = gate_up[:, n_d:].reshape(D, FFq)

        heads = q_c // HD
        group_in = all_tokens.astype(f32)
        scale_attn = rms_scale(group_in)
        normed_attn = (group_in * scale_attn * gain_attn).astype(bf16)
        queries = dot_nn(normed_attn, query_w).astype(bf16)
        latents = dot_nn(normed_attn, latent_w).astype(bf16)
        keys = dot_nn(latents, key_w).astype(bf16)
        values = dot_nn(latents, value_w).astype(bf16)
        qh = queries.reshape(R, T, heads, HD)
        kh = keys.reshape(R, T, heads, HD)
        vh = values.reshape(R, T, heads, HD)
        row_ids = lax.broadcasted_iota(jnp.int32, (SEQ, SEQ), 0)
        col_ids = lax.broadcasted_iota(jnp.int32, (SEQ, SEQ), 1)
        scores = jnp.einsum("bqhd,bkhd->bhqk", qh, kh, preferred_element_type=f32) * HD**-0.5
        scores = jnp.where(col_ids <= row_ids, scores, -1e30)
        maxima = jnp.max(scores, axis=-1, keepdims=True)
        exps = jnp.exp(scores - maxima)
        probs = exps / jnp.sum(exps, axis=-1, keepdims=True)
        low_probs = probs.astype(bf16)
        mixed = jnp.einsum("bhqk,bkhd->bqhd", low_probs, vh, preferred_element_type=f32)
        mixed = mixed.astype(bf16).reshape(R * T, q_c)
        attn_part = dot_nt(mixed, out_w).reshape(R, T, D)
        inputs = tokens.astype(f32)
        residual = inputs + scatter_rep(attn_part)
        scale_ffn = rms_scale(residual)
        normed_own = (residual * scale_ffn * gain_ffn).astype(bf16)
        normed_ffn = gather_rep(normed_own).reshape(R * T, D)

        gate_proj = dot_nn(normed_ffn, gate_w)
        up_proj = dot_nn(normed_ffn, up_w)
        sig = jax.nn.sigmoid(gate_proj)
        silu = gate_proj * sig
        activated = (silu * up_proj).astype(bf16)
        grad_down = dot_tn(activated, all_cot).astype(bf16).reshape(S, n_f, D)
        grad_act = dot_nt(all_cot, down)
        grad_gate = (grad_act * up_proj * sig * (1.0 + gate_proj * (1.0 - sig))).astype(bf16)
        grad_up = (grad_act * silu).astype(bf16)
        grad_gate_w = dot_tn(normed_ffn, grad_gate).astype(bf16).reshape(S, n_d, FFq)
        grad_up_w = dot_tn(normed_ffn, grad_up).astype(bf16).reshape(S, n_d, FFq)
        ffn_back = dot_nt(grad_gate, gate_w) + dot_nt(grad_up, up_w)
        grad_normed_ffn = scatter_rep(ffn_back.reshape(R, T, D))
        ffn_part = dot_nn(activated, down).reshape(R, T, D)
        output = (residual + scatter_rep(ffn_part)).astype(bf16)

        weighted = grad_normed_ffn * gain_ffn
        grad_residual = (
            cotangent.astype(f32)
            + scale_ffn * weighted
            - residual * scale_ffn**3 * jnp.mean(weighted * residual, axis=-1, keepdims=True)
        )
        grad_attn = gather_rep(grad_residual.astype(bf16)).reshape(R * T, D)

        grad_out_w = dot_tn(grad_attn, mixed).astype(bf16)
        grad_mixed = dot_nn(grad_attn, out_w).astype(bf16).reshape(R, T, heads, HD)
        grad_probs = jnp.einsum("bqhd,bkhd->bhqk", grad_mixed, vh, preferred_element_type=f32)
        grad_scores = (
            probs * (grad_probs - jnp.sum(probs * grad_probs, axis=-1, keepdims=True))
        ).astype(bf16)
        grad_q = jnp.einsum("bhqk,bkhd->bqhd", grad_scores, kh, preferred_element_type=f32)
        grad_k = jnp.einsum("bhqk,bqhd->bkhd", grad_scores, qh, preferred_element_type=f32)
        grad_v = jnp.einsum("bhqk,bqhd->bkhd", low_probs, grad_mixed, preferred_element_type=f32)
        grad_q = (grad_q * HD**-0.5).astype(bf16).reshape(R * T, q_c)
        grad_k = (grad_k * HD**-0.5).astype(bf16).reshape(R * T, q_c)
        grad_v = grad_v.astype(bf16).reshape(R * T, q_c)
        grad_key_w = dot_tn(latents, grad_k).astype(bf16)
        grad_value_w = dot_tn(latents, grad_v).astype(bf16)
        grad_query_w = dot_tn(normed_attn, grad_q).astype(bf16)
        lat_part = (dot_nt(grad_k, key_w) + dot_nt(grad_v, value_w)).reshape(R, T, LAT)
        near = flip_core(lat_part[1::2])
        grad_lat = (lat_part[0::2] + near).astype(bf16).reshape(2 * T, LAT)
        half_normed = normed_attn.reshape(R, T, D)[0::2].reshape(2 * T, D)
        grad_latent_w = dot_tn(half_normed, grad_lat).astype(bf16)
        attn_back = dot_nt(grad_q, query_w).reshape(R, T, D)
        lat_back = dot_nt(grad_lat, latent_w).reshape(2, T, D)
        attn_back = jnp.stack(
            [attn_back[0] + lat_back[0], attn_back[1], attn_back[2] + lat_back[1], attn_back[3]]
        )
        grad_normed_attn = scatter_rep(attn_back)
        weighted = grad_normed_attn * gain_attn
        scale_own = rms_scale(inputs)
        grad_tokens = (
            grad_residual
            + scale_own * weighted
            - inputs * scale_own**3 * jnp.mean(weighted * inputs, axis=-1, keepdims=True)
        ).astype(bf16)

        sum_down = scatter_shard(grad_down)
        sum_gate = scatter_shard(grad_gate_w)
        sum_up = scatter_shard(grad_up_w)
        grad_pack = jnp.concatenate(
            [
                grad_query_w.reshape(S, n_d, q_c),
                grad_latent_w.reshape(S, n_d, LAT),
                grad_key_w.reshape(S, n_l, q_c),
                grad_value_w.reshape(S, n_l, q_c),
                grad_out_w.reshape(S, n_d, q_c),
            ],
            1,
        )
        sum_pack = scatter_shard(grad_pack).astype(f32)
        g_query = sum_pack[:, : cuts[0]].transpose(1, 0, 2).reshape(n_d, R * q_c)
        g_latent = sum_pack[:, cuts[0] : cuts[1]]
        g_latent = jnp.concatenate([g_latent[0] + g_latent[1], g_latent[2] + g_latent[3]], 1)
        g_key = sum_pack[:, cuts[1] : cuts[2]].reshape(LG, 2, n_l, q_c)
        g_key = g_key.transpose(0, 2, 1, 3).reshape(LG, n_l, 2 * q_c)
        g_value = sum_pack[:, cuts[2] : cuts[3]].reshape(LG, 2, n_l, q_c)
        g_value = g_value.transpose(0, 2, 1, 3).reshape(LG, n_l, 2 * q_c)
        g_out = sum_pack[:, cuts[3] : cuts[4]].transpose(0, 2, 1).reshape(R * q_c, n_d)
        g_down = sum_down.reshape(R * n_f, D).astype(f32)

        def spread(v):
            v = v.reshape(R, n_d, S, n_f).transpose(1, 2, 0, 3)
            return v.reshape(n_d, S * R * n_f).astype(f32)

        g_gate = spread(sum_gate)
        g_up = spread(sum_up)
        g_norm_attn = (
            jnp.sum(g_query * w_query.astype(f32), axis=1)
            + jnp.sum(g_latent * w_latent.astype(f32), axis=1)
        ) / norm_attn.astype(f32)
        g_norm_ffn = (
            jnp.sum(g_gate * w_gate.astype(f32), axis=1) + jnp.sum(g_up * w_up.astype(f32), axis=1)
        ) / norm_ffn.astype(f32)
        return (
            output,
            grad_tokens,
            g_norm_attn,
            g_query,
            g_latent,
            g_key,
            g_value,
            g_out,
            g_norm_ffn,
            g_gate,
            g_up,
            g_down,
        )

    return layer


HBM = pl.BlockSpec(memory_space=pl.ANY)
VMEM = pl.BlockSpec(memory_space=pltpu.VMEM)
LOAD = pl.BlockSpec(memory_space=pltpu.HBM)
KEEP = pl.BlockSpec(memory_space=pltpu.HBM)


def sds(shape, dtype=bf16):
    return jax.ShapeDtypeStruct(shape, dtype)


def call(body, outs, in_specs, scratch=(), name=None, after=(), token=False):
    n, flat = len(in_specs), isinstance(outs, tuple)
    loads = [i for i, spec in enumerate(in_specs) if spec is LOAD]

    def run(*refs):
        ins, rest = list(refs[:n]), list(refs[n + len(after) :])
        if token:
            mark = rest.pop(len(outs) if flat else 1)
            mark[...] = jnp.zeros_like(mark)
        if loads:
            sems, buffers = rest[-1], rest[-1 - len(loads) : -1]
            rest = rest[: -1 - len(loads)]
            run_copies([(ins[i], buffer) for i, buffer in zip(loads, buffers)], sems)
            for i, buffer in zip(loads, buffers):
                ins[i] = buffer
        body(*ins, *rest)

    def bind(*args):
        shapes = outs if flat else (outs,)
        if token:
            shapes = shapes + (sds((8, 128), f32),)
        extra = [pltpu.VMEM(args[i].shape, args[i].dtype) for i in loads]
        if loads:
            extra.append(pltpu.SemaphoreType.DMA((len(loads),)))
        result = pl.pallas_call(
            run,
            out_shape=shapes,
            in_specs=list(in_specs) + [HBM] * len(after),
            out_specs=tuple(VMEM for _ in shapes),
            scratch_shapes=list(scratch) + extra,
            compiler_params=pltpu.CompilerParams(
                vmem_limit_bytes=LIMITS.get(name, 24 if name in WIDE else 8) * 1024 * 1024
            ),
            cost_estimate=pl.CostEstimate(
                flops=0, bytes_accessed=COSTS.get(name, 2500) * 3000, transcendentals=0
            ),
            name=name,
        )(*args, *after)
        if token:
            main = result[:-1] if flat else result[0]
            return main, result[-1]
        return result if flat else result[0]

    return bind


WIDE = ("attn", "ffn", "attnback", "wback", "ghid", "gdown", "part", "inback", "fhid")
LIMITS = {"pack": 60, "wback": 54, "attnback": 54}
COSTS = {
    "pack": 2000,
    "prep": 4500,
    "attn": 11300,
    "norm": 3300,
    "ffn": 15300,
    "ghid": 8500,
    "gdown": 5000,
    "part": 500,
    "gres": 3900,
    "attnback": 1000,
    "wback": 4000,
    "chip": 300,
    "inback": 4000,
}


def hold(v, after):
    def body(*refs):
        pass

    return pl.pallas_call(
        body,
        out_shape=sds(v.shape, v.dtype),
        in_specs=[HBM] * (1 + len(after)),
        out_specs=HBM,
        input_output_aliases={0: 0},
        name="hold",
    )(v, *after)


def run_copies(pairs, sems):
    copies = [pltpu.make_async_copy(a, b, sems.at[i]) for i, (a, b) in enumerate(pairs)]
    for copy in copies:
        copy.start()
    for copy in copies:
        copy.wait()


def halves(v):
    low = lax.broadcasted_iota(jnp.int32, v.shape, 1) < HD
    zero = jnp.zeros_like(v)
    return jnp.where(low, v, zero), jnp.where(low, zero, v)


def join(a, b):
    return jnp.where(lax.broadcasted_iota(jnp.int32, a.shape, 1) < HD, a, b)


def softmax_block(qm, k):
    scores = dot_nt(qm, k) * HD**-0.5
    row_ids = lax.broadcasted_iota(jnp.int32, scores.shape, 0)
    col_ids = lax.broadcasted_iota(jnp.int32, scores.shape, 1)
    scores = jnp.where(col_ids <= row_ids, scores, -1e30)
    exps = jnp.exp(scores - jnp.max(scores, axis=-1, keepdims=True))
    return exps / jnp.sum(exps, axis=-1, keepdims=True)


def make_fast(mesh):
    S = mesh.shape["shard"]
    Z = S // 2

    def flip_core(v):
        return lax.ppermute(v, "rep", [(i, i ^ 1) for i in range(R)])

    def flip_x(v):
        return lax.ppermute(v, "rep", [(i, i ^ 2) for i in range(R)])

    def flip_y(v):
        return lax.ppermute(v, "shard", [(i, i ^ 1) for i in range(S)])

    def rot_z(v, k):
        return lax.ppermute(v, "shard", [(i, (i + 2 * k) % S) for i in range(S)])

    def place():
        r = lax.axis_index("rep")
        s = lax.axis_index("shard")
        return r, r // 2, r % 2, s // 2, s % 2

    def gather_rep(v):
        far = flip_x(v)
        return v, flip_core(v), far, flip_core(far)

    def gather_shard(v):
        out = []
        for k in range(Z):
            piece = v if k == 0 else rot_z(v, k)
            out += [piece, flip_y(piece)]
        return out

    def from_shard(p, z, y):
        return 2 * lax.rem(z - p // 2 + Z, Z) + (y if p % 2 == 0 else 1 - y)

    def ring_shard(v):
        out = []
        for k in range(Z):
            piece = v if k == 0 else rot_z(piece, 1)
            out += [piece, flip_y(piece)]
        return out

    def to_shard(k, b, z, y):
        return 2 * lax.rem(z + k, Z) + (y if b == 0 else 1 - y)

    def swap_z(v):
        groups = [[2 * i + j for i in range(Z)] for j in range(2)]
        return lax.all_to_all(v, "shard", 0, 0, axis_index_groups=groups, tiled=True)

    def add_body(mine, got, *outs):
        for k in range(Z):
            total = (mine[k].astype(f32) + got[k].astype(f32)).astype(bf16)
            if len(outs) == 1:
                outs[0][k] = total
            else:
                outs[k][...] = total

    def sum_body(*refs):
        parts = [refs[0][k] for k in range(Z)] if len(refs) == 2 else [r[...] for r in refs[:-1]]
        total = parts[0].astype(f32)
        for part in parts[1:]:
            total = total + part.astype(f32)
        refs[-1][...] = total.astype(bf16)

    def half_sum(mine, got, name, split, after=()):
        shape = sds(mine.shape[1:])
        outs = (shape,) * Z if split else sds(mine.shape)
        add = call(add_body, outs, [LOAD, VMEM], name=name + "_add", after=after, token=True)
        return add(mine, got)

    def turn_z(parts):
        return [parts[0]] + [rot_z(parts[k], k) for k in range(1, Z)]

    def part_sum(parts, name, after=()):
        shape = parts[0].shape if len(parts) > 1 else parts[0].shape[1:]
        specs = [VMEM] * len(parts)
        return call(sum_body, sds(shape), specs, name=name + "_sum", after=after, token=True)(*parts)

    def layer(
        tokens,
        norm_attn,
        w_query,
        w_latent,
        w_key_up,
        w_value_up,
        w_out,
        norm_ffn,
        w_gate,
        w_up,
        w_down,
        cotangent,
    ):
        T, D = tokens.shape
        n_d = w_query.shape[0]
        n_l = w_key_up.shape[1]
        n_f = w_down.shape[0] // R
        p_f = -(-n_f // 16) * 16
        F = S * p_f
        q_c = w_query.shape[1] // R
        FF = S * R * n_f
        cuts = [0]
        for rows in (n_d, n_d, n_l, n_l, n_d, 16):
            cuts.append(cuts[-1] + rows)

        def pack_body(wq, wl, wk, wv, wo, na, nf, out, wo_in, sems):
            r, x, c, _, _ = place()
            wide = pl.ds(pl.multiple_of(r * q_c, q_c), q_c)
            group = pl.ds(pl.multiple_of(x * LAT, LAT), LAT)
            part = pl.ds(pl.multiple_of(c * q_c, q_c), q_c)
            pairs = [
                (wq.at[:, wide], out.at[cuts[0] : cuts[1]]),
                (wl.at[:, group], out.at[cuts[1] : cuts[2]]),
                (wk.at[x, :, part], out.at[cuts[2] : cuts[3]]),
                (wv.at[x, :, part], out.at[cuts[3] : cuts[4]]),
                (wo.at[wide, :], wo_in),
            ]
            run_copies(pairs, sems)
            out[cuts[4] : cuts[5]] = wo_in[...].astype(f32).T.astype(bf16)
            gains = jnp.concatenate([na[...], nf[...]], 1)
            out[cuts[5] : cuts[6]] = jnp.broadcast_to(gains, (16, 2 * n_d))

        pack = call(
            pack_body,
            sds((cuts[6], q_c)),
            [KEEP] * 5 + [LOAD] * 2,
            [pltpu.VMEM((q_c, n_d), bf16), pltpu.SemaphoreType.DMA((5,))],
            name="pack",
        )(
            w_query,
            w_latent,
            w_key_up,
            w_value_up,
            w_out,
            norm_attn.reshape(1, n_d),
            norm_ffn.reshape(1, n_d),
        )

        w_f = D - F
        u_f = F // w_f
        f_rows = [0, n_d, 2 * n_d, 2 * n_d + p_f, 2 * n_d + p_f + p_f // u_f]

        def prep_body(wg, wu, wd, out):
            r = place()[0]
            for j0 in range(0, F, 128):
                s_lo, s_hi = j0 // p_f, (j0 + 127) // p_f
                a = s_lo * R * n_f // 128 * 128
                b = min(-(-(s_hi + 1) * R * n_f // 128) * 128, FF)
                col = j0 + lax.broadcasted_iota(jnp.int32, (b - a, 128), 1)
                row = a + lax.broadcasted_iota(jnp.int32, (b - a, 128), 0)
                pick = jnp.zeros((b - a, 128), jnp.bool_)
                for s in range(s_lo, s_hi + 1):
                    i = col - s * p_f
                    hit = (i >= 0) & (i < n_f) & (row == s * R * n_f + r * n_f + i)
                    pick = pick | hit
                pick = pick.astype(f32).astype(bf16)
                cols = slice(j0, j0 + 128)
                out[f_rows[0] : f_rows[1], cols] = dot_nn(wg[:, a:b], pick).astype(bf16)
                out[f_rows[1] : f_rows[2], cols] = dot_nn(wu[:, a:b], pick).astype(bf16)
            i = lax.broadcasted_iota(jnp.int32, (p_f, R * n_f), 0)
            m = lax.broadcasted_iota(jnp.int32, (p_f, R * n_f), 1)
            pick = ((i < n_f) & (m == r * n_f + i)).astype(f32).astype(bf16)
            down = dot_nn(pick, wd[...])
            out[f_rows[2] : f_rows[3]] = down[:, :F].astype(bf16)
            for u in range(u_f):
                block = down[u * p_f // u_f : (u + 1) * p_f // u_f, F:]
                out[f_rows[3] : f_rows[4], u * w_f : (u + 1) * w_f] = block.astype(bf16)


        toks = gather_rep(tokens)
        packs = gather_shard(pack)
        my_ffn = call(
            prep_body, sds((f_rows[4], F)), [LOAD] * 3, name="prep", after=(pack,)
        )(w_gate, w_up, w_down)
        ffns = ring_shard(my_ffn)
        cots = gather_rep(cotangent)

        def attn_body(*refs):
            tok, pieces = refs[:R], refs[R : R + S]
            normed, q_o, k_o, v_o, lat_o, mixed = refs[R + S : R + S + 6]
            parts, (wq, wl, wk, wv, wo, gains) = refs[R + S + 6 : R + S + 10], refs[R + S + 10 : R + S + 16]
            rows, sems = refs[R + S + 16 :]
            _, _, _, z, y = place()
            pairs = []
            for p, piece in enumerate(pieces):
                s = from_shard(p, z, y)
                at_d = pl.ds(pl.multiple_of(s * n_d, n_d), n_d)
                at_l = pl.ds(pl.multiple_of(s * n_l, n_l), n_l)
                spots = (wq.at[at_d], wl.at[at_d], wk.at[at_l], wv.at[at_l], wo.at[at_d], rows.at[s])
                for i, spot in enumerate(spots):
                    pairs.append((piece.at[pl.ds(cuts[i], cuts[i + 1] - cuts[i])], spot))
            run_copies(pairs, sems)
            for s in range(S):
                both = rows[s][0:1].astype(f32)
                gains[0:1, s * n_d : (s + 1) * n_d] = both[:, :n_d]
                gains[1:2, s * n_d : (s + 1) * n_d] = both[:, n_d : 2 * n_d]
            for j in range(R):
                ins = tok[j][...].astype(f32)
                nrm = (ins * rms_scale(ins) * gains[0:1, :]).astype(bf16)
                normed[j] = nrm
                q = dot_nn(nrm, wq[...]).astype(bf16)
                lat = dot_nn(nrm, wl[...]).astype(bf16)
                k = dot_nn(lat, wk[...]).astype(bf16)
                v = dot_nn(lat, wv[...]).astype(bf16)
                q_o[j], lat_o[j], k_o[j], v_o[j] = q, lat, k, v
                for h in range(0, q_c, 2 * HD):
                    kk, vv = k[:, h : h + 2 * HD], v[:, h : h + 2 * HD]
                    both = []
                    for qm in halves(q[:, h : h + 2 * HD]):
                        both.append(dot_nn(softmax_block(qm, kk).astype(bf16), vv))
                    mixed[j, :, h : h + 2 * HD] = join(*both).astype(bf16)
                parts[j][...] = dot_nt(mixed[j], wo[...]).astype(bf16)

        small = sds((R, T, q_c))
        flat = sds((T, D))
        (normed, q_s, k_s, v_s, lat_s, mixed, *parts, wq, wl, wk, wv, wo, gains) = call(
            attn_body,
            (
                sds((R, T, D)),
                small,
                small,
                small,
                small,
                small,
                flat,
                flat,
                flat,
                flat,
                sds((D, q_c)),
                sds((D, LAT)),
                sds((LAT, q_c)),
                sds((LAT, q_c)),
                sds((D, q_c)),
                sds((8, D), f32),
            ),
            [VMEM] * R + [HBM] * S,
            [pltpu.VMEM((S, 16, q_c), bf16), pltpu.SemaphoreType.DMA((6 * S,))],
            name="attn",
            after=(cots[2], ffns[1]),
        )(*toks, *packs)

        def chip_body(keep, near, out):
            out[...] = (keep[...].astype(f32) + near[...].astype(f32)).astype(bf16)

        def scatter_rep(parts, after=()):
            near_far = flip_core(parts[3])
            near = flip_core(parts[1])
            if after:
                chip = call(chip_body, flat, [VMEM] * 2, name="chip", after=after)(parts[2], near_far)
            else:
                chip = (parts[2].astype(f32) + near_far.astype(f32)).astype(bf16)
            return (parts[0], near, flip_x(chip)), chip

        def own_sum(keep, near, far):
            return keep[...].astype(f32) + near[...].astype(f32) + far[...].astype(f32)

        def norm_body(tok, gains, keep, near, far, residual, normed):
            res = tok[...].astype(f32) + own_sum(keep, near, far)
            residual[...] = res
            normed[...] = (res * rms_scale(res) * gains[1:2, :]).astype(bf16)

        residual, normed_own = call(
            norm_body,
            (sds((T, D), f32), sds((T, D))),
            [VMEM] * 5,
            name="norm",
            after=(ffns[5], ffns[6]),
        )(tokens, gains, *scatter_rep(parts, after=(ffns[3], ffns[4]))[0])
        nffn = gather_rep(normed_own)

        def ffn_body(*refs):
            n_in, cot, pieces = refs[:4], refs[4:8], refs[8 : 8 + S]
            act_o, gg_o, gu_o, *parts, wd_o, wg, wu, sems = refs[8 + S :]
            _, _, _, z, y = place()
            pairs = []
            for p, piece in enumerate(pieces):
                s = from_shard(p, z, y)
                at = pl.ds(pl.multiple_of(s * n_d, n_d), n_d)
                at_f = pl.ds(pl.multiple_of(s * p_f, p_f), p_f)
                pairs.append((piece.at[pl.ds(f_rows[0], n_d)], wg.at[at]))
                pairs.append((piece.at[pl.ds(f_rows[1], n_d)], wu.at[at]))
                left = wd_o.at[at_f, pl.ds(0, F)]
                pairs.append((piece.at[pl.ds(f_rows[2], p_f)], left))
                for u in range(u_f):
                    block = piece.at[pl.ds(f_rows[3], p_f // u_f), pl.ds(u * w_f, w_f)]
                    n_u = p_f // u_f
                    at_u = pl.ds(pl.multiple_of(s * p_f + u * n_u, n_u), n_u)
                    pairs.append((block, wd_o.at[at_u, pl.ds(F, w_f)]))
            run_copies(pairs, sems)
            for j in range(R):
                n = n_in[j][...]
                gate = dot_nn(n, wg[...])
                up = dot_nn(n, wu[...])
                g_act = dot_nt(cot[j][...], wd_o[...])
                sig = jax.nn.sigmoid(gate)
                silu = gate * sig
                act_o[j] = (silu * up).astype(bf16)
                gg = (g_act * up * sig * (1.0 + gate * (1.0 - sig))).astype(bf16)
                gu = (g_act * silu).astype(bf16)
                gg_o[j], gu_o[j] = gg, gu
                back = dot_nt(gg, wg[...]) + dot_nt(gu, wu[...])
                parts[j][...] = back.astype(bf16)

        hid = sds((R, T, F))
        act, g_gate, g_up, *parts, wd = call(
            ffn_body,
            (hid, hid, hid, flat, flat, flat, flat, sds((F, D))),
            [VMEM] * 8 + [HBM] * S,
            [
                pltpu.VMEM((D, F), bf16),
                pltpu.VMEM((D, F), bf16),
                pltpu.SemaphoreType.DMA(((3 + u_f) * S,)),
            ],
            name="ffn",
        )(*nffn, *cots, *ffns)
        back, chip = scatter_rep(parts)

        def down_body(act, c0, c1, c2, c3, out):
            cot = jnp.concatenate([c0[...], c1[...], c2[...], c3[...]], 0)
            out[...] = dot_tn(act[...].reshape(R * T, F), cot).astype(bf16)

        def hidden_body(n0, n1, n2, n3, gg, gu, mine, give, full):
            y = place()[4]
            n_all = jnp.concatenate([n0[...], n1[...], n2[...], n3[...]], 0)
            for i, grad in enumerate((gg, gu)):
                full[...] = dot_tn(n_all, grad[...].reshape(R * T, F)).astype(bf16)
                for k in range(Z):
                    for b, out in enumerate((mine, give)):
                        s = 2 * k + (y if b == 0 else 1 - y)
                        rows = full[pl.ds(pl.multiple_of(s * n_d, n_d), n_d), :]
                        out[k, i * n_d : (i + 1) * n_d] = rows

        piece = sds((Z, 2 * n_d, F))
        (m_h, e_h), t_hid = call(
            hidden_body,
            (piece, piece),
            [VMEM] * 6,
            [pltpu.VMEM((D, F), bf16)],
            name="ghid",
            after=(chip,),
            token=True,
        )(*nffn, g_gate, g_up)
        g_down, t_down = call(
            down_body, sds((F, D)), [VMEM] * 5, name="gdown", after=(t_hid,), token=True
        )(act, *cots)
        sum_dn = gather_rep(lax.psum_scatter(g_down, "shard", scatter_dimension=0, tiled=True))

        def part_body(act, wd, *parts):
            for j in range(R):
                parts[j][...] = dot_nn(act[j], wd[...]).astype(bf16)

        def back_norm(ins, grad, gain):
            scale = rms_scale(ins)
            u = grad * gain
            return scale * u - ins * scale**3 * jnp.mean(u * ins, axis=-1, keepdims=True)

        def res_body(cot, res, gains, keep, near, far, g_res, g_attn):
            grad = back_norm(res[...], own_sum(keep, near, far), gains[1:2, :])
            grad = cot[...].astype(f32) + grad
            g_res[...] = grad
            g_attn[...] = grad.astype(bf16)

        (grad_res, g_attn), t_res = call(
            res_body,
            (sds((T, D), f32), flat),
            [LOAD, LOAD, VMEM, LOAD, VMEM, VMEM],
            name="gres",
            after=(t_down, t_hid),
            token=True,
        )(cotangent, residual, gains, *back)
        part, t_part = call(
            part_body, (flat,) * R, [VMEM, LOAD], name="part", after=(t_res,), token=True
        )(act, wd)
        out_back, out_chip = scatter_rep(part, after=(t_res,))

        def out_body(res, keep, near, far, out):
            out[...] = (res[...] + own_sum(keep, near, far)).astype(bf16)

        output, t_out = call(
            out_body, flat, [LOAD, LOAD, VMEM, VMEM], name="outsum", token=True
        )(residual, *out_back)

        def attn_back_body(first, g0, g1, q_s, k_s, v_s, wk, wv, wo, gq_o, gk_o, gv_o, gl_o):
            for j, ga in enumerate((g0, g1)):
                gm = dot_nn(ga[...], wo[...]).astype(bf16)
                q, k, v = q_s[first + j], k_s[first + j], v_s[first + j]
                for h in range(0, q_c, 2 * HD):
                    cols = slice(h, h + 2 * HD)
                    qq, kk, vv, gg = q[:, cols], k[:, cols], v[:, cols], gm[:, cols]
                    gqs, gks, gvs = [], [], []
                    for qm, gmm in zip(halves(qq), halves(gg)):
                        probs = softmax_block(qm, kk)
                        gp = dot_nt(gmm, vv)
                        gs = probs * (gp - jnp.sum(probs * gp, axis=-1, keepdims=True))
                        gs = gs.astype(bf16)
                        gqs.append(dot_nn(gs, kk))
                        gks.append(dot_tn(gs, qq))
                        gvs.append(dot_tn(probs.astype(bf16), gg))
                    gq_o[j, :, cols] = (join(*gqs) * HD**-0.5).astype(bf16)
                    gk_o[j, :, cols] = (join(*gks) * HD**-0.5).astype(bf16)
                    gv_o[j, :, cols] = join(*gvs).astype(bf16)
                gl_o[j] = (dot_nt(gk_o[j], wk[...]) + dot_nt(gv_o[j], wv[...])).astype(bf16)

        def attn_back(first, grads, after):
            pair = sds((2, T, q_c))
            return call(
                functools.partial(attn_back_body, first),
                (pair,) * 4,
                [VMEM] * 8,
                name="attnback",
                after=after,
                token=True,
            )(*grads, q_s, k_s, v_s, wk, wv, wo)

        near = (g_attn, flip_core(g_attn))
        near_back, t_near = attn_back(0, near, (t_part, out_chip))
        far = hold(flip_x(g_attn), (t_near,))
        far = (far, flip_core(far))
        far_back, t_far = attn_back(2, far, ())
        g_attns = near + far

        def weights_body(*refs):
            ga, near, far, (mixed, lat_s, normed) = refs[:R], refs[4:8], refs[8:12], refs[12:15]
            mine, give, f_wide, f_low = refs[15:]
            _, _, _, z, y = place()
            gq, gk, gv, gl = (
                jnp.concatenate([a[...], b[...]], 0).reshape(R * T, q_c) for a, b in zip(near, far)
            )
            n_all = normed[...].reshape(R * T, D)
            lat = lat_s[...].reshape(R * T, LAT)
            g_all = jnp.concatenate([g[...] for g in ga], 0)
            f_wide[0] = dot_tn(n_all, gq).astype(bf16)
            f_wide[1] = dot_tn(n_all, gl).astype(bf16)
            f_wide[2] = dot_tn(g_all, mixed[...].reshape(R * T, q_c)).astype(bf16)
            f_low[0] = dot_tn(lat, gk).astype(bf16)
            f_low[1] = dot_tn(lat, gv).astype(bf16)
            for k in range(Z):
                for b, out in enumerate((mine, give)):
                    s = to_shard(k, b, z, y)
                    at_d = pl.ds(pl.multiple_of(s * n_d, n_d), n_d)
                    at_l = pl.ds(pl.multiple_of(s * n_l, n_l), n_l)
                    out[k, cuts[0] : cuts[1]] = f_wide[0, at_d, :]
                    out[k, cuts[1] : cuts[2]] = f_wide[1, at_d, :]
                    out[k, cuts[2] : cuts[3]] = f_low[0, at_l, :]
                    out[k, cuts[3] : cuts[4]] = f_low[1, at_l, :]
                    out[k, cuts[4] : cuts[5]] = f_wide[2, at_d, :]

        got_h = flip_y(e_h)
        half_h, t_half = half_sum(m_h, got_h, "hid", False, after=(t_far,))
        piece = sds((Z, cuts[5], q_c))
        (m_p, e_p), t_back = call(
            weights_body,
            (piece, piece),
            [VMEM] * 15,
            [pltpu.VMEM((3, D, q_c), bf16), pltpu.VMEM((2, LAT, q_c), bf16)],
            name="wback",
            after=(t_half,),
            token=True,
        )(*g_attns, *near_back, *far_back, mixed, lat_s, normed)

        def in_body(gq0, gl0, gq1, gl1, wq, wl, *parts):
            for j, (gq, gl) in enumerate(((gq0, gl0), (gq1, gl1))):
                for i in range(2):
                    back = dot_nt(gq[i], wq[...]) + dot_nt(gl[i], wl[...])
                    parts[2 * j + i][...] = back.astype(bf16)

        got_p = flip_y(e_p)
        ins_part, t_in = call(
            in_body, (flat,) * R, [VMEM] * 4 + [LOAD] * 2, name="inback", after=(t_back,), token=True
        )(near_back[0], near_back[3], far_back[0], far_back[3], wq, wl)
        half_p, t_pack = half_sum(m_p, got_p, "pack", True, after=(t_half, t_in, t_out))
        ins_back = scatter_rep(ins_part, after=(t_pack,))[0]

        def tok_body(tok, g_res, gains, keep, near, far, out):
            grad = back_norm(tok[...].astype(f32), own_sum(keep, near, far), gains[0:1, :])
            out[...] = (g_res[...] + grad).astype(bf16)

        grad_tokens, t_tok = call(
            tok_body, flat, [LOAD, LOAD, VMEM, LOAD, VMEM, VMEM], name="gtok", token=True
        )(
            tokens, grad_res, gains, *ins_back
        )

        own_h, t_sum = part_sum([swap_z(half_h)], "hid", after=(t_pack, sum_dn[0]))
        own_p, _ = part_sum(turn_z(half_p), "pack", after=(t_sum,))
        sum_h = gather_rep(own_h)
        sum_p = gather_rep(own_p)

        def lane_sum(v):
            total = v[:, :128]
            for j in range(128, v.shape[1], 128):
                total = total + v[:, j : j + 128]
            return jnp.sum(total.T, axis=0, keepdims=True)

        def final_hidden_body(*refs):
            d_in, (v0, v1, v2, v3, w_g, w_u, nf, out_d, out_g, out_u, dots) = refs[:R], refs[R:]
            r, x, c, _, _ = place()
            for k, d in enumerate(d_in):
                q = lax.bitwise_xor(r, k)
                out_d[pl.ds(pl.multiple_of(q * n_f, 8), n_f), :] = d[...].astype(f32)[:n_f]
            total = 0.0
            for i, (w, out) in enumerate(((w_g, out_g), (w_u, out_u))):
                vs = [v[i * n_d : (i + 1) * n_d].astype(f32) for v in (v0, v1, v2, v3)]
                vs = [jnp.where(c == 1, vs[k ^ 1], vs[k]) for k in range(R)]
                vs = [jnp.where(x == 1, vs[k ^ 2], vs[k]) for k in range(R)]
                for q in range(R):
                    for s in range(S):
                        at = s * R * n_f + q * n_f
                        out[:, at : at + n_f] = vs[q][:, s * p_f : s * p_f + n_f]
                total = total + lane_sum(out[...] * w[...].astype(f32))
            dots[...] = total / nf[...].astype(f32)

        row = sds((1, n_d), f32)
        wide = sds((n_d, FF), f32)
        (g_down, g_gate_w, g_up_w, g_nf), t_hid = call(
            final_hidden_body,
            (sds((R * n_f, D), f32), wide, wide, row),
            [VMEM] * (2 * R) + [LOAD] * 3,
            name="fhid",
            token=True,
        )(*sum_dn, *sum_h, w_gate, w_up, norm_ffn.reshape(1, n_d))

        def final_pack_body(v0, v1, v2, v3, w_q, w_l, na, gq, gl, gk, gv, go, gna):
            r, x, _, _, _ = place()
            vs = (v0, v1, v2, v3)
            for k, v in enumerate(vs):
                q = lax.bitwise_xor(r, k)
                wide = pl.ds(pl.multiple_of(q * q_c, q_c), q_c)
                part = pl.ds(pl.multiple_of((q % 2) * q_c, q_c), q_c)
                gq[:, wide] = v[cuts[0] : cuts[1]].astype(f32)
                gk[q // 2, :, part] = v[cuts[2] : cuts[3]].astype(f32)
                gv[q // 2, :, part] = v[cuts[3] : cuts[4]].astype(f32)
                go[wide, :] = v[cuts[4] : cuts[5]].astype(f32).T
            for k in (0, 2):
                g = lax.bitwise_xor(x, k // 2)
                both = vs[k][cuts[1] : cuts[2]].astype(f32) + vs[k + 1][cuts[1] : cuts[2]].astype(f32)
                gl[:, pl.ds(pl.multiple_of(g * LAT, LAT), LAT)] = both
            dots = lane_sum(gq[...] * w_q[...].astype(f32)) + lane_sum(gl[...] * w_l[...].astype(f32))
            gna[...] = dots / na[...].astype(f32)

        g_query, g_latent, g_key, g_value, g_out, g_na = call(
            final_pack_body,
            (
                sds((n_d, R * q_c), f32),
                sds((n_d, LG * LAT), f32),
                sds((LG, n_l, 2 * q_c), f32),
                sds((LG, n_l, 2 * q_c), f32),
                sds((R * q_c, n_d), f32),
                row,
            ),
            [VMEM] * R + [LOAD] * 3,
            name="fpack",
            after=(t_hid, t_out, t_tok),
        )(*sum_p, w_query, w_latent, norm_attn.reshape(1, n_d))
        return (
            output,
            grad_tokens,
            g_na.reshape(n_d),
            g_query,
            g_latent,
            g_key,
            g_value,
            g_out,
            g_nf.reshape(n_d),
            g_gate_w,
            g_up_w,
            g_down,
        )

    return layer


def make_layer(mesh):
    aligned = (LAT // mesh.shape["shard"]) % 16 == 0
    return make_fast(mesh) if aligned else make_plain(mesh)


def solution(mesh):
    return jax.shard_map(
        make_layer(mesh),
        mesh=mesh,
        in_specs=(
            P(("rep", "shard"), None),
            P("shard"),
            P("shard", None),
            P("shard", None),
            P(None, "shard", None),
            P(None, "shard", None),
            P(None, "shard"),
            P("shard"),
            P("shard", None),
            P("shard", None),
            P("shard", None),
            P(("rep", "shard"), None),
        ),
        out_specs=(
            P(("rep", "shard"), None),
            P(("rep", "shard"), None),
            P("shard"),
            P("shard", None),
            P("shard", None),
            P(None, "shard", None),
            P(None, "shard", None),
            P(None, "shard"),
            P("shard"),
            P("shard", None),
            P("shard", None),
            P("shard", None),
        ),
        check_vma=False,
    )
```

```python
import functools

import jax
import jax.numpy as jnp
from jax import lax
from jax.experimental import pallas as pl
from jax.experimental.pallas import tpu as pltpu
from jax.sharding import PartitionSpec as P

HQ = 16
HD = 64
LG = 2
LAT = 256
SEQ = 256
R = 4
f32 = jnp.float32
bf16 = jnp.bfloat16
epsilon = 1e-05


def rms_scale(rows_in):
    return lax.rsqrt(jnp.mean(rows_in * rows_in, axis=-1, keepdims=True) + epsilon)


def dot_nn(a, b):
    return lax.dot_general(a, b, (((1,), (0,)), ((), ())), preferred_element_type=f32)


def dot_nt(a, b):
    return lax.dot_general(a, b, (((1,), (1,)), ((), ())), preferred_element_type=f32)


def dot_tn(a, b):
    return lax.dot_general(a, b, (((0,), (0,)), ((), ())), preferred_element_type=f32)


def make_plain(mesh):
    S = mesh.shape["shard"]
    Z = S // 2
    assert mesh.shape["rep"] == R

    def flip_core(v):
        return lax.ppermute(v, "rep", [(i, i ^ 1) for i in range(R)])

    def flip_x(v):
        return lax.ppermute(v, "rep", [(i, i ^ 2) for i in range(R)])

    def flip_y(v):
        return lax.ppermute(v, "shard", [(i, i ^ 1) for i in range(S)])

    def rot_z(v, k):
        return lax.ppermute(v, "shard", [(i, (i + 2 * k) % S) for i in range(S)])

    def layer(
        tokens,
        norm_attn,
        w_query,
        w_latent,
        w_key_up,
        w_value_up,
        w_out,
        norm_ffn,
        w_gate,
        w_up,
        w_down,
        cotangent,
    ):
        r = lax.axis_index("rep")
        s = lax.axis_index("shard")
        x, c, z, y = r // 2, r % 2, s // 2, s % 2
        T, D = tokens.shape
        n_d = w_query.shape[0]
        n_l = w_key_up.shape[1]
        n_f = w_down.shape[0] // R
        q_c = w_query.shape[1] // R
        FFq = n_f * S

        def gather_rep(v):
            far = flip_x(v)
            near = flip_core(jnp.stack([v, far]))
            return jnp.stack([v, near[0], far, near[1]])

        def scatter_rep(v):
            near = flip_core(v[1::2].astype(bf16))
            chip = v[0::2] + near
            far = flip_x(chip[1].astype(bf16))
            return chip[0] + far

        def absolute(v):
            v = jnp.where(c == 1, v[jnp.array([1, 0, 3, 2])], v)
            return jnp.where(x == 1, v[jnp.array([2, 3, 0, 1])], v)

        def gather_shard(v):
            full = jnp.zeros((Z, 2) + v.shape, v.dtype)
            zeros = (0,) * v.ndim
            for k in range(Z):
                piece = v if k == 0 else rot_z(v, k)
                other = flip_y(piece)
                at = lax.rem(z - k + Z, Z)
                full = lax.dynamic_update_slice(full, piece[None, None], (at, y) + zeros)
                full = lax.dynamic_update_slice(full, other[None, None], (at, 1 - y) + zeros)
            return full.reshape((S,) + v.shape)

        def scatter_shard(v):
            v = v.reshape((Z, 2) + v.shape[1:])
            mine = lax.dynamic_index_in_dim(v, y, 1, False)
            give = lax.dynamic_index_in_dim(v, 1 - y, 1, False)
            half = (mine.astype(f32) + flip_y(give).astype(f32)).astype(bf16)
            total = lax.dynamic_index_in_dim(half, z, 0, False).astype(f32)
            for k in range(1, Z):
                piece = lax.dynamic_index_in_dim(half, lax.rem(z + k, Z), 0, False)
                total = total + rot_z(piece, k).astype(f32)
            return absolute(gather_rep(total.astype(bf16)))

        my_query = lax.dynamic_slice_in_dim(w_query, r * q_c, q_c, 1)
        my_latent = lax.dynamic_slice_in_dim(w_latent, x * LAT, LAT, 1)
        my_key = lax.dynamic_slice_in_dim(
            lax.dynamic_index_in_dim(w_key_up, x, 0, False), c * q_c, q_c, 1
        )
        my_value = lax.dynamic_slice_in_dim(
            lax.dynamic_index_in_dim(w_value_up, x, 0, False), c * q_c, q_c, 1
        )
        my_out = lax.dynamic_slice_in_dim(w_out, r * q_c, q_c, 0).T
        gains = jnp.zeros((16, q_c), bf16)
        gains = gains.at[0, :n_d].set(norm_attn).at[1, :n_d].set(norm_ffn)
        pack = jnp.concatenate([my_query, my_latent, my_key, my_value, my_out, gains], 0)
        cuts = [n_d, 2 * n_d, 2 * n_d + n_l, 2 * n_d + 2 * n_l, 3 * n_d + 2 * n_l]

        col = lax.broadcasted_iota(jnp.int32, (S * R * n_f, FFq), 1)
        row = lax.broadcasted_iota(jnp.int32, (S * R * n_f, FFq), 0)
        pick = (row == (col // n_f) * (R * n_f) + r * n_f + col % n_f).astype(bf16)
        my_gate_up = dot_nn(jnp.concatenate([w_gate, w_up], 0), pick).astype(bf16)
        my_down = lax.dynamic_slice_in_dim(w_down, r * n_f, n_f, 0)

        all_tokens = gather_rep(tokens).reshape(R * T, D)
        packs = gather_shard(pack)
        all_cot = gather_rep(cotangent).reshape(R * T, D)
        gate_up = gather_shard(my_gate_up)
        down = gather_shard(my_down).reshape(FFq, D)

        query_w = packs[:, : cuts[0]].reshape(D, q_c)
        latent_w = packs[:, cuts[0] : cuts[1]].reshape(D, LAT)
        key_w = packs[:, cuts[1] : cuts[2]].reshape(LAT, q_c)
        value_w = packs[:, cuts[2] : cuts[3]].reshape(LAT, q_c)
        out_w = packs[:, cuts[3] : cuts[4]].reshape(D, q_c)
        gain_attn = packs[:, cuts[4], :n_d].reshape(D).astype(f32)
        gain_ffn = packs[:, cuts[4] + 1, :n_d].reshape(D).astype(f32)
        gate_w = gate_up[:, :n_d].reshape(D, FFq)
        up_w = gate_up[:, n_d:].reshape(D, FFq)

        heads = q_c // HD
        group_in = all_tokens.astype(f32)
        scale_attn = rms_scale(group_in)
        normed_attn = (group_in * scale_attn * gain_attn).astype(bf16)
        queries = dot_nn(normed_attn, query_w).astype(bf16)
        latents = dot_nn(normed_attn, latent_w).astype(bf16)
        keys = dot_nn(latents, key_w).astype(bf16)
        values = dot_nn(latents, value_w).astype(bf16)
        qh = queries.reshape(R, T, heads, HD)
        kh = keys.reshape(R, T, heads, HD)
        vh = values.reshape(R, T, heads, HD)
        row_ids = lax.broadcasted_iota(jnp.int32, (SEQ, SEQ), 0)
        col_ids = lax.broadcasted_iota(jnp.int32, (SEQ, SEQ), 1)
        scores = jnp.einsum("bqhd,bkhd->bhqk", qh, kh, preferred_element_type=f32) * HD**-0.5
        scores = jnp.where(col_ids <= row_ids, scores, -1e30)
        maxima = jnp.max(scores, axis=-1, keepdims=True)
        exps = jnp.exp(scores - maxima)
        probs = exps / jnp.sum(exps, axis=-1, keepdims=True)
        low_probs = probs.astype(bf16)
        mixed = jnp.einsum("bhqk,bkhd->bqhd", low_probs, vh, preferred_element_type=f32)
        mixed = mixed.astype(bf16).reshape(R * T, q_c)
        attn_part = dot_nt(mixed, out_w).reshape(R, T, D)
        inputs = tokens.astype(f32)
        residual = inputs + scatter_rep(attn_part)
        scale_ffn = rms_scale(residual)
        normed_own = (residual * scale_ffn * gain_ffn).astype(bf16)
        normed_ffn = gather_rep(normed_own).reshape(R * T, D)

        gate_proj = dot_nn(normed_ffn, gate_w)
        up_proj = dot_nn(normed_ffn, up_w)
        sig = jax.nn.sigmoid(gate_proj)
        silu = gate_proj * sig
        activated = (silu * up_proj).astype(bf16)
        grad_down = dot_tn(activated, all_cot).astype(bf16).reshape(S, n_f, D)
        grad_act = dot_nt(all_cot, down)
        grad_gate = (grad_act * up_proj * sig * (1.0 + gate_proj * (1.0 - sig))).astype(bf16)
        grad_up = (grad_act * silu).astype(bf16)
        grad_gate_w = dot_tn(normed_ffn, grad_gate).astype(bf16).reshape(S, n_d, FFq)
        grad_up_w = dot_tn(normed_ffn, grad_up).astype(bf16).reshape(S, n_d, FFq)
        ffn_back = dot_nt(grad_gate, gate_w) + dot_nt(grad_up, up_w)
        grad_normed_ffn = scatter_rep(ffn_back.reshape(R, T, D))
        ffn_part = dot_nn(activated, down).reshape(R, T, D)
        output = (residual + scatter_rep(ffn_part)).astype(bf16)

        weighted = grad_normed_ffn * gain_ffn
        grad_residual = (
            cotangent.astype(f32)
            + scale_ffn * weighted
            - residual * scale_ffn**3 * jnp.mean(weighted * residual, axis=-1, keepdims=True)
        )
        grad_attn = gather_rep(grad_residual.astype(bf16)).reshape(R * T, D)

        grad_out_w = dot_tn(grad_attn, mixed).astype(bf16)
        grad_mixed = dot_nn(grad_attn, out_w).astype(bf16).reshape(R, T, heads, HD)
        grad_probs = jnp.einsum("bqhd,bkhd->bhqk", grad_mixed, vh, preferred_element_type=f32)
        grad_scores = (
            probs * (grad_probs - jnp.sum(probs * grad_probs, axis=-1, keepdims=True))
        ).astype(bf16)
        grad_q = jnp.einsum("bhqk,bkhd->bqhd", grad_scores, kh, preferred_element_type=f32)
        grad_k = jnp.einsum("bhqk,bqhd->bkhd", grad_scores, qh, preferred_element_type=f32)
        grad_v = jnp.einsum("bhqk,bqhd->bkhd", low_probs, grad_mixed, preferred_element_type=f32)
        grad_q = (grad_q * HD**-0.5).astype(bf16).reshape(R * T, q_c)
        grad_k = (grad_k * HD**-0.5).astype(bf16).reshape(R * T, q_c)
        grad_v = grad_v.astype(bf16).reshape(R * T, q_c)
        grad_key_w = dot_tn(latents, grad_k).astype(bf16)
        grad_value_w = dot_tn(latents, grad_v).astype(bf16)
        grad_query_w = dot_tn(normed_attn, grad_q).astype(bf16)
        lat_part = (dot_nt(grad_k, key_w) + dot_nt(grad_v, value_w)).reshape(R, T, LAT)
        near = flip_core(lat_part[1::2])
        grad_lat = (lat_part[0::2] + near).astype(bf16).reshape(2 * T, LAT)
        half_normed = normed_attn.reshape(R, T, D)[0::2].reshape(2 * T, D)
        grad_latent_w = dot_tn(half_normed, grad_lat).astype(bf16)
        attn_back = dot_nt(grad_q, query_w).reshape(R, T, D)
        lat_back = dot_nt(grad_lat, latent_w).reshape(2, T, D)
        attn_back = jnp.stack(
            [attn_back[0] + lat_back[0], attn_back[1], attn_back[2] + lat_back[1], attn_back[3]]
        )
        grad_normed_attn = scatter_rep(attn_back)
        weighted = grad_normed_attn * gain_attn
        scale_own = rms_scale(inputs)
        grad_tokens = (
            grad_residual
            + scale_own * weighted
            - inputs * scale_own**3 * jnp.mean(weighted * inputs, axis=-1, keepdims=True)
        ).astype(bf16)

        sum_down = scatter_shard(grad_down)
        sum_gate = scatter_shard(grad_gate_w)
        sum_up = scatter_shard(grad_up_w)
        grad_pack = jnp.concatenate(
            [
                grad_query_w.reshape(S, n_d, q_c),
                grad_latent_w.reshape(S, n_d, LAT),
                grad_key_w.reshape(S, n_l, q_c),
                grad_value_w.reshape(S, n_l, q_c),
                grad_out_w.reshape(S, n_d, q_c),
            ],
            1,
        )
        sum_pack = scatter_shard(grad_pack).astype(f32)
        g_query = sum_pack[:, : cuts[0]].transpose(1, 0, 2).reshape(n_d, R * q_c)
        g_latent = sum_pack[:, cuts[0] : cuts[1]]
        g_latent = jnp.concatenate([g_latent[0] + g_latent[1], g_latent[2] + g_latent[3]], 1)
        g_key = sum_pack[:, cuts[1] : cuts[2]].reshape(LG, 2, n_l, q_c)
        g_key = g_key.transpose(0, 2, 1, 3).reshape(LG, n_l, 2 * q_c)
        g_value = sum_pack[:, cuts[2] : cuts[3]].reshape(LG, 2, n_l, q_c)
        g_value = g_value.transpose(0, 2, 1, 3).reshape(LG, n_l, 2 * q_c)
        g_out = sum_pack[:, cuts[3] : cuts[4]].transpose(0, 2, 1).reshape(R * q_c, n_d)
        g_down = sum_down.reshape(R * n_f, D).astype(f32)

        def spread(v):
            v = v.reshape(R, n_d, S, n_f).transpose(1, 2, 0, 3)
            return v.reshape(n_d, S * R * n_f).astype(f32)

        g_gate = spread(sum_gate)
        g_up = spread(sum_up)
        g_norm_attn = (
            jnp.sum(g_query * w_query.astype(f32), axis=1)
            + jnp.sum(g_latent * w_latent.astype(f32), axis=1)
        ) / norm_attn.astype(f32)
        g_norm_ffn = (
            jnp.sum(g_gate * w_gate.astype(f32), axis=1) + jnp.sum(g_up * w_up.astype(f32), axis=1)
        ) / norm_ffn.astype(f32)
        return (
            output,
            grad_tokens,
            g_norm_attn,
            g_query,
            g_latent,
            g_key,
            g_value,
            g_out,
            g_norm_ffn,
            g_gate,
            g_up,
            g_down,
        )

    return layer


HBM = pl.BlockSpec(memory_space=pl.ANY)
VMEM = pl.BlockSpec(memory_space=pltpu.VMEM)
LOAD = pl.BlockSpec(memory_space=pltpu.HBM)
KEEP = pl.BlockSpec(memory_space=pltpu.HBM)


def sds(shape, dtype=bf16):
    return jax.ShapeDtypeStruct(shape, dtype)


def call(body, outs, in_specs, scratch=(), name=None, after=(), token=False):
    n, flat = len(in_specs), isinstance(outs, tuple)
    loads = [i for i, spec in enumerate(in_specs) if spec is LOAD]

    def run(*refs):
        ins, rest = list(refs[:n]), list(refs[n + len(after) :])
        if token:
            mark = rest.pop(len(outs) if flat else 1)
            mark[...] = jnp.zeros_like(mark)
        if loads:
            sems, buffers = rest[-1], rest[-1 - len(loads) : -1]
            rest = rest[: -1 - len(loads)]
            run_copies([(ins[i], buffer) for i, buffer in zip(loads, buffers)], sems)
            for i, buffer in zip(loads, buffers):
                ins[i] = buffer
        body(*ins, *rest)

    def bind(*args):
        shapes = outs if flat else (outs,)
        if token:
            shapes = shapes + (sds((8, 128), f32),)
        extra = [pltpu.VMEM(args[i].shape, args[i].dtype) for i in loads]
        if loads:
            extra.append(pltpu.SemaphoreType.DMA((len(loads),)))
        result = pl.pallas_call(
            run,
            out_shape=shapes,
            in_specs=list(in_specs) + [HBM] * len(after),
            out_specs=tuple(VMEM for _ in shapes),
            scratch_shapes=list(scratch) + extra,
            compiler_params=pltpu.CompilerParams(
                vmem_limit_bytes=LIMITS.get(name, 24 if name in WIDE else 8) * 1024 * 1024
            ),
            cost_estimate=pl.CostEstimate(
                flops=0, bytes_accessed=COSTS.get(name, 2500) * 3000, transcendentals=0
            ),
            name=name,
        )(*args, *after)
        if token:
            main = result[:-1] if flat else result[0]
            return main, result[-1]
        return result if flat else result[0]

    return bind


WIDE = ("attn", "ffn", "attnback", "wback", "ghid", "gdown", "part", "inback", "fhid")
LIMITS = {"pack": 60, "wback": 54, "attnback": 54}
COSTS = {
    "pack": 2000,
    "prep": 4500,
    "attn": 11300,
    "norm": 3300,
    "ffn": 15300,
    "ghid": 8500,
    "gdown": 5000,
    "part": 500,
    "gres": 3900,
    "attnback": 1000,
    "wback": 4000,
    "chip": 300,
    "inback": 4000,
}


def hold(v, after):
    def body(*refs):
        pass

    return pl.pallas_call(
        body,
        out_shape=sds(v.shape, v.dtype),
        in_specs=[HBM] * (1 + len(after)),
        out_specs=HBM,
        input_output_aliases={0: 0},
        name="hold",
    )(v, *after)


def run_copies(pairs, sems):
    copies = [pltpu.make_async_copy(a, b, sems.at[i]) for i, (a, b) in enumerate(pairs)]
    for copy in copies:
        copy.start()
    for copy in copies:
        copy.wait()


def halves(v):
    low = lax.broadcasted_iota(jnp.int32, v.shape, 1) < HD
    zero = jnp.zeros_like(v)
    return jnp.where(low, v, zero), jnp.where(low, zero, v)


def join(a, b):
    return jnp.where(lax.broadcasted_iota(jnp.int32, a.shape, 1) < HD, a, b)


def softmax_block(qm, k):
    scores = dot_nt(qm, k) * HD**-0.5
    row_ids = lax.broadcasted_iota(jnp.int32, scores.shape, 0)
    col_ids = lax.broadcasted_iota(jnp.int32, scores.shape, 1)
    scores = jnp.where(col_ids <= row_ids, scores, -1e30)
    exps = jnp.exp(scores - jnp.max(scores, axis=-1, keepdims=True))
    return exps / jnp.sum(exps, axis=-1, keepdims=True)


def make_fast(mesh):
    S = mesh.shape["shard"]
    Z = S // 2

    def flip_core(v):
        return lax.ppermute(v, "rep", [(i, i ^ 1) for i in range(R)])

    def flip_x(v):
        return lax.ppermute(v, "rep", [(i, i ^ 2) for i in range(R)])

    def flip_y(v):
        return lax.ppermute(v, "shard", [(i, i ^ 1) for i in range(S)])

    def rot_z(v, k):
        return lax.ppermute(v, "shard", [(i, (i + 2 * k) % S) for i in range(S)])

    def place():
        r = lax.axis_index("rep")
        s = lax.axis_index("shard")
        return r, r // 2, r % 2, s // 2, s % 2

    def gather_rep(v):
        far = flip_x(v)
        return v, flip_core(v), far, flip_core(far)

    def gather_shard(v):
        out = []
        for k in range(Z):
            piece = v if k == 0 else rot_z(v, k)
            out += [piece, flip_y(piece)]
        return out

    def from_shard(p, z, y):
        return 2 * lax.rem(z - p // 2 + Z, Z) + (y if p % 2 == 0 else 1 - y)

    def ring_shard(v):
        out = []
        for k in range(Z):
            piece = v if k == 0 else rot_z(piece, 1)
            out += [piece, flip_y(piece)]
        return out

    def to_shard(k, b, z, y):
        return 2 * lax.rem(z + k, Z) + (y if b == 0 else 1 - y)

    def swap_z(v):
        groups = [[2 * i + j for i in range(Z)] for j in range(2)]
        return lax.all_to_all(v, "shard", 0, 0, axis_index_groups=groups, tiled=True)

    def add_body(mine, got, *outs):
        for k in range(Z):
            total = (mine[k].astype(f32) + got[k].astype(f32)).astype(bf16)
            if len(outs) == 1:
                outs[0][k] = total
            else:
                outs[k][...] = total

    def sum_body(*refs):
        parts = [refs[0][k] for k in range(Z)] if len(refs) == 2 else [r[...] for r in refs[:-1]]
        total = parts[0].astype(f32)
        for part in parts[1:]:
            total = total + part.astype(f32)
        refs[-1][...] = total.astype(bf16)

    def half_sum(mine, got, name, split, after=()):
        shape = sds(mine.shape[1:])
        outs = (shape,) * Z if split else sds(mine.shape)
        add = call(add_body, outs, [LOAD, VMEM], name=name + "_add", after=after, token=True)
        return add(mine, got)

    def turn_z(parts):
        return [parts[0]] + [rot_z(parts[k], k) for k in range(1, Z)]

    def part_sum(parts, name, after=()):
        shape = parts[0].shape if len(parts) > 1 else parts[0].shape[1:]
        specs = [VMEM] * len(parts)
        return call(sum_body, sds(shape), specs, name=name + "_sum", after=after, token=True)(*parts)

    def layer(
        tokens,
        norm_attn,
        w_query,
        w_latent,
        w_key_up,
        w_value_up,
        w_out,
        norm_ffn,
        w_gate,
        w_up,
        w_down,
        cotangent,
    ):
        T, D = tokens.shape
        n_d = w_query.shape[0]
        n_l = w_key_up.shape[1]
        n_f = w_down.shape[0] // R
        p_f = -(-n_f // 16) * 16
        F = S * p_f
        q_c = w_query.shape[1] // R
        FF = S * R * n_f
        cuts = [0]
        for rows in (n_d, n_d, n_l, n_l, n_d, 16):
            cuts.append(cuts[-1] + rows)

        def pack_body(wq, wl, wk, wv, wo, na, nf, out, wo_in, sems):
            r, x, c, _, _ = place()
            wide = pl.ds(pl.multiple_of(r * q_c, q_c), q_c)
            group = pl.ds(pl.multiple_of(x * LAT, LAT), LAT)
            part = pl.ds(pl.multiple_of(c * q_c, q_c), q_c)
            pairs = [
                (wq.at[:, wide], out.at[cuts[0] : cuts[1]]),
                (wl.at[:, group], out.at[cuts[1] : cuts[2]]),
                (wk.at[x, :, part], out.at[cuts[2] : cuts[3]]),
                (wv.at[x, :, part], out.at[cuts[3] : cuts[4]]),
                (wo.at[wide, :], wo_in),
            ]
            run_copies(pairs, sems)
            out[cuts[4] : cuts[5]] = wo_in[...].astype(f32).T.astype(bf16)
            gains = jnp.concatenate([na[...], nf[...]], 1)
            out[cuts[5] : cuts[6]] = jnp.broadcast_to(gains, (16, 2 * n_d))

        pack = call(
            pack_body,
            sds((cuts[6], q_c)),
            [KEEP] * 5 + [LOAD] * 2,
            [pltpu.VMEM((q_c, n_d), bf16), pltpu.SemaphoreType.DMA((5,))],
            name="pack",
        )(
            w_query,
            w_latent,
            w_key_up,
            w_value_up,
            w_out,
            norm_attn.reshape(1, n_d),
            norm_ffn.reshape(1, n_d),
        )

        w_f = D - F
        u_f = F // w_f
        f_rows = [0, n_d, 2 * n_d, 2 * n_d + p_f, 2 * n_d + p_f + p_f // u_f]

        def prep_body(wg, wu, wd, out):
            r = place()[0]
            for j0 in range(0, F, 128):
                s_lo, s_hi = j0 // p_f, (j0 + 127) // p_f
                a = s_lo * R * n_f // 128 * 128
                b = min(-(-(s_hi + 1) * R * n_f // 128) * 128, FF)
                col = j0 + lax.broadcasted_iota(jnp.int32, (b - a, 128), 1)
                row = a + lax.broadcasted_iota(jnp.int32, (b - a, 128), 0)
                pick = jnp.zeros((b - a, 128), jnp.bool_)
                for s in range(s_lo, s_hi + 1):
                    i = col - s * p_f
                    hit = (i >= 0) & (i < n_f) & (row == s * R * n_f + r * n_f + i)
                    pick = pick | hit
                pick = pick.astype(f32).astype(bf16)
                cols = slice(j0, j0 + 128)
                out[f_rows[0] : f_rows[1], cols] = dot_nn(wg[:, a:b], pick).astype(bf16)
                out[f_rows[1] : f_rows[2], cols] = dot_nn(wu[:, a:b], pick).astype(bf16)
            i = lax.broadcasted_iota(jnp.int32, (p_f, R * n_f), 0)
            m = lax.broadcasted_iota(jnp.int32, (p_f, R * n_f), 1)
            pick = ((i < n_f) & (m == r * n_f + i)).astype(f32).astype(bf16)
            down = dot_nn(pick, wd[...])
            out[f_rows[2] : f_rows[3]] = down[:, :F].astype(bf16)
            for u in range(u_f):
                block = down[u * p_f // u_f : (u + 1) * p_f // u_f, F:]
                out[f_rows[3] : f_rows[4], u * w_f : (u + 1) * w_f] = block.astype(bf16)


        toks = gather_rep(tokens)
        packs = gather_shard(pack)
        my_ffn = call(
            prep_body, sds((f_rows[4], F)), [LOAD] * 3, name="prep", after=(pack,)
        )(w_gate, w_up, w_down)
        ffns = ring_shard(my_ffn)
        cots = gather_rep(cotangent)

        def attn_body(*refs):
            tok, pieces = refs[:R], refs[R : R + S]
            normed, q_o, k_o, v_o, lat_o, mixed = refs[R + S : R + S + 6]
            parts, (wq, wl, wk, wv, wo, gains) = refs[R + S + 6 : R + S + 10], refs[R + S + 10 : R + S + 16]
            rows, sems = refs[R + S + 16 :]
            _, _, _, z, y = place()
            pairs = []
            for p, piece in enumerate(pieces):
                s = from_shard(p, z, y)
                at_d = pl.ds(pl.multiple_of(s * n_d, n_d), n_d)
                at_l = pl.ds(pl.multiple_of(s * n_l, n_l), n_l)
                spots = (wq.at[at_d], wl.at[at_d], wk.at[at_l], wv.at[at_l], wo.at[at_d], rows.at[s])
                for i, spot in enumerate(spots):
                    pairs.append((piece.at[pl.ds(cuts[i], cuts[i + 1] - cuts[i])], spot))
            run_copies(pairs, sems)
            for s in range(S):
                both = rows[s][0:1].astype(f32)
                gains[0:1, s * n_d : (s + 1) * n_d] = both[:, :n_d]
                gains[1:2, s * n_d : (s + 1) * n_d] = both[:, n_d : 2 * n_d]
            for j in range(R):
                ins = tok[j][...].astype(f32)
                nrm = (ins * rms_scale(ins) * gains[0:1, :]).astype(bf16)
                normed[j] = nrm
                q = dot_nn(nrm, wq[...]).astype(bf16)
                lat = dot_nn(nrm, wl[...]).astype(bf16)
                k = dot_nn(lat, wk[...]).astype(bf16)
                v = dot_nn(lat, wv[...]).astype(bf16)
                q_o[j], lat_o[j], k_o[j], v_o[j] = q, lat, k, v
                for h in range(0, q_c, 2 * HD):
                    kk, vv = k[:, h : h + 2 * HD], v[:, h : h + 2 * HD]
                    both = []
                    for qm in halves(q[:, h : h + 2 * HD]):
                        both.append(dot_nn(softmax_block(qm, kk).astype(bf16), vv))
                    mixed[j, :, h : h + 2 * HD] = join(*both).astype(bf16)
                parts[j][...] = dot_nt(mixed[j], wo[...]).astype(bf16)

        small = sds((R, T, q_c))
        flat = sds((T, D))
        (normed, q_s, k_s, v_s, lat_s, mixed, *parts, wq, wl, wk, wv, wo, gains) = call(
            attn_body,
            (
                sds((R, T, D)),
                small,
                small,
                small,
                small,
                small,
                flat,
                flat,
                flat,
                flat,
                sds((D, q_c)),
                sds((D, LAT)),
                sds((LAT, q_c)),
                sds((LAT, q_c)),
                sds((D, q_c)),
                sds((8, D), f32),
            ),
            [VMEM] * R + [HBM] * S,
            [pltpu.VMEM((S, 16, q_c), bf16), pltpu.SemaphoreType.DMA((6 * S,))],
            name="attn",
            after=(cots[2], ffns[1]),
        )(*toks, *packs)

        def chip_body(keep, near, out):
            out[...] = (keep[...].astype(f32) + near[...].astype(f32)).astype(bf16)

        def scatter_rep(parts, after=()):
            near_far = flip_core(parts[3])
            near = flip_core(parts[1])
            if after:
                chip = call(chip_body, flat, [VMEM] * 2, name="chip", after=after)(parts[2], near_far)
            else:
                chip = (parts[2].astype(f32) + near_far.astype(f32)).astype(bf16)
            return (parts[0], near, flip_x(chip)), chip

        def own_sum(keep, near, far):
            return keep[...].astype(f32) + near[...].astype(f32) + far[...].astype(f32)

        def norm_body(tok, gains, keep, near, far, residual, normed):
            res = tok[...].astype(f32) + own_sum(keep, near, far)
            residual[...] = res
            normed[...] = (res * rms_scale(res) * gains[1:2, :]).astype(bf16)

        residual, normed_own = call(
            norm_body,
            (sds((T, D), f32), sds((T, D))),
            [VMEM] * 5,
            name="norm",
            after=(ffns[5], ffns[6]),
        )(tokens, gains, *scatter_rep(parts, after=(ffns[3], ffns[4]))[0])
        nffn = gather_rep(normed_own)

        def ffn_body(*refs):
            n_in, cot, pieces = refs[:4], refs[4:8], refs[8 : 8 + S]
            act_o, gg_o, gu_o, *parts, wd_o, wg, wu, sems = refs[8 + S :]
            _, _, _, z, y = place()
            pairs = []
            for p, piece in enumerate(pieces):
                s = from_shard(p, z, y)
                at = pl.ds(pl.multiple_of(s * n_d, n_d), n_d)
                at_f = pl.ds(pl.multiple_of(s * p_f, p_f), p_f)
                pairs.append((piece.at[pl.ds(f_rows[0], n_d)], wg.at[at]))
                pairs.append((piece.at[pl.ds(f_rows[1], n_d)], wu.at[at]))
                left = wd_o.at[at_f, pl.ds(0, F)]
                pairs.append((piece.at[pl.ds(f_rows[2], p_f)], left))
                for u in range(u_f):
                    block = piece.at[pl.ds(f_rows[3], p_f // u_f), pl.ds(u * w_f, w_f)]
                    n_u = p_f // u_f
                    at_u = pl.ds(pl.multiple_of(s * p_f + u * n_u, n_u), n_u)
                    pairs.append((block, wd_o.at[at_u, pl.ds(F, w_f)]))
            run_copies(pairs, sems)
            for j in range(R):
                n = n_in[j][...]
                gate = dot_nn(n, wg[...])
                up = dot_nn(n, wu[...])
                g_act = dot_nt(cot[j][...], wd_o[...])
                sig = jax.nn.sigmoid(gate)
                silu = gate * sig
                act_o[j] = (silu * up).astype(bf16)
                gg = (g_act * up * sig * (1.0 + gate * (1.0 - sig))).astype(bf16)
                gu = (g_act * silu).astype(bf16)
                gg_o[j], gu_o[j] = gg, gu
                back = dot_nt(gg, wg[...]) + dot_nt(gu, wu[...])
                parts[j][...] = back.astype(bf16)

        hid = sds((R, T, F))
        act, g_gate, g_up, *parts, wd = call(
            ffn_body,
            (hid, hid, hid, flat, flat, flat, flat, sds((F, D))),
            [VMEM] * 8 + [HBM] * S,
            [
                pltpu.VMEM((D, F), bf16),
                pltpu.VMEM((D, F), bf16),
                pltpu.SemaphoreType.DMA(((3 + u_f) * S,)),
            ],
            name="ffn",
        )(*nffn, *cots, *ffns)
        back, chip = scatter_rep(parts)

        def down_body(act, c0, c1, c2, c3, out):
            cot = jnp.concatenate([c0[...], c1[...], c2[...], c3[...]], 0)
            full = dot_tn(act[...].reshape(R * T, F), cot).astype(bf16)
            out[...] = full.reshape(Z, 2 * p_f, D)

        def hidden_body(n0, n1, n2, n3, gg, gu, mine, give, full):
            y = place()[4]
            n_all = jnp.concatenate([n0[...], n1[...], n2[...], n3[...]], 0)
            for i, grad in enumerate((gg, gu)):
                full[...] = dot_tn(n_all, grad[...].reshape(R * T, F)).astype(bf16)
                for k in range(Z):
                    for b, out in enumerate((mine, give)):
                        s = 2 * k + (y if b == 0 else 1 - y)
                        rows = full[pl.ds(pl.multiple_of(s * n_d, n_d), n_d), :]
                        out[k, i * n_d : (i + 1) * n_d] = rows

        piece = sds((Z, 2 * n_d, F))
        (m_h, e_h), t_hid = call(
            hidden_body,
            (piece, piece),
            [VMEM] * 6,
            [pltpu.VMEM((D, F), bf16)],
            name="ghid",
            after=(chip,),
            token=True,
        )(*nffn, g_gate, g_up)
        g_down, t_down = call(
            down_body, sds((Z, 2 * p_f, D)), [VMEM] * 5, name="gdown", token=True
        )(act, *cots)
        moved_d = swap_z(g_down)

        def part_body(act, wd, *parts):
            for j in range(R):
                parts[j][...] = dot_nn(act[j], wd[...]).astype(bf16)

        def back_norm(ins, grad, gain):
            scale = rms_scale(ins)
            u = grad * gain
            return scale * u - ins * scale**3 * jnp.mean(u * ins, axis=-1, keepdims=True)

        def res_body(cot, res, gains, keep, near, far, g_res, g_attn):
            grad = back_norm(res[...], own_sum(keep, near, far), gains[1:2, :])
            grad = cot[...].astype(f32) + grad
            g_res[...] = grad
            g_attn[...] = grad.astype(bf16)

        (grad_res, g_attn), t_res = call(
            res_body,
            (sds((T, D), f32), flat),
            [LOAD, LOAD, VMEM, LOAD, VMEM, VMEM],
            name="gres",
            after=(t_down, t_hid),
            token=True,
        )(cotangent, residual, gains, *back)
        part, t_part = call(
            part_body, (flat,) * R, [VMEM, LOAD], name="part", after=(t_res,), token=True
        )(act, wd)
        out_back, out_chip = scatter_rep(part, after=(t_res,))

        def out_body(res, keep, near, far, out):
            out[...] = (res[...] + own_sum(keep, near, far)).astype(bf16)

        output, t_out = call(
            out_body, flat, [LOAD, LOAD, VMEM, VMEM], name="outsum", token=True
        )(residual, *out_back)

        def attn_back_body(first, g0, g1, q_s, k_s, v_s, wk, wv, wo, gq_o, gk_o, gv_o, gl_o):
            for j, ga in enumerate((g0, g1)):
                gm = dot_nn(ga[...], wo[...]).astype(bf16)
                q, k, v = q_s[first + j], k_s[first + j], v_s[first + j]
                for h in range(0, q_c, 2 * HD):
                    cols = slice(h, h + 2 * HD)
                    qq, kk, vv, gg = q[:, cols], k[:, cols], v[:, cols], gm[:, cols]
                    gqs, gks, gvs = [], [], []
                    for qm, gmm in zip(halves(qq), halves(gg)):
                        probs = softmax_block(qm, kk)
                        gp = dot_nt(gmm, vv)
                        gs = probs * (gp - jnp.sum(probs * gp, axis=-1, keepdims=True))
                        gs = gs.astype(bf16)
                        gqs.append(dot_nn(gs, kk))
                        gks.append(dot_tn(gs, qq))
                        gvs.append(dot_tn(probs.astype(bf16), gg))
                    gq_o[j, :, cols] = (join(*gqs) * HD**-0.5).astype(bf16)
                    gk_o[j, :, cols] = (join(*gks) * HD**-0.5).astype(bf16)
                    gv_o[j, :, cols] = join(*gvs).astype(bf16)
                gl_o[j] = (dot_nt(gk_o[j], wk[...]) + dot_nt(gv_o[j], wv[...])).astype(bf16)

        def attn_back(first, grads, after):
            pair = sds((2, T, q_c))
            return call(
                functools.partial(attn_back_body, first),
                (pair,) * 4,
                [VMEM] * 8,
                name="attnback",
                after=after,
                token=True,
            )(*grads, q_s, k_s, v_s, wk, wv, wo)

        near = (g_attn, flip_core(g_attn))
        near_back, t_near = attn_back(0, near, (t_part, out_chip))
        far = hold(flip_x(g_attn), (t_near,))
        far = (far, flip_core(far))
        far_back, t_far = attn_back(2, far, ())
        g_attns = near + far

        def weights_body(*refs):
            ga, near, far, (mixed, lat_s, normed) = refs[:R], refs[4:8], refs[8:12], refs[12:15]
            mine, give, f_wide, f_low = refs[15:]
            _, _, _, z, y = place()
            gq, gk, gv, gl = (
                jnp.concatenate([a[...], b[...]], 0).reshape(R * T, q_c) for a, b in zip(near, far)
            )
            n_all = normed[...].reshape(R * T, D)
            lat = lat_s[...].reshape(R * T, LAT)
            g_all = jnp.concatenate([g[...] for g in ga], 0)
            f_wide[0] = dot_tn(n_all, gq).astype(bf16)
            f_wide[1] = dot_tn(n_all, gl).astype(bf16)
            f_wide[2] = dot_tn(g_all, mixed[...].reshape(R * T, q_c)).astype(bf16)
            f_low[0] = dot_tn(lat, gk).astype(bf16)
            f_low[1] = dot_tn(lat, gv).astype(bf16)
            for k in range(Z):
                for b, out in enumerate((mine, give)):
                    s = to_shard(k, b, z, y)
                    at_d = pl.ds(pl.multiple_of(s * n_d, n_d), n_d)
                    at_l = pl.ds(pl.multiple_of(s * n_l, n_l), n_l)
                    out[k, cuts[0] : cuts[1]] = f_wide[0, at_d, :]
                    out[k, cuts[1] : cuts[2]] = f_wide[1, at_d, :]
                    out[k, cuts[2] : cuts[3]] = f_low[0, at_l, :]
                    out[k, cuts[3] : cuts[4]] = f_low[1, at_l, :]
                    out[k, cuts[4] : cuts[5]] = f_wide[2, at_d, :]

        got_h = flip_y(e_h)
        half_h, t_half = half_sum(m_h, got_h, "hid", False, after=(t_far,))
        piece = sds((Z, cuts[5], q_c))
        (m_p, e_p), t_back = call(
            weights_body,
            (piece, piece),
            [VMEM] * 15,
            [pltpu.VMEM((3, D, q_c), bf16), pltpu.VMEM((2, LAT, q_c), bf16)],
            name="wback",
            after=(t_half,),
            token=True,
        )(*g_attns, *near_back, *far_back, mixed, lat_s, normed)

        def down_sum_body(parts, mine, give):
            y = place()[4]
            total = parts[0].astype(f32)
            for k in range(1, Z):
                total = total + parts[k].astype(f32)
            low, high = total[:p_f], total[p_f:]
            mine[...] = jnp.where(y == 0, low, high).astype(bf16)
            give[...] = jnp.where(y == 0, high, low).astype(bf16)

        slab = sds((p_f, D))
        (mine_d, give_d), t_dsum = call(
            down_sum_body, (slab, slab), [VMEM], name="dsum", after=(t_back,), token=True
        )(moved_d)
        own_d = (mine_d.astype(f32) + flip_y(give_d).astype(f32)).astype(bf16)
        sum_dn = gather_rep(own_d)

        def in_body(gq0, gl0, gq1, gl1, wq, wl, *parts):
            for j, (gq, gl) in enumerate(((gq0, gl0), (gq1, gl1))):
                for i in range(2):
                    back = dot_nt(gq[i], wq[...]) + dot_nt(gl[i], wl[...])
                    parts[2 * j + i][...] = back.astype(bf16)

        got_p = flip_y(e_p)
        ins_part, t_in = call(
            in_body, (flat,) * R, [VMEM] * 4 + [LOAD] * 2, name="inback", after=(t_back,), token=True
        )(near_back[0], near_back[3], far_back[0], far_back[3], wq, wl)
        half_p, t_pack = half_sum(m_p, got_p, "pack", True, after=(t_half, t_in, t_out, t_dsum))
        ins_back = scatter_rep(ins_part, after=(t_pack,))[0]

        def tok_body(tok, g_res, gains, keep, near, far, out):
            grad = back_norm(tok[...].astype(f32), own_sum(keep, near, far), gains[0:1, :])
            out[...] = (g_res[...] + grad).astype(bf16)

        grad_tokens, t_tok = call(
            tok_body, flat, [LOAD, LOAD, VMEM, LOAD, VMEM, VMEM], name="gtok", token=True
        )(
            tokens, grad_res, gains, *ins_back
        )

        own_h, t_sum = part_sum([swap_z(half_h)], "hid", after=(t_pack, t_tok))
        own_p, _ = part_sum(turn_z(half_p), "pack", after=(t_sum,))
        sum_h = gather_rep(own_h)
        sum_p = gather_rep(own_p)

        def lane_sum(v):
            total = v[:, :128]
            for j in range(128, v.shape[1], 128):
                total = total + v[:, j : j + 128]
            return jnp.sum(total.T, axis=0, keepdims=True)

        def final_hidden_body(*refs):
            d_in, (v0, v1, v2, v3, w_g, w_u, nf, out_d, out_g, out_u, dots) = refs[:R], refs[R:]
            r, x, c, _, _ = place()
            for k, d in enumerate(d_in):
                q = lax.bitwise_xor(r, k)
                out_d[pl.ds(pl.multiple_of(q * n_f, 8), n_f), :] = d[...].astype(f32)[:n_f]
            total = 0.0
            for i, (w, out) in enumerate(((w_g, out_g), (w_u, out_u))):
                vs = [v[i * n_d : (i + 1) * n_d].astype(f32) for v in (v0, v1, v2, v3)]
                vs = [jnp.where(c == 1, vs[k ^ 1], vs[k]) for k in range(R)]
                vs = [jnp.where(x == 1, vs[k ^ 2], vs[k]) for k in range(R)]
                for q in range(R):
                    for s in range(S):
                        at = s * R * n_f + q * n_f
                        out[:, at : at + n_f] = vs[q][:, s * p_f : s * p_f + n_f]
                total = total + lane_sum(out[...] * w[...].astype(f32))
            dots[...] = total / nf[...].astype(f32)

        row = sds((1, n_d), f32)
        wide = sds((n_d, FF), f32)
        (g_down, g_gate_w, g_up_w, g_nf), t_hid = call(
            final_hidden_body,
            (sds((R * n_f, D), f32), wide, wide, row),
            [VMEM] * (2 * R) + [LOAD] * 3,
            name="fhid",
            token=True,
        )(*sum_dn, *sum_h, w_gate, w_up, norm_ffn.reshape(1, n_d))

        def final_pack_body(v0, v1, v2, v3, w_q, w_l, na, gq, gl, gk, gv, go, gna):
            r, x, _, _, _ = place()
            vs = (v0, v1, v2, v3)
            for k, v in enumerate(vs):
                q = lax.bitwise_xor(r, k)
                wide = pl.ds(pl.multiple_of(q * q_c, q_c), q_c)
                part = pl.ds(pl.multiple_of((q % 2) * q_c, q_c), q_c)
                gq[:, wide] = v[cuts[0] : cuts[1]].astype(f32)
                gk[q // 2, :, part] = v[cuts[2] : cuts[3]].astype(f32)
                gv[q // 2, :, part] = v[cuts[3] : cuts[4]].astype(f32)
                go[wide, :] = v[cuts[4] : cuts[5]].astype(f32).T
            for k in (0, 2):
                g = lax.bitwise_xor(x, k // 2)
                both = vs[k][cuts[1] : cuts[2]].astype(f32) + vs[k + 1][cuts[1] : cuts[2]].astype(f32)
                gl[:, pl.ds(pl.multiple_of(g * LAT, LAT), LAT)] = both
            dots = lane_sum(gq[...] * w_q[...].astype(f32)) + lane_sum(gl[...] * w_l[...].astype(f32))
            gna[...] = dots / na[...].astype(f32)

        g_query, g_latent, g_key, g_value, g_out, g_na = call(
            final_pack_body,
            (
                sds((n_d, R * q_c), f32),
                sds((n_d, LG * LAT), f32),
                sds((LG, n_l, 2 * q_c), f32),
                sds((LG, n_l, 2 * q_c), f32),
                sds((R * q_c, n_d), f32),
                row,
            ),
            [VMEM] * R + [LOAD] * 3,
            name="fpack",
            after=(t_hid, t_out, t_tok),
        )(*sum_p, w_query, w_latent, norm_attn.reshape(1, n_d))
        return (
            output,
            grad_tokens,
            g_na.reshape(n_d),
            g_query,
            g_latent,
            g_key,
            g_value,
            g_out,
            g_nf.reshape(n_d),
            g_gate_w,
            g_up_w,
            g_down,
        )

    return layer


def make_layer(mesh):
    aligned = (LAT // mesh.shape["shard"]) % 16 == 0
    return make_fast(mesh) if aligned else make_plain(mesh)


def solution(mesh):
    return jax.shard_map(
        make_layer(mesh),
        mesh=mesh,
        in_specs=(
            P(("rep", "shard"), None),
            P("shard"),
            P("shard", None),
            P("shard", None),
            P(None, "shard", None),
            P(None, "shard", None),
            P(None, "shard"),
            P("shard"),
            P("shard", None),
            P("shard", None),
            P("shard", None),
            P(("rep", "shard"), None),
        ),
        out_specs=(
            P(("rep", "shard"), None),
            P(("rep", "shard"), None),
            P("shard"),
            P("shard", None),
            P("shard", None),
            P(None, "shard", None),
            P(None, "shard", None),
            P(None, "shard"),
            P("shard"),
            P("shard", None),
            P("shard", None),
            P("shard", None),
        ),
        check_vma=False,
    )
```

```python
import functools

import jax
import jax.numpy as jnp
from jax import lax
from jax.experimental import pallas as pl
from jax.experimental.pallas import tpu as pltpu
from jax.sharding import PartitionSpec as P

HQ = 16
HD = 64
LG = 2
LAT = 256
SEQ = 256
R = 4
f32 = jnp.float32
bf16 = jnp.bfloat16
epsilon = 1e-05


def rms_scale(rows_in):
    return lax.rsqrt(jnp.mean(rows_in * rows_in, axis=-1, keepdims=True) + epsilon)


def dot_nn(a, b):
    return lax.dot_general(a, b, (((1,), (0,)), ((), ())), preferred_element_type=f32)


def dot_nt(a, b):
    return lax.dot_general(a, b, (((1,), (1,)), ((), ())), preferred_element_type=f32)


def dot_tn(a, b):
    return lax.dot_general(a, b, (((0,), (0,)), ((), ())), preferred_element_type=f32)


def make_plain(mesh):
    S = mesh.shape["shard"]
    Z = S // 2
    assert mesh.shape["rep"] == R

    def flip_core(v):
        return lax.ppermute(v, "rep", [(i, i ^ 1) for i in range(R)])

    def flip_x(v):
        return lax.ppermute(v, "rep", [(i, i ^ 2) for i in range(R)])

    def flip_y(v):
        return lax.ppermute(v, "shard", [(i, i ^ 1) for i in range(S)])

    def rot_z(v, k):
        return lax.ppermute(v, "shard", [(i, (i + 2 * k) % S) for i in range(S)])

    def layer(
        tokens,
        norm_attn,
        w_query,
        w_latent,
        w_key_up,
        w_value_up,
        w_out,
        norm_ffn,
        w_gate,
        w_up,
        w_down,
        cotangent,
    ):
        r = lax.axis_index("rep")
        s = lax.axis_index("shard")
        x, c, z, y = r // 2, r % 2, s // 2, s % 2
        T, D = tokens.shape
        n_d = w_query.shape[0]
        n_l = w_key_up.shape[1]
        n_f = w_down.shape[0] // R
        q_c = w_query.shape[1] // R
        FFq = n_f * S

        def gather_rep(v):
            far = flip_x(v)
            near = flip_core(jnp.stack([v, far]))
            return jnp.stack([v, near[0], far, near[1]])

        def scatter_rep(v):
            near = flip_core(v[1::2].astype(bf16))
            chip = v[0::2] + near
            far = flip_x(chip[1].astype(bf16))
            return chip[0] + far

        def absolute(v):
            v = jnp.where(c == 1, v[jnp.array([1, 0, 3, 2])], v)
            return jnp.where(x == 1, v[jnp.array([2, 3, 0, 1])], v)

        def gather_shard(v):
            full = jnp.zeros((Z, 2) + v.shape, v.dtype)
            zeros = (0,) * v.ndim
            for k in range(Z):
                piece = v if k == 0 else rot_z(v, k)
                other = flip_y(piece)
                at = lax.rem(z - k + Z, Z)
                full = lax.dynamic_update_slice(full, piece[None, None], (at, y) + zeros)
                full = lax.dynamic_update_slice(full, other[None, None], (at, 1 - y) + zeros)
            return full.reshape((S,) + v.shape)

        def scatter_shard(v):
            v = v.reshape((Z, 2) + v.shape[1:])
            mine = lax.dynamic_index_in_dim(v, y, 1, False)
            give = lax.dynamic_index_in_dim(v, 1 - y, 1, False)
            half = (mine.astype(f32) + flip_y(give).astype(f32)).astype(bf16)
            total = lax.dynamic_index_in_dim(half, z, 0, False).astype(f32)
            for k in range(1, Z):
                piece = lax.dynamic_index_in_dim(half, lax.rem(z + k, Z), 0, False)
                total = total + rot_z(piece, k).astype(f32)
            return absolute(gather_rep(total.astype(bf16)))

        my_query = lax.dynamic_slice_in_dim(w_query, r * q_c, q_c, 1)
        my_latent = lax.dynamic_slice_in_dim(w_latent, x * LAT, LAT, 1)
        my_key = lax.dynamic_slice_in_dim(
            lax.dynamic_index_in_dim(w_key_up, x, 0, False), c * q_c, q_c, 1
        )
        my_value = lax.dynamic_slice_in_dim(
            lax.dynamic_index_in_dim(w_value_up, x, 0, False), c * q_c, q_c, 1
        )
        my_out = lax.dynamic_slice_in_dim(w_out, r * q_c, q_c, 0).T
        gains = jnp.zeros((16, q_c), bf16)
        gains = gains.at[0, :n_d].set(norm_attn).at[1, :n_d].set(norm_ffn)
        pack = jnp.concatenate([my_query, my_latent, my_key, my_value, my_out, gains], 0)
        cuts = [n_d, 2 * n_d, 2 * n_d + n_l, 2 * n_d + 2 * n_l, 3 * n_d + 2 * n_l]

        col = lax.broadcasted_iota(jnp.int32, (S * R * n_f, FFq), 1)
        row = lax.broadcasted_iota(jnp.int32, (S * R * n_f, FFq), 0)
        pick = (row == (col // n_f) * (R * n_f) + r * n_f + col % n_f).astype(bf16)
        my_gate_up = dot_nn(jnp.concatenate([w_gate, w_up], 0), pick).astype(bf16)
        my_down = lax.dynamic_slice_in_dim(w_down, r * n_f, n_f, 0)

        all_tokens = gather_rep(tokens).reshape(R * T, D)
        packs = gather_shard(pack)
        all_cot = gather_rep(cotangent).reshape(R * T, D)
        gate_up = gather_shard(my_gate_up)
        down = gather_shard(my_down).reshape(FFq, D)

        query_w = packs[:, : cuts[0]].reshape(D, q_c)
        latent_w = packs[:, cuts[0] : cuts[1]].reshape(D, LAT)
        key_w = packs[:, cuts[1] : cuts[2]].reshape(LAT, q_c)
        value_w = packs[:, cuts[2] : cuts[3]].reshape(LAT, q_c)
        out_w = packs[:, cuts[3] : cuts[4]].reshape(D, q_c)
        gain_attn = packs[:, cuts[4], :n_d].reshape(D).astype(f32)
        gain_ffn = packs[:, cuts[4] + 1, :n_d].reshape(D).astype(f32)
        gate_w = gate_up[:, :n_d].reshape(D, FFq)
        up_w = gate_up[:, n_d:].reshape(D, FFq)

        heads = q_c // HD
        group_in = all_tokens.astype(f32)
        scale_attn = rms_scale(group_in)
        normed_attn = (group_in * scale_attn * gain_attn).astype(bf16)
        queries = dot_nn(normed_attn, query_w).astype(bf16)
        latents = dot_nn(normed_attn, latent_w).astype(bf16)
        keys = dot_nn(latents, key_w).astype(bf16)
        values = dot_nn(latents, value_w).astype(bf16)
        qh = queries.reshape(R, T, heads, HD)
        kh = keys.reshape(R, T, heads, HD)
        vh = values.reshape(R, T, heads, HD)
        row_ids = lax.broadcasted_iota(jnp.int32, (SEQ, SEQ), 0)
        col_ids = lax.broadcasted_iota(jnp.int32, (SEQ, SEQ), 1)
        scores = jnp.einsum("bqhd,bkhd->bhqk", qh, kh, preferred_element_type=f32) * HD**-0.5
        scores = jnp.where(col_ids <= row_ids, scores, -1e30)
        maxima = jnp.max(scores, axis=-1, keepdims=True)
        exps = jnp.exp(scores - maxima)
        probs = exps / jnp.sum(exps, axis=-1, keepdims=True)
        low_probs = probs.astype(bf16)
        mixed = jnp.einsum("bhqk,bkhd->bqhd", low_probs, vh, preferred_element_type=f32)
        mixed = mixed.astype(bf16).reshape(R * T, q_c)
        attn_part = dot_nt(mixed, out_w).reshape(R, T, D)
        inputs = tokens.astype(f32)
        residual = inputs + scatter_rep(attn_part)
        scale_ffn = rms_scale(residual)
        normed_own = (residual * scale_ffn * gain_ffn).astype(bf16)
        normed_ffn = gather_rep(normed_own).reshape(R * T, D)

        gate_proj = dot_nn(normed_ffn, gate_w)
        up_proj = dot_nn(normed_ffn, up_w)
        sig = jax.nn.sigmoid(gate_proj)
        silu = gate_proj * sig
        activated = (silu * up_proj).astype(bf16)
        grad_down = dot_tn(activated, all_cot).astype(bf16).reshape(S, n_f, D)
        grad_act = dot_nt(all_cot, down)
        grad_gate = (grad_act * up_proj * sig * (1.0 + gate_proj * (1.0 - sig))).astype(bf16)
        grad_up = (grad_act * silu).astype(bf16)
        grad_gate_w = dot_tn(normed_ffn, grad_gate).astype(bf16).reshape(S, n_d, FFq)
        grad_up_w = dot_tn(normed_ffn, grad_up).astype(bf16).reshape(S, n_d, FFq)
        ffn_back = dot_nt(grad_gate, gate_w) + dot_nt(grad_up, up_w)
        grad_normed_ffn = scatter_rep(ffn_back.reshape(R, T, D))
        ffn_part = dot_nn(activated, down).reshape(R, T, D)
        output = (residual + scatter_rep(ffn_part)).astype(bf16)

        weighted = grad_normed_ffn * gain_ffn
        grad_residual = (
            cotangent.astype(f32)
            + scale_ffn * weighted
            - residual * scale_ffn**3 * jnp.mean(weighted * residual, axis=-1, keepdims=True)
        )
        grad_attn = gather_rep(grad_residual.astype(bf16)).reshape(R * T, D)

        grad_out_w = dot_tn(grad_attn, mixed).astype(bf16)
        grad_mixed = dot_nn(grad_attn, out_w).astype(bf16).reshape(R, T, heads, HD)
        grad_probs = jnp.einsum("bqhd,bkhd->bhqk", grad_mixed, vh, preferred_element_type=f32)
        grad_scores = (
            probs * (grad_probs - jnp.sum(probs * grad_probs, axis=-1, keepdims=True))
        ).astype(bf16)
        grad_q = jnp.einsum("bhqk,bkhd->bqhd", grad_scores, kh, preferred_element_type=f32)
        grad_k = jnp.einsum("bhqk,bqhd->bkhd", grad_scores, qh, preferred_element_type=f32)
        grad_v = jnp.einsum("bhqk,bqhd->bkhd", low_probs, grad_mixed, preferred_element_type=f32)
        grad_q = (grad_q * HD**-0.5).astype(bf16).reshape(R * T, q_c)
        grad_k = (grad_k * HD**-0.5).astype(bf16).reshape(R * T, q_c)
        grad_v = grad_v.astype(bf16).reshape(R * T, q_c)
        grad_key_w = dot_tn(latents, grad_k).astype(bf16)
        grad_value_w = dot_tn(latents, grad_v).astype(bf16)
        grad_query_w = dot_tn(normed_attn, grad_q).astype(bf16)
        lat_part = (dot_nt(grad_k, key_w) + dot_nt(grad_v, value_w)).reshape(R, T, LAT)
        near = flip_core(lat_part[1::2])
        grad_lat = (lat_part[0::2] + near).astype(bf16).reshape(2 * T, LAT)
        half_normed = normed_attn.reshape(R, T, D)[0::2].reshape(2 * T, D)
        grad_latent_w = dot_tn(half_normed, grad_lat).astype(bf16)
        attn_back = dot_nt(grad_q, query_w).reshape(R, T, D)
        lat_back = dot_nt(grad_lat, latent_w).reshape(2, T, D)
        attn_back = jnp.stack(
            [attn_back[0] + lat_back[0], attn_back[1], attn_back[2] + lat_back[1], attn_back[3]]
        )
        grad_normed_attn = scatter_rep(attn_back)
        weighted = grad_normed_attn * gain_attn
        scale_own = rms_scale(inputs)
        grad_tokens = (
            grad_residual
            + scale_own * weighted
            - inputs * scale_own**3 * jnp.mean(weighted * inputs, axis=-1, keepdims=True)
        ).astype(bf16)

        sum_down = scatter_shard(grad_down)
        sum_gate = scatter_shard(grad_gate_w)
        sum_up = scatter_shard(grad_up_w)
        grad_pack = jnp.concatenate(
            [
                grad_query_w.reshape(S, n_d, q_c),
                grad_latent_w.reshape(S, n_d, LAT),
                grad_key_w.reshape(S, n_l, q_c),
                grad_value_w.reshape(S, n_l, q_c),
                grad_out_w.reshape(S, n_d, q_c),
            ],
            1,
        )
        sum_pack = scatter_shard(grad_pack).astype(f32)
        g_query = sum_pack[:, : cuts[0]].transpose(1, 0, 2).reshape(n_d, R * q_c)
        g_latent = sum_pack[:, cuts[0] : cuts[1]]
        g_latent = jnp.concatenate([g_latent[0] + g_latent[1], g_latent[2] + g_latent[3]], 1)
        g_key = sum_pack[:, cuts[1] : cuts[2]].reshape(LG, 2, n_l, q_c)
        g_key = g_key.transpose(0, 2, 1, 3).reshape(LG, n_l, 2 * q_c)
        g_value = sum_pack[:, cuts[2] : cuts[3]].reshape(LG, 2, n_l, q_c)
        g_value = g_value.transpose(0, 2, 1, 3).reshape(LG, n_l, 2 * q_c)
        g_out = sum_pack[:, cuts[3] : cuts[4]].transpose(0, 2, 1).reshape(R * q_c, n_d)
        g_down = sum_down.reshape(R * n_f, D).astype(f32)

        def spread(v):
            v = v.reshape(R, n_d, S, n_f).transpose(1, 2, 0, 3)
            return v.reshape(n_d, S * R * n_f).astype(f32)

        g_gate = spread(sum_gate)
        g_up = spread(sum_up)
        g_norm_attn = (
            jnp.sum(g_query * w_query.astype(f32), axis=1)
            + jnp.sum(g_latent * w_latent.astype(f32), axis=1)
        ) / norm_attn.astype(f32)
        g_norm_ffn = (
            jnp.sum(g_gate * w_gate.astype(f32), axis=1) + jnp.sum(g_up * w_up.astype(f32), axis=1)
        ) / norm_ffn.astype(f32)
        return (
            output,
            grad_tokens,
            g_norm_attn,
            g_query,
            g_latent,
            g_key,
            g_value,
            g_out,
            g_norm_ffn,
            g_gate,
            g_up,
            g_down,
        )

    return layer


HBM = pl.BlockSpec(memory_space=pl.ANY)
VMEM = pl.BlockSpec(memory_space=pltpu.VMEM)
LOAD = pl.BlockSpec(memory_space=pltpu.HBM)
KEEP = pl.BlockSpec(memory_space=pltpu.HBM)


def sds(shape, dtype=bf16):
    return jax.ShapeDtypeStruct(shape, dtype)


def call(body, outs, in_specs, scratch=(), name=None, after=(), token=False):
    n, flat = len(in_specs), isinstance(outs, tuple)
    loads = [i for i, spec in enumerate(in_specs) if spec is LOAD]

    def run(*refs):
        ins, rest = list(refs[:n]), list(refs[n + len(after) :])
        if token:
            mark = rest.pop(len(outs) if flat else 1)
            mark[...] = jnp.zeros_like(mark)
        if loads:
            sems, buffers = rest[-1], rest[-1 - len(loads) : -1]
            rest = rest[: -1 - len(loads)]
            run_copies([(ins[i], buffer) for i, buffer in zip(loads, buffers)], sems)
            for i, buffer in zip(loads, buffers):
                ins[i] = buffer
        body(*ins, *rest)

    def bind(*args):
        shapes = outs if flat else (outs,)
        if token:
            shapes = shapes + (sds((8, 128), f32),)
        extra = [pltpu.VMEM(args[i].shape, args[i].dtype) for i in loads]
        if loads:
            extra.append(pltpu.SemaphoreType.DMA((len(loads),)))
        result = pl.pallas_call(
            run,
            out_shape=shapes,
            in_specs=list(in_specs) + [HBM] * len(after),
            out_specs=tuple(VMEM for _ in shapes),
            scratch_shapes=list(scratch) + extra,
            compiler_params=pltpu.CompilerParams(
                vmem_limit_bytes=LIMITS.get(name, 24 if name in WIDE else 8) * 1024 * 1024
            ),
            cost_estimate=pl.CostEstimate(
                flops=0, bytes_accessed=COSTS.get(name, 2500) * 3000, transcendentals=0
            ),
            name=name,
        )(*args, *after)
        if token:
            main = result[:-1] if flat else result[0]
            return main, result[-1]
        return result if flat else result[0]

    return bind


WIDE = ("attn", "ffn", "attnback", "wback", "ghid", "gdown", "part", "inback", "fhid")
LIMITS = {"pack": 60, "wback": 54, "attnback": 54}
COSTS = {
    "pack": 2000,
    "prep": 4500,
    "attn": 11300,
    "norm": 3300,
    "ffn": 15300,
    "ghid": 8500,
    "gdown": 5000,
    "part": 500,
    "gres": 3900,
    "attnback": 1000,
    "wback": 4000,
    "chip": 300,
    "inback": 4000,
}


def hold(v, after):
    def body(*refs):
        pass

    return pl.pallas_call(
        body,
        out_shape=sds(v.shape, v.dtype),
        in_specs=[HBM] * (1 + len(after)),
        out_specs=HBM,
        input_output_aliases={0: 0},
        name="hold",
    )(v, *after)


def run_copies(pairs, sems):
    copies = [pltpu.make_async_copy(a, b, sems.at[i]) for i, (a, b) in enumerate(pairs)]
    for copy in copies:
        copy.start()
    for copy in copies:
        copy.wait()


def halves(v):
    low = lax.broadcasted_iota(jnp.int32, v.shape, 1) < HD
    zero = jnp.zeros_like(v)
    return jnp.where(low, v, zero), jnp.where(low, zero, v)


def join(a, b):
    return jnp.where(lax.broadcasted_iota(jnp.int32, a.shape, 1) < HD, a, b)


def softmax_block(qm, k):
    scores = dot_nt(qm, k) * HD**-0.5
    row_ids = lax.broadcasted_iota(jnp.int32, scores.shape, 0)
    col_ids = lax.broadcasted_iota(jnp.int32, scores.shape, 1)
    scores = jnp.where(col_ids <= row_ids, scores, -1e30)
    exps = jnp.exp(scores - jnp.max(scores, axis=-1, keepdims=True))
    return exps * (1.0 / jnp.sum(exps, axis=-1, keepdims=True))


def make_fast(mesh):
    S = mesh.shape["shard"]
    Z = S // 2

    def flip_core(v):
        return lax.ppermute(v, "rep", [(i, i ^ 1) for i in range(R)])

    def flip_x(v):
        return lax.ppermute(v, "rep", [(i, i ^ 2) for i in range(R)])

    def flip_y(v):
        return lax.ppermute(v, "shard", [(i, i ^ 1) for i in range(S)])

    def rot_z(v, k):
        return lax.ppermute(v, "shard", [(i, (i + 2 * k) % S) for i in range(S)])

    def place():
        r = lax.axis_index("rep")
        s = lax.axis_index("shard")
        return r, r // 2, r % 2, s // 2, s % 2

    def gather_rep(v):
        far = flip_x(v)
        return v, flip_core(v), far, flip_core(far)

    def gather_shard(v):
        out = []
        for k in range(Z):
            piece = v if k == 0 else rot_z(v, k)
            out += [piece, flip_y(piece)]
        return out

    def from_shard(p, z, y):
        return 2 * lax.rem(z - p // 2 + Z, Z) + (y if p % 2 == 0 else 1 - y)

    def ring_shard(v):
        out = []
        for k in range(Z):
            piece = v if k == 0 else rot_z(piece, 1)
            out += [piece, flip_y(piece)]
        return out

    def to_shard(k, b, z, y):
        return 2 * lax.rem(z + k, Z) + (y if b == 0 else 1 - y)

    def swap_z(v):
        groups = [[2 * i + j for i in range(Z)] for j in range(2)]
        return lax.all_to_all(v, "shard", 0, 0, axis_index_groups=groups, tiled=True)

    def add_body(mine, got, *outs):
        for k in range(Z):
            total = (mine[k].astype(f32) + got[k].astype(f32)).astype(bf16)
            if len(outs) == 1:
                outs[0][k] = total
            else:
                outs[k][...] = total

    def sum_body(*refs):
        parts = [refs[0][k] for k in range(Z)] if len(refs) == 2 else [r[...] for r in refs[:-1]]
        total = parts[0].astype(f32)
        for part in parts[1:]:
            total = total + part.astype(f32)
        refs[-1][...] = total.astype(bf16)

    def half_sum(mine, got, name, split, after=()):
        shape = sds(mine.shape[1:])
        outs = (shape,) * Z if split else sds(mine.shape)
        add = call(add_body, outs, [LOAD, VMEM], name=name + "_add", after=after, token=True)
        return add(mine, got)

    def turn_z(parts):
        return [parts[0]] + [rot_z(parts[k], k) for k in range(1, Z)]

    def part_sum(parts, name, after=()):
        shape = parts[0].shape if len(parts) > 1 else parts[0].shape[1:]
        specs = [VMEM] * len(parts)
        return call(sum_body, sds(shape), specs, name=name + "_sum", after=after, token=True)(*parts)

    def layer(
        tokens,
        norm_attn,
        w_query,
        w_latent,
        w_key_up,
        w_value_up,
        w_out,
        norm_ffn,
        w_gate,
        w_up,
        w_down,
        cotangent,
    ):
        T, D = tokens.shape
        n_d = w_query.shape[0]
        n_l = w_key_up.shape[1]
        n_f = w_down.shape[0] // R
        p_f = -(-n_f // 16) * 16
        F = S * p_f
        q_c = w_query.shape[1] // R
        FF = S * R * n_f
        cuts = [0]
        for rows in (n_d, n_d, n_l, n_l, n_d, 16):
            cuts.append(cuts[-1] + rows)

        def pack_body(wq, wl, wk, wv, wo, na, nf, out, wo_in, sems):
            r, x, c, _, _ = place()
            wide = pl.ds(pl.multiple_of(r * q_c, q_c), q_c)
            group = pl.ds(pl.multiple_of(x * LAT, LAT), LAT)
            part = pl.ds(pl.multiple_of(c * q_c, q_c), q_c)
            pairs = [
                (wq.at[:, wide], out.at[cuts[0] : cuts[1]]),
                (wl.at[:, group], out.at[cuts[1] : cuts[2]]),
                (wk.at[x, :, part], out.at[cuts[2] : cuts[3]]),
                (wv.at[x, :, part], out.at[cuts[3] : cuts[4]]),
                (wo.at[wide, :], wo_in),
            ]
            run_copies(pairs, sems)
            out[cuts[4] : cuts[5]] = wo_in[...].astype(f32).T.astype(bf16)
            gains = jnp.concatenate([na[...], nf[...]], 1)
            out[cuts[5] : cuts[6]] = jnp.broadcast_to(gains, (16, 2 * n_d))

        pack = call(
            pack_body,
            sds((cuts[6], q_c)),
            [KEEP] * 5 + [VMEM] * 2,
            [pltpu.VMEM((q_c, n_d), bf16), pltpu.SemaphoreType.DMA((5,))],
            name="pack",
        )(
            w_query,
            w_latent,
            w_key_up,
            w_value_up,
            w_out,
            norm_attn.reshape(1, n_d),
            norm_ffn.reshape(1, n_d),
        )

        w_f = D - F
        u_f = F // w_f
        f_rows = [0, n_d, 2 * n_d, 2 * n_d + p_f, 2 * n_d + p_f + p_f // u_f]

        def prep_body(wg, wu, wd, out):
            r = place()[0]
            for j0 in range(0, F, 128):
                s_lo, s_hi = j0 // p_f, (j0 + 127) // p_f
                a = s_lo * R * n_f // 128 * 128
                b = min(-(-(s_hi + 1) * R * n_f // 128) * 128, FF)
                col = j0 + lax.broadcasted_iota(jnp.int32, (b - a, 128), 1)
                row = a + lax.broadcasted_iota(jnp.int32, (b - a, 128), 0)
                pick = jnp.zeros((b - a, 128), jnp.bool_)
                for s in range(s_lo, s_hi + 1):
                    i = col - s * p_f
                    hit = (i >= 0) & (i < n_f) & (row == s * R * n_f + r * n_f + i)
                    pick = pick | hit
                pick = pick.astype(f32).astype(bf16)
                cols = slice(j0, j0 + 128)
                out[f_rows[0] : f_rows[1], cols] = dot_nn(wg[:, a:b], pick).astype(bf16)
                out[f_rows[1] : f_rows[2], cols] = dot_nn(wu[:, a:b], pick).astype(bf16)
            i = lax.broadcasted_iota(jnp.int32, (p_f, R * n_f), 0)
            m = lax.broadcasted_iota(jnp.int32, (p_f, R * n_f), 1)
            pick = ((i < n_f) & (m == r * n_f + i)).astype(f32).astype(bf16)
            down = dot_nn(pick, wd[...])
            out[f_rows[2] : f_rows[3]] = down[:, :F].astype(bf16)
            for u in range(u_f):
                block = down[u * p_f // u_f : (u + 1) * p_f // u_f, F:]
                out[f_rows[3] : f_rows[4], u * w_f : (u + 1) * w_f] = block.astype(bf16)


        toks = gather_rep(tokens)
        packs = gather_shard(pack)
        my_ffn = call(
            prep_body, sds((f_rows[4], F)), [LOAD] * 3, name="prep", after=(pack,)
        )(w_gate, w_up, w_down)
        ffns = ring_shard(my_ffn)
        cots = gather_rep(cotangent)

        def attn_body(*refs):
            tok, pieces = refs[:R], refs[R : R + S]
            normed, q_o, k_o, v_o, lat_o, mixed = refs[R + S : R + S + 6]
            parts, (wq, wl, wk, wv, wo, gains) = refs[R + S + 6 : R + S + 10], refs[R + S + 10 : R + S + 16]
            rows, sems = refs[R + S + 16 :]
            _, _, _, z, y = place()
            pairs = []
            for p, piece in enumerate(pieces):
                s = from_shard(p, z, y)
                at_d = pl.ds(pl.multiple_of(s * n_d, n_d), n_d)
                at_l = pl.ds(pl.multiple_of(s * n_l, n_l), n_l)
                spots = (wq.at[at_d], wl.at[at_d], wk.at[at_l], wv.at[at_l], wo.at[at_d], rows.at[s])
                for i, spot in enumerate(spots):
                    pairs.append((piece.at[pl.ds(cuts[i], cuts[i + 1] - cuts[i])], spot))
            run_copies(pairs, sems)
            for s in range(S):
                both = rows[s].astype(f32)[0:1]
                gains[0:1, s * n_d : (s + 1) * n_d] = both[:, :n_d]
                gains[1:2, s * n_d : (s + 1) * n_d] = both[:, n_d : 2 * n_d]
            for j in range(R):
                ins = tok[j][...].astype(f32)
                nrm = (ins * rms_scale(ins) * gains[0:1, :]).astype(bf16)
                normed[j] = nrm
                q = dot_nn(nrm, wq[...]).astype(bf16)
                lat = dot_nn(nrm, wl[...]).astype(bf16)
                k = dot_nn(lat, wk[...]).astype(bf16)
                v = dot_nn(lat, wv[...]).astype(bf16)
                q_o[j], lat_o[j], k_o[j], v_o[j] = q, lat, k, v
                for h in range(0, q_c, 2 * HD):
                    kk, vv = k[:, h : h + 2 * HD], v[:, h : h + 2 * HD]
                    both = []
                    for qm in halves(q[:, h : h + 2 * HD]):
                        both.append(dot_nn(softmax_block(qm, kk).astype(bf16), vv))
                    mixed[j, :, h : h + 2 * HD] = join(*both).astype(bf16)
                parts[j][...] = dot_nt(mixed[j], wo[...]).astype(bf16)

        small = sds((R, T, q_c))
        flat = sds((T, D))
        (normed, q_s, k_s, v_s, lat_s, mixed, *parts, wq, wl, wk, wv, wo, gains) = call(
            attn_body,
            (
                sds((R, T, D)),
                small,
                small,
                small,
                small,
                small,
                flat,
                flat,
                flat,
                flat,
                sds((D, q_c)),
                sds((D, LAT)),
                sds((LAT, q_c)),
                sds((LAT, q_c)),
                sds((D, q_c)),
                sds((8, D), f32),
            ),
            [VMEM] * R + [HBM] * S,
            [pltpu.VMEM((S, 16, q_c), bf16), pltpu.SemaphoreType.DMA((6 * S,))],
            name="attn",
            after=(cots[2], ffns[1]),
        )(*toks, *packs)

        def chip_body(keep, near, out):
            out[...] = (keep[...].astype(f32) + near[...].astype(f32)).astype(bf16)

        def scatter_rep(parts, after=()):
            near_far = flip_core(parts[3])
            near = flip_core(parts[1])
            if after:
                chip = call(chip_body, flat, [VMEM] * 2, name="chip", after=after)(parts[2], near_far)
            else:
                chip = (parts[2].astype(f32) + near_far.astype(f32)).astype(bf16)
            return (parts[0], near, flip_x(chip)), chip

        def own_sum(keep, near, far):
            return keep[...].astype(f32) + near[...].astype(f32) + far[...].astype(f32)

        def norm_body(tok, gains, keep, near, far, residual, normed):
            res = tok[...].astype(f32) + own_sum(keep, near, far)
            residual[...] = res
            normed[...] = (res * rms_scale(res) * gains[1:2, :]).astype(bf16)

        residual, normed_own = call(
            norm_body,
            (sds((T, D), f32), sds((T, D))),
            [VMEM] * 5,
            name="norm",
            after=(ffns[5], ffns[6]),
        )(tokens, gains, *scatter_rep(parts, after=(ffns[3], ffns[4]))[0])
        nffn = gather_rep(normed_own)

        def ffn_body(*refs):
            n_in, cot, pieces = refs[:4], refs[4:8], refs[8 : 8 + S]
            act_o, gg_o, gu_o, *parts, wd_o, wg, wu, sems = refs[8 + S :]
            _, _, _, z, y = place()
            pairs = []
            for p, piece in enumerate(pieces):
                s = from_shard(p, z, y)
                at = pl.ds(pl.multiple_of(s * n_d, n_d), n_d)
                at_f = pl.ds(pl.multiple_of(s * p_f, p_f), p_f)
                pairs.append((piece.at[pl.ds(f_rows[0], n_d)], wg.at[at]))
                pairs.append((piece.at[pl.ds(f_rows[1], n_d)], wu.at[at]))
                left = wd_o.at[at_f, pl.ds(0, F)]
                pairs.append((piece.at[pl.ds(f_rows[2], p_f)], left))
                for u in range(u_f):
                    block = piece.at[pl.ds(f_rows[3], p_f // u_f), pl.ds(u * w_f, w_f)]
                    n_u = p_f // u_f
                    at_u = pl.ds(pl.multiple_of(s * p_f + u * n_u, n_u), n_u)
                    pairs.append((block, wd_o.at[at_u, pl.ds(F, w_f)]))
            run_copies(pairs, sems)
            for j in range(R):
                n = n_in[j][...]
                gate = dot_nn(n, wg[...])
                up = dot_nn(n, wu[...])
                g_act = dot_nt(cot[j][...], wd_o[...])
                sig = jax.nn.sigmoid(gate)
                silu = gate * sig
                act_o[j] = (silu * up).astype(bf16)
                gg = (g_act * up * sig * (1.0 + gate * (1.0 - sig))).astype(bf16)
                gu = (g_act * silu).astype(bf16)
                gg_o[j], gu_o[j] = gg, gu
                back = dot_nt(gg, wg[...]) + dot_nt(gu, wu[...])
                parts[j][...] = back.astype(bf16)

        hid = sds((R, T, F))
        act, g_gate, g_up, *parts, wd = call(
            ffn_body,
            (hid, hid, hid, flat, flat, flat, flat, sds((F, D))),
            [VMEM] * 8 + [HBM] * S,
            [
                pltpu.VMEM((D, F), bf16),
                pltpu.VMEM((D, F), bf16),
                pltpu.SemaphoreType.DMA(((3 + u_f) * S,)),
            ],
            name="ffn",
        )(*nffn, *cots, *ffns)
        back, chip = scatter_rep(parts)

        def down_body(act, c0, c1, c2, c3, out):
            cot = jnp.concatenate([c0[...], c1[...], c2[...], c3[...]], 0)
            full = dot_tn(act[...].reshape(R * T, F), cot).astype(bf16)
            out[...] = full.reshape(Z, 2 * p_f, D)

        def hidden_body(n0, n1, n2, n3, gg, gu, mine, give, full):
            y = place()[4]
            n_all = jnp.concatenate([n0[...], n1[...], n2[...], n3[...]], 0)
            for i, grad in enumerate((gg, gu)):
                full[...] = dot_tn(n_all, grad[...].reshape(R * T, F)).astype(bf16)
                for k in range(Z):
                    for b, out in enumerate((mine, give)):
                        s = 2 * k + (y if b == 0 else 1 - y)
                        rows = full[pl.ds(pl.multiple_of(s * n_d, n_d), n_d), :]
                        out[k, i * n_d : (i + 1) * n_d] = rows

        piece = sds((Z, 2 * n_d, F))
        (m_h, e_h), t_hid = call(
            hidden_body,
            (piece, piece),
            [VMEM] * 6,
            [pltpu.VMEM((D, F), bf16)],
            name="ghid",
            after=(chip,),
            token=True,
        )(*nffn, g_gate, g_up)
        g_down, t_down = call(
            down_body, sds((Z, 2 * p_f, D)), [VMEM] * 5, name="gdown", token=True
        )(act, *cots)
        moved_d = swap_z(g_down)

        def part_body(act, wd, *parts):
            for j in range(R):
                parts[j][...] = dot_nn(act[j], wd[...]).astype(bf16)

        def back_norm(ins, grad, gain):
            scale = rms_scale(ins)
            u = grad * gain
            return scale * u - ins * scale**3 * jnp.mean(u * ins, axis=-1, keepdims=True)

        def res_body(cot, res, gains, keep, near, far, g_res, g_attn):
            grad = back_norm(res[...], own_sum(keep, near, far), gains[1:2, :])
            grad = cot[...].astype(f32) + grad
            g_res[...] = grad
            g_attn[...] = grad.astype(bf16)

        (grad_res, g_attn), t_res = call(
            res_body,
            (sds((T, D), f32), flat),
            [LOAD, LOAD, VMEM, LOAD, VMEM, VMEM],
            name="gres",
            after=(t_down, t_hid),
            token=True,
        )(cotangent, residual, gains, *back)
        part, t_part = call(
            part_body, (flat,) * R, [VMEM, LOAD], name="part", after=(t_res,), token=True
        )(act, wd)
        out_back, out_chip = scatter_rep(part, after=(t_res,))

        def out_body(res, keep, near, far, out):
            out[...] = (res[...] + own_sum(keep, near, far)).astype(bf16)

        output, t_out = call(
            out_body, flat, [LOAD, LOAD, VMEM, VMEM], name="outsum", token=True
        )(residual, *out_back)

        def attn_back_body(first, g0, g1, q_s, k_s, v_s, wk, wv, wo, gq_o, gk_o, gv_o, gl_o):
            for j, ga in enumerate((g0, g1)):
                gm = dot_nn(ga[...], wo[...]).astype(bf16)
                q, k, v = q_s[first + j], k_s[first + j], v_s[first + j]
                for h in range(0, q_c, 2 * HD):
                    cols = slice(h, h + 2 * HD)
                    qq, kk, vv, gg = q[:, cols], k[:, cols], v[:, cols], gm[:, cols]
                    gqs, gks, gvs = [], [], []
                    for qm, gmm in zip(halves(qq), halves(gg)):
                        probs = softmax_block(qm, kk)
                        gp = dot_nt(gmm, vv)
                        gs = probs * (gp - jnp.sum(probs * gp, axis=-1, keepdims=True))
                        gs = gs.astype(bf16)
                        gqs.append(dot_nn(gs, kk))
                        gks.append(dot_tn(gs, qq))
                        gvs.append(dot_tn(probs.astype(bf16), gg))
                    gq_o[j, :, cols] = (join(*gqs) * HD**-0.5).astype(bf16)
                    gk_o[j, :, cols] = (join(*gks) * HD**-0.5).astype(bf16)
                    gv_o[j, :, cols] = join(*gvs).astype(bf16)
                gl_o[j] = (dot_nt(gk_o[j], wk[...]) + dot_nt(gv_o[j], wv[...])).astype(bf16)

        def attn_back(first, grads, after):
            pair = sds((2, T, q_c))
            return call(
                functools.partial(attn_back_body, first),
                (pair,) * 4,
                [VMEM] * 8,
                name="attnback",
                after=after,
                token=True,
            )(*grads, q_s, k_s, v_s, wk, wv, wo)

        near = (g_attn, flip_core(g_attn))
        near_back, t_near = attn_back(0, near, (t_part, out_chip))
        far = hold(flip_x(g_attn), (t_near,))
        far = (far, flip_core(far))
        far_back, t_far = attn_back(2, far, ())
        g_attns = near + far

        def weights_body(*refs):
            ga, near, far, (mixed, lat_s, normed) = refs[:R], refs[4:8], refs[8:12], refs[12:15]
            mine, give, f_wide, f_low = refs[15:]
            _, _, _, z, y = place()
            gq, gk, gv, gl = (
                jnp.concatenate([a[...], b[...]], 0).reshape(R * T, q_c) for a, b in zip(near, far)
            )
            n_all = normed[...].reshape(R * T, D)
            lat = lat_s[...].reshape(R * T, LAT)
            g_all = jnp.concatenate([g[...] for g in ga], 0)
            f_wide[0] = dot_tn(n_all, gq).astype(bf16)
            f_wide[1] = dot_tn(n_all, gl).astype(bf16)
            f_wide[2] = dot_tn(g_all, mixed[...].reshape(R * T, q_c)).astype(bf16)
            f_low[0] = dot_tn(lat, gk).astype(bf16)
            f_low[1] = dot_tn(lat, gv).astype(bf16)
            for k in range(Z):
                for b, out in enumerate((mine, give)):
                    s = to_shard(k, b, z, y)
                    at_d = pl.ds(pl.multiple_of(s * n_d, n_d), n_d)
                    at_l = pl.ds(pl.multiple_of(s * n_l, n_l), n_l)
                    out[k, cuts[0] : cuts[1]] = f_wide[0, at_d, :]
                    out[k, cuts[1] : cuts[2]] = f_wide[1, at_d, :]
                    out[k, cuts[2] : cuts[3]] = f_low[0, at_l, :]
                    out[k, cuts[3] : cuts[4]] = f_low[1, at_l, :]
                    out[k, cuts[4] : cuts[5]] = f_wide[2, at_d, :]

        got_h = flip_y(e_h)
        half_h, t_half = half_sum(m_h, got_h, "hid", False, after=(t_far,))
        piece = sds((Z, cuts[5], q_c))
        (m_p, e_p), t_back = call(
            weights_body,
            (piece, piece),
            [VMEM] * 15,
            [pltpu.VMEM((3, D, q_c), bf16), pltpu.VMEM((2, LAT, q_c), bf16)],
            name="wback",
            after=(t_half,),
            token=True,
        )(*g_attns, *near_back, *far_back, mixed, lat_s, normed)

        def down_sum_body(parts, mine, give):
            y = place()[4]
            total = parts[0].astype(f32)
            for k in range(1, Z):
                total = total + parts[k].astype(f32)
            low, high = total[:p_f], total[p_f:]
            mine[...] = jnp.where(y == 0, low, high).astype(bf16)
            give[...] = jnp.where(y == 0, high, low).astype(bf16)

        slab = sds((p_f, D))
        (mine_d, give_d), t_dsum = call(
            down_sum_body, (slab, slab), [VMEM], name="dsum", after=(t_half,), token=True
        )(moved_d)
        own_d = (mine_d.astype(f32) + flip_y(give_d).astype(f32)).astype(bf16)
        sum_dn = gather_rep(own_d)

        def in_body(gq0, gl0, gq1, gl1, wq, wl, *parts):
            for j, (gq, gl) in enumerate(((gq0, gl0), (gq1, gl1))):
                for i in range(2):
                    back = dot_nt(gq[i], wq[...]) + dot_nt(gl[i], wl[...])
                    parts[2 * j + i][...] = back.astype(bf16)

        got_p = flip_y(e_p)
        ins_part, t_in = call(
            in_body, (flat,) * R, [VMEM] * 4 + [LOAD] * 2, name="inback", after=(t_back,), token=True
        )(near_back[0], near_back[3], far_back[0], far_back[3], wq, wl)
        half_p, t_pack = half_sum(m_p, got_p, "pack", True, after=(t_half, t_in, t_out, t_dsum))
        ins_back = scatter_rep(ins_part, after=(t_pack,))[0]

        def tok_body(tok, g_res, gains, keep, near, far, out):
            grad = back_norm(tok[...].astype(f32), own_sum(keep, near, far), gains[0:1, :])
            out[...] = (g_res[...] + grad).astype(bf16)

        grad_tokens, t_tok = call(
            tok_body, flat, [LOAD, LOAD, VMEM, LOAD, VMEM, VMEM], name="gtok", token=True
        )(
            tokens, grad_res, gains, *ins_back
        )

        own_h, t_sum = part_sum([swap_z(half_h)], "hid", after=(t_pack, t_tok))
        own_p, _ = part_sum(turn_z(half_p), "pack", after=(t_sum,))
        sum_h = gather_rep(own_h)
        sum_p = gather_rep(own_p)

        def lane_sum(v):
            total = v[:, :128]
            for j in range(128, v.shape[1], 128):
                total = total + v[:, j : j + 128]
            return jnp.sum(total.T, axis=0, keepdims=True)

        def final_hidden_body(*refs):
            d_in, (v0, v1, v2, v3, w_g, w_u, nf, out_d, out_g, out_u, dots) = refs[:R], refs[R:]
            r, x, c, _, _ = place()
            for k, d in enumerate(d_in):
                q = lax.bitwise_xor(r, k)
                out_d[pl.ds(pl.multiple_of(q * n_f, 8), n_f), :] = d[...].astype(f32)[:n_f]
            total = 0.0
            for i, (w, out) in enumerate(((w_g, out_g), (w_u, out_u))):
                vs = [v[i * n_d : (i + 1) * n_d].astype(f32) for v in (v0, v1, v2, v3)]
                vs = [jnp.where(c == 1, vs[k ^ 1], vs[k]) for k in range(R)]
                vs = [jnp.where(x == 1, vs[k ^ 2], vs[k]) for k in range(R)]
                for q in range(R):
                    for s in range(S):
                        at = s * R * n_f + q * n_f
                        out[:, at : at + n_f] = vs[q][:, s * p_f : s * p_f + n_f]
                total = total + lane_sum(out[...] * w[...].astype(f32))
            dots[...] = total / nf[...].astype(f32)

        row = sds((1, n_d), f32)
        wide = sds((n_d, FF), f32)
        (g_down, g_gate_w, g_up_w, g_nf), t_hid = call(
            final_hidden_body,
            (sds((R * n_f, D), f32), wide, wide, row),
            [VMEM] * (2 * R) + [LOAD] * 2 + [VMEM],
            name="fhid",
            token=True,
        )(*sum_dn, *sum_h, w_gate, w_up, norm_ffn.reshape(1, n_d))

        def final_pack_body(v0, v1, v2, v3, w_q, w_l, na, gq, gl, gk, gv, go, gna):
            r, x, _, _, _ = place()
            vs = (v0, v1, v2, v3)
            for k, v in enumerate(vs):
                q = lax.bitwise_xor(r, k)
                wide = pl.ds(pl.multiple_of(q * q_c, q_c), q_c)
                part = pl.ds(pl.multiple_of((q % 2) * q_c, q_c), q_c)
                gq[:, wide] = v[cuts[0] : cuts[1]].astype(f32)
                gk[q // 2, :, part] = v[cuts[2] : cuts[3]].astype(f32)
                gv[q // 2, :, part] = v[cuts[3] : cuts[4]].astype(f32)
                go[wide, :] = v[cuts[4] : cuts[5]].astype(f32).T
            for k in (0, 2):
                g = lax.bitwise_xor(x, k // 2)
                both = vs[k][cuts[1] : cuts[2]].astype(f32) + vs[k + 1][cuts[1] : cuts[2]].astype(f32)
                gl[:, pl.ds(pl.multiple_of(g * LAT, LAT), LAT)] = both
            dots = lane_sum(gq[...] * w_q[...].astype(f32)) + lane_sum(gl[...] * w_l[...].astype(f32))
            gna[...] = dots / na[...].astype(f32)

        g_query, g_latent, g_key, g_value, g_out, g_na = call(
            final_pack_body,
            (
                sds((n_d, R * q_c), f32),
                sds((n_d, LG * LAT), f32),
                sds((LG, n_l, 2 * q_c), f32),
                sds((LG, n_l, 2 * q_c), f32),
                sds((R * q_c, n_d), f32),
                row,
            ),
            [VMEM] * R + [LOAD] * 2 + [VMEM],
            name="fpack",
            after=(t_hid, t_out, t_tok),
        )(*sum_p, w_query, w_latent, norm_attn.reshape(1, n_d))
        return (
            output,
            grad_tokens,
            g_na.reshape(n_d),
            g_query,
            g_latent,
            g_key,
            g_value,
            g_out,
            g_nf.reshape(n_d),
            g_gate_w,
            g_up_w,
            g_down,
        )

    return layer


def make_layer(mesh):
    aligned = (LAT // mesh.shape["shard"]) % 16 == 0
    return make_fast(mesh) if aligned else make_plain(mesh)


def solution(mesh):
    return jax.shard_map(
        make_layer(mesh),
        mesh=mesh,
        in_specs=(
            P(("rep", "shard"), None),
            P("shard"),
            P("shard", None),
            P("shard", None),
            P(None, "shard", None),
            P(None, "shard", None),
            P(None, "shard"),
            P("shard"),
            P("shard", None),
            P("shard", None),
            P("shard", None),
            P(("rep", "shard"), None),
        ),
        out_specs=(
            P(("rep", "shard"), None),
            P(("rep", "shard"), None),
            P("shard"),
            P("shard", None),
            P("shard", None),
            P(None, "shard", None),
            P(None, "shard", None),
            P(None, "shard"),
            P("shard"),
            P("shard", None),
            P("shard", None),
            P("shard", None),
        ),
        check_vma=False,
    )
```

```python
import functools

import jax
import jax.numpy as jnp
from jax import lax
from jax.experimental import pallas as pl
from jax.experimental.pallas import tpu as pltpu
from jax.sharding import PartitionSpec as P

HQ = 16
HD = 64
LG = 2
LAT = 256
SEQ = 256
R = 4
f32 = jnp.float32
bf16 = jnp.bfloat16
epsilon = 1e-05


def rms_scale(rows_in):
    return lax.rsqrt(jnp.mean(rows_in * rows_in, axis=-1, keepdims=True) + epsilon)


def dot_nn(a, b):
    return lax.dot_general(a, b, (((1,), (0,)), ((), ())), preferred_element_type=f32)


def dot_nt(a, b):
    return lax.dot_general(a, b, (((1,), (1,)), ((), ())), preferred_element_type=f32)


def dot_tn(a, b):
    return lax.dot_general(a, b, (((0,), (0,)), ((), ())), preferred_element_type=f32)


def make_plain(mesh):
    S = mesh.shape["shard"]
    Z = S // 2
    assert mesh.shape["rep"] == R

    def flip_core(v):
        return lax.ppermute(v, "rep", [(i, i ^ 1) for i in range(R)])

    def flip_x(v):
        return lax.ppermute(v, "rep", [(i, i ^ 2) for i in range(R)])

    def flip_y(v):
        return lax.ppermute(v, "shard", [(i, i ^ 1) for i in range(S)])

    def rot_z(v, k):
        return lax.ppermute(v, "shard", [(i, (i + 2 * k) % S) for i in range(S)])

    def layer(
        tokens,
        norm_attn,
        w_query,
        w_latent,
        w_key_up,
        w_value_up,
        w_out,
        norm_ffn,
        w_gate,
        w_up,
        w_down,
        cotangent,
    ):
        r = lax.axis_index("rep")
        s = lax.axis_index("shard")
        x, c, z, y = r // 2, r % 2, s // 2, s % 2
        T, D = tokens.shape
        n_d = w_query.shape[0]
        n_l = w_key_up.shape[1]
        n_f = w_down.shape[0] // R
        q_c = w_query.shape[1] // R
        FFq = n_f * S

        def gather_rep(v):
            far = flip_x(v)
            near = flip_core(jnp.stack([v, far]))
            return jnp.stack([v, near[0], far, near[1]])

        def scatter_rep(v):
            near = flip_core(v[1::2].astype(bf16))
            chip = v[0::2] + near
            far = flip_x(chip[1].astype(bf16))
            return chip[0] + far

        def absolute(v):
            v = jnp.where(c == 1, v[jnp.array([1, 0, 3, 2])], v)
            return jnp.where(x == 1, v[jnp.array([2, 3, 0, 1])], v)

        def gather_shard(v):
            full = jnp.zeros((Z, 2) + v.shape, v.dtype)
            zeros = (0,) * v.ndim
            for k in range(Z):
                piece = v if k == 0 else rot_z(v, k)
                other = flip_y(piece)
                at = lax.rem(z - k + Z, Z)
                full = lax.dynamic_update_slice(full, piece[None, None], (at, y) + zeros)
                full = lax.dynamic_update_slice(full, other[None, None], (at, 1 - y) + zeros)
            return full.reshape((S,) + v.shape)

        def scatter_shard(v):
            v = v.reshape((Z, 2) + v.shape[1:])
            mine = lax.dynamic_index_in_dim(v, y, 1, False)
            give = lax.dynamic_index_in_dim(v, 1 - y, 1, False)
            half = (mine.astype(f32) + flip_y(give).astype(f32)).astype(bf16)
            total = lax.dynamic_index_in_dim(half, z, 0, False).astype(f32)
            for k in range(1, Z):
                piece = lax.dynamic_index_in_dim(half, lax.rem(z + k, Z), 0, False)
                total = total + rot_z(piece, k).astype(f32)
            return absolute(gather_rep(total.astype(bf16)))

        my_query = lax.dynamic_slice_in_dim(w_query, r * q_c, q_c, 1)
        my_latent = lax.dynamic_slice_in_dim(w_latent, x * LAT, LAT, 1)
        my_key = lax.dynamic_slice_in_dim(
            lax.dynamic_index_in_dim(w_key_up, x, 0, False), c * q_c, q_c, 1
        )
        my_value = lax.dynamic_slice_in_dim(
            lax.dynamic_index_in_dim(w_value_up, x, 0, False), c * q_c, q_c, 1
        )
        my_out = lax.dynamic_slice_in_dim(w_out, r * q_c, q_c, 0).T
        gains = jnp.zeros((16, q_c), bf16)
        gains = gains.at[0, :n_d].set(norm_attn).at[1, :n_d].set(norm_ffn)
        pack = jnp.concatenate([my_query, my_latent, my_key, my_value, my_out, gains], 0)
        cuts = [n_d, 2 * n_d, 2 * n_d + n_l, 2 * n_d + 2 * n_l, 3 * n_d + 2 * n_l]

        col = lax.broadcasted_iota(jnp.int32, (S * R * n_f, FFq), 1)
        row = lax.broadcasted_iota(jnp.int32, (S * R * n_f, FFq), 0)
        pick = (row == (col // n_f) * (R * n_f) + r * n_f + col % n_f).astype(bf16)
        my_gate_up = dot_nn(jnp.concatenate([w_gate, w_up], 0), pick).astype(bf16)
        my_down = lax.dynamic_slice_in_dim(w_down, r * n_f, n_f, 0)

        all_tokens = gather_rep(tokens).reshape(R * T, D)
        packs = gather_shard(pack)
        all_cot = gather_rep(cotangent).reshape(R * T, D)
        gate_up = gather_shard(my_gate_up)
        down = gather_shard(my_down).reshape(FFq, D)

        query_w = packs[:, : cuts[0]].reshape(D, q_c)
        latent_w = packs[:, cuts[0] : cuts[1]].reshape(D, LAT)
        key_w = packs[:, cuts[1] : cuts[2]].reshape(LAT, q_c)
        value_w = packs[:, cuts[2] : cuts[3]].reshape(LAT, q_c)
        out_w = packs[:, cuts[3] : cuts[4]].reshape(D, q_c)
        gain_attn = packs[:, cuts[4], :n_d].reshape(D).astype(f32)
        gain_ffn = packs[:, cuts[4] + 1, :n_d].reshape(D).astype(f32)
        gate_w = gate_up[:, :n_d].reshape(D, FFq)
        up_w = gate_up[:, n_d:].reshape(D, FFq)

        heads = q_c // HD
        group_in = all_tokens.astype(f32)
        scale_attn = rms_scale(group_in)
        normed_attn = (group_in * scale_attn * gain_attn).astype(bf16)
        queries = dot_nn(normed_attn, query_w).astype(bf16)
        latents = dot_nn(normed_attn, latent_w).astype(bf16)
        keys = dot_nn(latents, key_w).astype(bf16)
        values = dot_nn(latents, value_w).astype(bf16)
        qh = queries.reshape(R, T, heads, HD)
        kh = keys.reshape(R, T, heads, HD)
        vh = values.reshape(R, T, heads, HD)
        row_ids = lax.broadcasted_iota(jnp.int32, (SEQ, SEQ), 0)
        col_ids = lax.broadcasted_iota(jnp.int32, (SEQ, SEQ), 1)
        scores = jnp.einsum("bqhd,bkhd->bhqk", qh, kh, preferred_element_type=f32) * HD**-0.5
        scores = jnp.where(col_ids <= row_ids, scores, -1e30)
        maxima = jnp.max(scores, axis=-1, keepdims=True)
        exps = jnp.exp(scores - maxima)
        probs = exps / jnp.sum(exps, axis=-1, keepdims=True)
        low_probs = probs.astype(bf16)
        mixed = jnp.einsum("bhqk,bkhd->bqhd", low_probs, vh, preferred_element_type=f32)
        mixed = mixed.astype(bf16).reshape(R * T, q_c)
        attn_part = dot_nt(mixed, out_w).reshape(R, T, D)
        inputs = tokens.astype(f32)
        residual = inputs + scatter_rep(attn_part)
        scale_ffn = rms_scale(residual)
        normed_own = (residual * scale_ffn * gain_ffn).astype(bf16)
        normed_ffn = gather_rep(normed_own).reshape(R * T, D)

        gate_proj = dot_nn(normed_ffn, gate_w)
        up_proj = dot_nn(normed_ffn, up_w)
        sig = jax.nn.sigmoid(gate_proj)
        silu = gate_proj * sig
        activated = (silu * up_proj).astype(bf16)
        grad_down = dot_tn(activated, all_cot).astype(bf16).reshape(S, n_f, D)
        grad_act = dot_nt(all_cot, down)
        grad_gate = (grad_act * up_proj * sig * (1.0 + gate_proj * (1.0 - sig))).astype(bf16)
        grad_up = (grad_act * silu).astype(bf16)
        grad_gate_w = dot_tn(normed_ffn, grad_gate).astype(bf16).reshape(S, n_d, FFq)
        grad_up_w = dot_tn(normed_ffn, grad_up).astype(bf16).reshape(S, n_d, FFq)
        ffn_back = dot_nt(grad_gate, gate_w) + dot_nt(grad_up, up_w)
        grad_normed_ffn = scatter_rep(ffn_back.reshape(R, T, D))
        ffn_part = dot_nn(activated, down).reshape(R, T, D)
        output = (residual + scatter_rep(ffn_part)).astype(bf16)

        weighted = grad_normed_ffn * gain_ffn
        grad_residual = (
            cotangent.astype(f32)
            + scale_ffn * weighted
            - residual * scale_ffn**3 * jnp.mean(weighted * residual, axis=-1, keepdims=True)
        )
        grad_attn = gather_rep(grad_residual.astype(bf16)).reshape(R * T, D)

        grad_out_w = dot_tn(grad_attn, mixed).astype(bf16)
        grad_mixed = dot_nn(grad_attn, out_w).astype(bf16).reshape(R, T, heads, HD)
        grad_probs = jnp.einsum("bqhd,bkhd->bhqk", grad_mixed, vh, preferred_element_type=f32)
        grad_scores = (
            probs * (grad_probs - jnp.sum(probs * grad_probs, axis=-1, keepdims=True))
        ).astype(bf16)
        grad_q = jnp.einsum("bhqk,bkhd->bqhd", grad_scores, kh, preferred_element_type=f32)
        grad_k = jnp.einsum("bhqk,bqhd->bkhd", grad_scores, qh, preferred_element_type=f32)
        grad_v = jnp.einsum("bhqk,bqhd->bkhd", low_probs, grad_mixed, preferred_element_type=f32)
        grad_q = (grad_q * HD**-0.5).astype(bf16).reshape(R * T, q_c)
        grad_k = (grad_k * HD**-0.5).astype(bf16).reshape(R * T, q_c)
        grad_v = grad_v.astype(bf16).reshape(R * T, q_c)
        grad_key_w = dot_tn(latents, grad_k).astype(bf16)
        grad_value_w = dot_tn(latents, grad_v).astype(bf16)
        grad_query_w = dot_tn(normed_attn, grad_q).astype(bf16)
        lat_part = (dot_nt(grad_k, key_w) + dot_nt(grad_v, value_w)).reshape(R, T, LAT)
        near = flip_core(lat_part[1::2])
        grad_lat = (lat_part[0::2] + near).astype(bf16).reshape(2 * T, LAT)
        half_normed = normed_attn.reshape(R, T, D)[0::2].reshape(2 * T, D)
        grad_latent_w = dot_tn(half_normed, grad_lat).astype(bf16)
        attn_back = dot_nt(grad_q, query_w).reshape(R, T, D)
        lat_back = dot_nt(grad_lat, latent_w).reshape(2, T, D)
        attn_back = jnp.stack(
            [attn_back[0] + lat_back[0], attn_back[1], attn_back[2] + lat_back[1], attn_back[3]]
        )
        grad_normed_attn = scatter_rep(attn_back)
        weighted = grad_normed_attn * gain_attn
        scale_own = rms_scale(inputs)
        grad_tokens = (
            grad_residual
            + scale_own * weighted
            - inputs * scale_own**3 * jnp.mean(weighted * inputs, axis=-1, keepdims=True)
        ).astype(bf16)

        sum_down = scatter_shard(grad_down)
        sum_gate = scatter_shard(grad_gate_w)
        sum_up = scatter_shard(grad_up_w)
        grad_pack = jnp.concatenate(
            [
                grad_query_w.reshape(S, n_d, q_c),
                grad_latent_w.reshape(S, n_d, LAT),
                grad_key_w.reshape(S, n_l, q_c),
                grad_value_w.reshape(S, n_l, q_c),
                grad_out_w.reshape(S, n_d, q_c),
            ],
            1,
        )
        sum_pack = scatter_shard(grad_pack).astype(f32)
        g_query = sum_pack[:, : cuts[0]].transpose(1, 0, 2).reshape(n_d, R * q_c)
        g_latent = sum_pack[:, cuts[0] : cuts[1]]
        g_latent = jnp.concatenate([g_latent[0] + g_latent[1], g_latent[2] + g_latent[3]], 1)
        g_key = sum_pack[:, cuts[1] : cuts[2]].reshape(LG, 2, n_l, q_c)
        g_key = g_key.transpose(0, 2, 1, 3).reshape(LG, n_l, 2 * q_c)
        g_value = sum_pack[:, cuts[2] : cuts[3]].reshape(LG, 2, n_l, q_c)
        g_value = g_value.transpose(0, 2, 1, 3).reshape(LG, n_l, 2 * q_c)
        g_out = sum_pack[:, cuts[3] : cuts[4]].transpose(0, 2, 1).reshape(R * q_c, n_d)
        g_down = sum_down.reshape(R * n_f, D).astype(f32)

        def spread(v):
            v = v.reshape(R, n_d, S, n_f).transpose(1, 2, 0, 3)
            return v.reshape(n_d, S * R * n_f).astype(f32)

        g_gate = spread(sum_gate)
        g_up = spread(sum_up)
        g_norm_attn = (
            jnp.sum(g_query * w_query.astype(f32), axis=1)
            + jnp.sum(g_latent * w_latent.astype(f32), axis=1)
        ) / norm_attn.astype(f32)
        g_norm_ffn = (
            jnp.sum(g_gate * w_gate.astype(f32), axis=1) + jnp.sum(g_up * w_up.astype(f32), axis=1)
        ) / norm_ffn.astype(f32)
        return (
            output,
            grad_tokens,
            g_norm_attn,
            g_query,
            g_latent,
            g_key,
            g_value,
            g_out,
            g_norm_ffn,
            g_gate,
            g_up,
            g_down,
        )

    return layer


HBM = pl.BlockSpec(memory_space=pl.ANY)
VMEM = pl.BlockSpec(memory_space=pltpu.VMEM)
LOAD = pl.BlockSpec(memory_space=pltpu.HBM)
KEEP = pl.BlockSpec(memory_space=pltpu.HBM)


def sds(shape, dtype=bf16):
    return jax.ShapeDtypeStruct(shape, dtype)


def call(body, outs, in_specs, scratch=(), name=None, after=(), token=False):
    n, flat = len(in_specs), isinstance(outs, tuple)
    loads = [i for i, spec in enumerate(in_specs) if spec is LOAD]

    def run(*refs):
        ins, rest = list(refs[:n]), list(refs[n + len(after) :])
        if token:
            mark = rest.pop(len(outs) if flat else 1)
            mark[...] = jnp.zeros_like(mark)
        if loads:
            sems, buffers = rest[-1], rest[-1 - len(loads) : -1]
            rest = rest[: -1 - len(loads)]
            run_copies([(ins[i], buffer) for i, buffer in zip(loads, buffers)], sems)
            for i, buffer in zip(loads, buffers):
                ins[i] = buffer
        body(*ins, *rest)

    def bind(*args):
        shapes = outs if flat else (outs,)
        if token:
            shapes = shapes + (sds((8, 128), f32),)
        extra = [pltpu.VMEM(args[i].shape, args[i].dtype) for i in loads]
        if loads:
            extra.append(pltpu.SemaphoreType.DMA((len(loads),)))
        result = pl.pallas_call(
            run,
            out_shape=shapes,
            in_specs=list(in_specs) + [HBM] * len(after),
            out_specs=tuple(VMEM for _ in shapes),
            scratch_shapes=list(scratch) + extra,
            compiler_params=pltpu.CompilerParams(
                vmem_limit_bytes=LIMITS.get(name, 24 if name in WIDE else 8) * 1024 * 1024
            ),
            cost_estimate=pl.CostEstimate(
                flops=0, bytes_accessed=COSTS.get(name, 2500) * 3000, transcendentals=0
            ),
            name=name,
        )(*args, *after)
        if token:
            main = result[:-1] if flat else result[0]
            return main, result[-1]
        return result if flat else result[0]

    return bind


WIDE = ("attn", "ffn", "attnback", "wback", "ghid", "gdown", "part", "inback", "fhid")
LIMITS = {"pack": 60, "wback": 54, "attnback": 54}
COSTS = {
    "pack": 2000,
    "prep": 4500,
    "attn": 11300,
    "norm": 3300,
    "ffn": 15300,
    "ghid": 8500,
    "gdown": 5000,
    "part": 500,
    "gres": 3900,
    "attnback": 1000,
    "wback": 4000,
    "chip": 300,
    "inback": 4000,
}


def hold(v, after):
    def body(*refs):
        pass

    return pl.pallas_call(
        body,
        out_shape=sds(v.shape, v.dtype),
        in_specs=[HBM] * (1 + len(after)),
        out_specs=HBM,
        input_output_aliases={0: 0},
        name="hold",
    )(v, *after)


def run_copies(pairs, sems):
    copies = [pltpu.make_async_copy(a, b, sems.at[i]) for i, (a, b) in enumerate(pairs)]
    for copy in copies:
        copy.start()
    for copy in copies:
        copy.wait()


def halves(v):
    low = lax.broadcasted_iota(jnp.int32, v.shape, 1) < HD
    zero = jnp.zeros_like(v)
    return jnp.where(low, v, zero), jnp.where(low, zero, v)


def join(a, b):
    return jnp.where(lax.broadcasted_iota(jnp.int32, a.shape, 1) < HD, a, b)


def softmax_block(qm, k):
    scores = dot_nt(qm, k) * HD**-0.5
    row_ids = lax.broadcasted_iota(jnp.int32, scores.shape, 0)
    col_ids = lax.broadcasted_iota(jnp.int32, scores.shape, 1)
    scores = jnp.where(col_ids <= row_ids, scores, -1e30)
    exps = jnp.exp(scores - jnp.max(scores, axis=-1, keepdims=True))
    return exps * (1.0 / jnp.sum(exps, axis=-1, keepdims=True))


def make_fast(mesh):
    S = mesh.shape["shard"]
    Z = S // 2

    def flip_core(v):
        return lax.ppermute(v, "rep", [(i, i ^ 1) for i in range(R)])

    def flip_x(v):
        return lax.ppermute(v, "rep", [(i, i ^ 2) for i in range(R)])

    def flip_y(v):
        return lax.ppermute(v, "shard", [(i, i ^ 1) for i in range(S)])

    def rot_z(v, k):
        return lax.ppermute(v, "shard", [(i, (i + 2 * k) % S) for i in range(S)])

    def place():
        r = lax.axis_index("rep")
        s = lax.axis_index("shard")
        return r, r // 2, r % 2, s // 2, s % 2

    def gather_rep(v):
        far = flip_x(v)
        return v, flip_core(v), far, flip_core(far)

    def gather_shard(v):
        out = []
        for k in range(Z):
            piece = v if k == 0 else rot_z(v, k)
            out += [piece, flip_y(piece)]
        return out

    def from_shard(p, z, y):
        return 2 * lax.rem(z - p // 2 + Z, Z) + (y if p % 2 == 0 else 1 - y)

    def ring_shard(v):
        out = []
        for k in range(Z):
            piece = v if k == 0 else rot_z(piece, 1)
            out += [piece, flip_y(piece)]
        return out

    def to_shard(k, b, z, y):
        return 2 * lax.rem(z + k, Z) + (y if b == 0 else 1 - y)

    def swap_z(v):
        groups = [[2 * i + j for i in range(Z)] for j in range(2)]
        return lax.all_to_all(v, "shard", 0, 0, axis_index_groups=groups, tiled=True)

    def add_body(mine, got, *outs):
        for k in range(Z):
            total = (mine[k].astype(f32) + got[k].astype(f32)).astype(bf16)
            if len(outs) == 1:
                outs[0][k] = total
            else:
                outs[k][...] = total

    def sum_body(*refs):
        parts = [refs[0][k] for k in range(Z)] if len(refs) == 2 else [r[...] for r in refs[:-1]]
        total = parts[0].astype(f32)
        for part in parts[1:]:
            total = total + part.astype(f32)
        refs[-1][...] = total.astype(bf16)

    def half_sum(mine, got, name, split, after=()):
        shape = sds(mine.shape[1:])
        outs = (shape,) * Z if split else sds(mine.shape)
        add = call(add_body, outs, [LOAD, VMEM], name=name + "_add", after=after, token=True)
        return add(mine, got)

    def turn_z(parts):
        return [parts[0]] + [rot_z(parts[k], k) for k in range(1, Z)]

    def part_sum(parts, name, after=()):
        shape = parts[0].shape if len(parts) > 1 else parts[0].shape[1:]
        specs = [VMEM] * len(parts)
        return call(sum_body, sds(shape), specs, name=name + "_sum", after=after, token=True)(*parts)

    def layer(
        tokens,
        norm_attn,
        w_query,
        w_latent,
        w_key_up,
        w_value_up,
        w_out,
        norm_ffn,
        w_gate,
        w_up,
        w_down,
        cotangent,
    ):
        T, D = tokens.shape
        n_d = w_query.shape[0]
        n_l = w_key_up.shape[1]
        n_f = w_down.shape[0] // R
        p_f = -(-n_f // 16) * 16
        F = S * p_f
        q_c = w_query.shape[1] // R
        FF = S * R * n_f
        cuts = [0]
        for rows in (n_d, n_d, n_l, n_l, n_d, 16):
            cuts.append(cuts[-1] + rows)

        def pack_body(wq, wl, wk, wv, wo, na, nf, out, wo_in, sems):
            r, x, c, _, _ = place()
            wide = pl.ds(pl.multiple_of(r * q_c, q_c), q_c)
            group = pl.ds(pl.multiple_of(x * LAT, LAT), LAT)
            part = pl.ds(pl.multiple_of(c * q_c, q_c), q_c)
            pairs = [
                (wq.at[:, wide], out.at[cuts[0] : cuts[1]]),
                (wl.at[:, group], out.at[cuts[1] : cuts[2]]),
                (wk.at[x, :, part], out.at[cuts[2] : cuts[3]]),
                (wv.at[x, :, part], out.at[cuts[3] : cuts[4]]),
                (wo.at[wide, :], wo_in),
            ]
            run_copies(pairs, sems)
            out[cuts[4] : cuts[5]] = wo_in[...].astype(f32).T.astype(bf16)
            gains = jnp.concatenate([na[...], nf[...]], 1)
            out[cuts[5] : cuts[6]] = jnp.broadcast_to(gains, (16, 2 * n_d))

        pack = call(
            pack_body,
            sds((cuts[6], q_c)),
            [KEEP] * 5 + [VMEM] * 2,
            [pltpu.VMEM((q_c, n_d), bf16), pltpu.SemaphoreType.DMA((5,))],
            name="pack",
        )(
            w_query,
            w_latent,
            w_key_up,
            w_value_up,
            w_out,
            norm_attn.reshape(1, n_d),
            norm_ffn.reshape(1, n_d),
        )

        w_f = D - F
        u_f = F // w_f
        f_rows = [0, n_d, 2 * n_d, 2 * n_d + p_f, 2 * n_d + p_f + p_f // u_f]

        def prep_body(wg, wu, wd, out):
            r = place()[0]
            for j0 in range(0, F, 128):
                s_lo, s_hi = j0 // p_f, (j0 + 127) // p_f
                a = s_lo * R * n_f // 128 * 128
                b = min(-(-(s_hi + 1) * R * n_f // 128) * 128, FF)
                col = j0 + lax.broadcasted_iota(jnp.int32, (b - a, 128), 1)
                row = a + lax.broadcasted_iota(jnp.int32, (b - a, 128), 0)
                pick = jnp.zeros((b - a, 128), jnp.bool_)
                for s in range(s_lo, s_hi + 1):
                    i = col - s * p_f
                    hit = (i >= 0) & (i < n_f) & (row == s * R * n_f + r * n_f + i)
                    pick = pick | hit
                pick = pick.astype(f32).astype(bf16)
                cols = slice(j0, j0 + 128)
                out[f_rows[0] : f_rows[1], cols] = dot_nn(wg[:, a:b], pick).astype(bf16)
                out[f_rows[1] : f_rows[2], cols] = dot_nn(wu[:, a:b], pick).astype(bf16)
            i = lax.broadcasted_iota(jnp.int32, (p_f, R * n_f), 0)
            m = lax.broadcasted_iota(jnp.int32, (p_f, R * n_f), 1)
            pick = ((i < n_f) & (m == r * n_f + i)).astype(f32).astype(bf16)
            down = dot_nn(pick, wd[...])
            out[f_rows[2] : f_rows[3]] = down[:, :F].astype(bf16)
            for u in range(u_f):
                block = down[u * p_f // u_f : (u + 1) * p_f // u_f, F:]
                out[f_rows[3] : f_rows[4], u * w_f : (u + 1) * w_f] = block.astype(bf16)


        toks = gather_rep(tokens)
        packs = gather_shard(pack)
        my_ffn = call(
            prep_body, sds((f_rows[4], F)), [LOAD] * 3, name="prep", after=(pack,)
        )(w_gate, w_up, w_down)
        ffns = ring_shard(my_ffn)
        cots = gather_rep(cotangent)

        def attn_body(*refs):
            tok, pieces = refs[:R], refs[R : R + S]
            normed, q_o, k_o, v_o, lat_o, mixed = refs[R + S : R + S + 6]
            parts, (wq, wl, wk, wv, wo, gains) = refs[R + S + 6 : R + S + 10], refs[R + S + 10 : R + S + 16]
            rows, sems = refs[R + S + 16 :]
            _, _, _, z, y = place()
            pairs = []
            for p, piece in enumerate(pieces):
                s = from_shard(p, z, y)
                at_d = pl.ds(pl.multiple_of(s * n_d, n_d), n_d)
                at_l = pl.ds(pl.multiple_of(s * n_l, n_l), n_l)
                spots = (wq.at[at_d], wl.at[at_d], wk.at[at_l], wv.at[at_l], wo.at[at_d], rows.at[s])
                for i, spot in enumerate(spots):
                    pairs.append((piece.at[pl.ds(cuts[i], cuts[i + 1] - cuts[i])], spot))
            run_copies(pairs, sems)
            for s in range(S):
                both = rows[s].astype(f32)[0:1]
                gains[0:1, s * n_d : (s + 1) * n_d] = both[:, :n_d]
                gains[1:2, s * n_d : (s + 1) * n_d] = both[:, n_d : 2 * n_d]
            for j in range(R):
                ins = tok[j][...].astype(f32)
                nrm = (ins * rms_scale(ins) * gains[0:1, :]).astype(bf16)
                normed[j] = nrm
                q = dot_nn(nrm, wq[...]).astype(bf16)
                lat = dot_nn(nrm, wl[...]).astype(bf16)
                k = dot_nn(lat, wk[...]).astype(bf16)
                v = dot_nn(lat, wv[...]).astype(bf16)
                q_o[j], lat_o[j], k_o[j], v_o[j] = q, lat, k, v
                for h in range(0, q_c, 2 * HD):
                    kk, vv = k[:, h : h + 2 * HD], v[:, h : h + 2 * HD]
                    both = []
                    for qm in halves(q[:, h : h + 2 * HD]):
                        both.append(dot_nn(softmax_block(qm, kk).astype(bf16), vv))
                    mixed[j, :, h : h + 2 * HD] = join(*both).astype(bf16)
                parts[j][...] = dot_nt(mixed[j], wo[...]).astype(bf16)

        small = sds((R, T, q_c))
        flat = sds((T, D))
        (normed, q_s, k_s, v_s, lat_s, mixed, *parts, wq, wl, wk, wv, wo, gains) = call(
            attn_body,
            (
                sds((R, T, D)),
                small,
                small,
                small,
                small,
                small,
                flat,
                flat,
                flat,
                flat,
                sds((D, q_c)),
                sds((D, LAT)),
                sds((LAT, q_c)),
                sds((LAT, q_c)),
                sds((D, q_c)),
                sds((8, D), f32),
            ),
            [VMEM] * R + [HBM] * S,
            [pltpu.VMEM((S, 16, q_c), bf16), pltpu.SemaphoreType.DMA((6 * S,))],
            name="attn",
            after=(cots[2], ffns[1]),
        )(*toks, *packs)

        def chip_body(keep, near, out):
            out[...] = (keep[...].astype(f32) + near[...].astype(f32)).astype(bf16)

        def scatter_rep(parts, after=()):
            near_far = flip_core(parts[3])
            near = flip_core(parts[1])
            if after:
                chip = call(chip_body, flat, [VMEM] * 2, name="chip", after=after)(parts[2], near_far)
            else:
                chip = (parts[2].astype(f32) + near_far.astype(f32)).astype(bf16)
            return (parts[0], near, flip_x(chip)), chip

        def own_sum(keep, near, far):
            return keep[...].astype(f32) + near[...].astype(f32) + far[...].astype(f32)

        def norm_body(tok, gains, keep, near, far, residual, normed):
            res = tok[...].astype(f32) + own_sum(keep, near, far)
            residual[...] = res
            normed[...] = (res * rms_scale(res) * gains[1:2, :]).astype(bf16)

        residual, normed_own = call(
            norm_body,
            (sds((T, D), f32), sds((T, D))),
            [VMEM] * 5,
            name="norm",
            after=(ffns[5], ffns[6]),
        )(tokens, gains, *scatter_rep(parts, after=(ffns[3], ffns[4]))[0])
        nffn = gather_rep(normed_own)

        def ffn_body(*refs):
            n_in, cot, pieces = refs[:4], refs[4:8], refs[8 : 8 + S]
            act_o, gg_o, gu_o, *parts, wd_o, wg, wu, sems = refs[8 + S :]
            _, _, _, z, y = place()
            pairs, late = [], []
            for p, piece in enumerate(pieces):
                s = from_shard(p, z, y)
                at = pl.ds(pl.multiple_of(s * n_d, n_d), n_d)
                at_f = pl.ds(pl.multiple_of(s * p_f, p_f), p_f)
                pairs.append((piece.at[pl.ds(f_rows[0], n_d)], wg.at[at]))
                pairs.append((piece.at[pl.ds(f_rows[1], n_d)], wu.at[at]))
                left = wd_o.at[at_f, pl.ds(0, F)]
                late.append((piece.at[pl.ds(f_rows[2], p_f)], left))
                for u in range(u_f):
                    block = piece.at[pl.ds(f_rows[3], p_f // u_f), pl.ds(u * w_f, w_f)]
                    n_u = p_f // u_f
                    at_u = pl.ds(pl.multiple_of(s * p_f + u * n_u, n_u), n_u)
                    late.append((block, wd_o.at[at_u, pl.ds(F, w_f)]))
            copies = [
                pltpu.make_async_copy(a, b, sems.at[i]) for i, (a, b) in enumerate(pairs + late)
            ]
            for copy in copies:
                copy.start()
            for copy in copies[: len(pairs)]:
                copy.wait()
            for j in range(R):
                n = n_in[j][...]
                gate = dot_nn(n, wg[...])
                up = dot_nn(n, wu[...])
                if j == 0:
                    for copy in copies[len(pairs) :]:
                        copy.wait()
                g_act = dot_nt(cot[j][...], wd_o[...])
                sig = jax.nn.sigmoid(gate)
                silu = gate * sig
                act_o[j] = (silu * up).astype(bf16)
                gg = (g_act * up * sig * (1.0 + gate * (1.0 - sig))).astype(bf16)
                gu = (g_act * silu).astype(bf16)
                gg_o[j], gu_o[j] = gg, gu
                back = dot_nt(gg, wg[...]) + dot_nt(gu, wu[...])
                parts[j][...] = back.astype(bf16)

        hid = sds((R, T, F))
        act, g_gate, g_up, *parts, wd = call(
            ffn_body,
            (hid, hid, hid, flat, flat, flat, flat, sds((F, D))),
            [VMEM] * 8 + [HBM] * S,
            [
                pltpu.VMEM((D, F), bf16),
                pltpu.VMEM((D, F), bf16),
                pltpu.SemaphoreType.DMA(((3 + u_f) * S,)),
            ],
            name="ffn",
        )(*nffn, *cots, *ffns)
        back, chip = scatter_rep(parts)

        def down_body(act, c0, c1, c2, c3, out):
            cot = jnp.concatenate([c0[...], c1[...], c2[...], c3[...]], 0)
            full = dot_tn(act[...].reshape(R * T, F), cot).astype(bf16)
            out[...] = full.reshape(Z, 2 * p_f, D)

        def hidden_body(n0, n1, n2, n3, gg, gu, mine, give, full):
            y = place()[4]
            n_all = jnp.concatenate([n0[...], n1[...], n2[...], n3[...]], 0)
            for i, grad in enumerate((gg, gu)):
                full[...] = dot_tn(n_all, grad[...].reshape(R * T, F)).astype(bf16)
                for k in range(Z):
                    for b, out in enumerate((mine, give)):
                        s = 2 * k + (y if b == 0 else 1 - y)
                        rows = full[pl.ds(pl.multiple_of(s * n_d, n_d), n_d), :]
                        out[k, i * n_d : (i + 1) * n_d] = rows

        piece = sds((Z, 2 * n_d, F))
        (m_h, e_h), t_hid = call(
            hidden_body,
            (piece, piece),
            [VMEM] * 6,
            [pltpu.VMEM((D, F), bf16)],
            name="ghid",
            after=(chip,),
            token=True,
        )(*nffn, g_gate, g_up)
        g_down, t_down = call(
            down_body, sds((Z, 2 * p_f, D)), [VMEM] * 5, name="gdown", token=True
        )(act, *cots)
        moved_d = swap_z(g_down)

        def part_body(act, wd, *parts):
            for j in range(R):
                parts[j][...] = dot_nn(act[j], wd[...]).astype(bf16)

        def back_norm(ins, grad, gain):
            scale = rms_scale(ins)
            u = grad * gain
            return scale * u - ins * scale**3 * jnp.mean(u * ins, axis=-1, keepdims=True)

        def res_body(cot, res, gains, keep, near, far, g_res, g_attn):
            grad = back_norm(res[...], own_sum(keep, near, far), gains[1:2, :])
            grad = cot[...].astype(f32) + grad
            g_res[...] = grad
            g_attn[...] = grad.astype(bf16)

        (grad_res, g_attn), t_res = call(
            res_body,
            (sds((T, D), f32), flat),
            [LOAD, LOAD, VMEM, LOAD, VMEM, VMEM],
            name="gres",
            after=(t_down, t_hid),
            token=True,
        )(cotangent, residual, gains, *back)
        part, t_part = call(
            part_body, (flat,) * R, [VMEM, LOAD], name="part", after=(t_res,), token=True
        )(act, wd)
        out_back, out_chip = scatter_rep(part, after=(t_res,))

        def out_body(res, keep, near, far, out):
            out[...] = (res[...] + own_sum(keep, near, far)).astype(bf16)

        output, t_out = call(
            out_body, flat, [LOAD, LOAD, VMEM, VMEM], name="outsum", token=True
        )(residual, *out_back)

        def attn_back_body(first, g0, g1, q_s, k_s, v_s, wk, wv, wo, gq_o, gk_o, gv_o, gl_o):
            for j, ga in enumerate((g0, g1)):
                gm = dot_nn(ga[...], wo[...]).astype(bf16)
                q, k, v = q_s[first + j], k_s[first + j], v_s[first + j]
                for h in range(0, q_c, 2 * HD):
                    cols = slice(h, h + 2 * HD)
                    qq, kk, vv, gg = q[:, cols], k[:, cols], v[:, cols], gm[:, cols]
                    gqs, gks, gvs = [], [], []
                    for qm, gmm in zip(halves(qq), halves(gg)):
                        probs = softmax_block(qm, kk)
                        gp = dot_nt(gmm, vv)
                        gs = probs * (gp - jnp.sum(probs * gp, axis=-1, keepdims=True))
                        gs = gs.astype(bf16)
                        gqs.append(dot_nn(gs, kk))
                        gks.append(dot_tn(gs, qq))
                        gvs.append(dot_tn(probs.astype(bf16), gg))
                    gq_o[j, :, cols] = (join(*gqs) * HD**-0.5).astype(bf16)
                    gk_o[j, :, cols] = (join(*gks) * HD**-0.5).astype(bf16)
                    gv_o[j, :, cols] = join(*gvs).astype(bf16)
                gl_o[j] = (dot_nt(gk_o[j], wk[...]) + dot_nt(gv_o[j], wv[...])).astype(bf16)

        def attn_back(first, grads, after):
            pair = sds((2, T, q_c))
            return call(
                functools.partial(attn_back_body, first),
                (pair,) * 4,
                [VMEM] * 8,
                name="attnback",
                after=after,
                token=True,
            )(*grads, q_s, k_s, v_s, wk, wv, wo)

        near = (g_attn, flip_core(g_attn))
        near_back, t_near = attn_back(0, near, (t_part, out_chip))
        far = hold(flip_x(g_attn), (t_near,))
        far = (far, flip_core(far))
        far_back, t_far = attn_back(2, far, ())
        g_attns = near + far

        def weights_body(*refs):
            ga, near, far, (mixed, lat_s, normed) = refs[:R], refs[4:8], refs[8:12], refs[12:15]
            mine, give, f_wide, f_low = refs[15:]
            _, _, _, z, y = place()
            gq, gk, gv, gl = (
                jnp.concatenate([a[...], b[...]], 0).reshape(R * T, q_c) for a, b in zip(near, far)
            )
            n_all = normed[...].reshape(R * T, D)
            lat = lat_s[...].reshape(R * T, LAT)
            g_all = jnp.concatenate([g[...] for g in ga], 0)
            f_wide[0] = dot_tn(n_all, gq).astype(bf16)
            f_wide[1] = dot_tn(n_all, gl).astype(bf16)
            f_wide[2] = dot_tn(g_all, mixed[...].reshape(R * T, q_c)).astype(bf16)
            f_low[0] = dot_tn(lat, gk).astype(bf16)
            f_low[1] = dot_tn(lat, gv).astype(bf16)
            for k in range(Z):
                for b, out in enumerate((mine, give)):
                    s = to_shard(k, b, z, y)
                    at_d = pl.ds(pl.multiple_of(s * n_d, n_d), n_d)
                    at_l = pl.ds(pl.multiple_of(s * n_l, n_l), n_l)
                    out[k, cuts[0] : cuts[1]] = f_wide[0, at_d, :]
                    out[k, cuts[1] : cuts[2]] = f_wide[1, at_d, :]
                    out[k, cuts[2] : cuts[3]] = f_low[0, at_l, :]
                    out[k, cuts[3] : cuts[4]] = f_low[1, at_l, :]
                    out[k, cuts[4] : cuts[5]] = f_wide[2, at_d, :]

        got_h = flip_y(e_h)
        half_h, t_half = half_sum(m_h, got_h, "hid", False, after=(t_far,))
        piece = sds((Z, cuts[5], q_c))
        (m_p, e_p), t_back = call(
            weights_body,
            (piece, piece),
            [VMEM] * 15,
            [pltpu.VMEM((3, D, q_c), bf16), pltpu.VMEM((2, LAT, q_c), bf16)],
            name="wback",
            after=(t_half,),
            token=True,
        )(*g_attns, *near_back, *far_back, mixed, lat_s, normed)

        def down_sum_body(parts, mine, give):
            y = place()[4]
            total = parts[0].astype(f32)
            for k in range(1, Z):
                total = total + parts[k].astype(f32)
            low, high = total[:p_f], total[p_f:]
            mine[...] = jnp.where(y == 0, low, high).astype(bf16)
            give[...] = jnp.where(y == 0, high, low).astype(bf16)

        slab = sds((p_f, D))
        (mine_d, give_d), t_dsum = call(
            down_sum_body, (slab, slab), [VMEM], name="dsum", after=(t_half,), token=True
        )(moved_d)
        own_d = (mine_d.astype(f32) + flip_y(give_d).astype(f32)).astype(bf16)
        sum_dn = gather_rep(own_d)

        def in_body(gq0, gl0, gq1, gl1, wq, wl, *parts):
            for j, (gq, gl) in enumerate(((gq0, gl0), (gq1, gl1))):
                for i in range(2):
                    back = dot_nt(gq[i], wq[...]) + dot_nt(gl[i], wl[...])
                    parts[2 * j + i][...] = back.astype(bf16)

        got_p = flip_y(e_p)
        ins_part, t_in = call(
            in_body, (flat,) * R, [VMEM] * 4 + [LOAD] * 2, name="inback", after=(t_back,), token=True
        )(near_back[0], near_back[3], far_back[0], far_back[3], wq, wl)
        half_p, t_pack = half_sum(m_p, got_p, "pack", True, after=(t_half, t_in, t_out, t_dsum))
        ins_back = scatter_rep(ins_part, after=(t_pack,))[0]

        def tok_body(tok, g_res, gains, keep, near, far, out):
            grad = back_norm(tok[...].astype(f32), own_sum(keep, near, far), gains[0:1, :])
            out[...] = (g_res[...] + grad).astype(bf16)

        grad_tokens, t_tok = call(
            tok_body, flat, [LOAD, LOAD, VMEM, LOAD, VMEM, VMEM], name="gtok", token=True
        )(
            tokens, grad_res, gains, *ins_back
        )

        own_h, t_sum = part_sum([swap_z(half_h)], "hid", after=(t_pack, t_tok))
        own_p, _ = part_sum(turn_z(half_p), "pack", after=(t_sum,))
        sum_h = gather_rep(own_h)
        sum_p = gather_rep(own_p)

        def lane_sum(v):
            total = v[:, :128]
            for j in range(128, v.shape[1], 128):
                total = total + v[:, j : j + 128]
            return jnp.sum(total.T, axis=0, keepdims=True)

        def final_hidden_body(*refs):
            d_in, (v0, v1, v2, v3, w_g, w_u, nf, out_d, out_g, out_u, dots) = refs[:R], refs[R:]
            r, x, c, _, _ = place()
            for k, d in enumerate(d_in):
                q = lax.bitwise_xor(r, k)
                out_d[pl.ds(pl.multiple_of(q * n_f, 8), n_f), :] = d[...].astype(f32)[:n_f]
            total = 0.0
            for i, (w, out) in enumerate(((w_g, out_g), (w_u, out_u))):
                vs = [v[i * n_d : (i + 1) * n_d].astype(f32) for v in (v0, v1, v2, v3)]
                vs = [jnp.where(c == 1, vs[k ^ 1], vs[k]) for k in range(R)]
                vs = [jnp.where(x == 1, vs[k ^ 2], vs[k]) for k in range(R)]
                for q in range(R):
                    for s in range(S):
                        at = s * R * n_f + q * n_f
                        out[:, at : at + n_f] = vs[q][:, s * p_f : s * p_f + n_f]
                total = total + lane_sum(out[...] * w[...].astype(f32))
            dots[...] = total / nf[...].astype(f32)

        row = sds((1, n_d), f32)
        wide = sds((n_d, FF), f32)
        (g_down, g_gate_w, g_up_w, g_nf), t_hid = call(
            final_hidden_body,
            (sds((R * n_f, D), f32), wide, wide, row),
            [VMEM] * (2 * R) + [LOAD] * 2 + [VMEM],
            name="fhid",
            token=True,
        )(*sum_dn, *sum_h, w_gate, w_up, norm_ffn.reshape(1, n_d))

        def final_pack_body(v0, v1, v2, v3, w_q, w_l, na, gq, gl, gk, gv, go, gna):
            r, x, _, _, _ = place()
            vs = (v0, v1, v2, v3)
            for k, v in enumerate(vs):
                q = lax.bitwise_xor(r, k)
                wide = pl.ds(pl.multiple_of(q * q_c, q_c), q_c)
                part = pl.ds(pl.multiple_of((q % 2) * q_c, q_c), q_c)
                gq[:, wide] = v[cuts[0] : cuts[1]].astype(f32)
                gk[q // 2, :, part] = v[cuts[2] : cuts[3]].astype(f32)
                gv[q // 2, :, part] = v[cuts[3] : cuts[4]].astype(f32)
                go[wide, :] = v[cuts[4] : cuts[5]].astype(f32).T
            for k in (0, 2):
                g = lax.bitwise_xor(x, k // 2)
                both = vs[k][cuts[1] : cuts[2]].astype(f32) + vs[k + 1][cuts[1] : cuts[2]].astype(f32)
                gl[:, pl.ds(pl.multiple_of(g * LAT, LAT), LAT)] = both
            dots = lane_sum(gq[...] * w_q[...].astype(f32)) + lane_sum(gl[...] * w_l[...].astype(f32))
            gna[...] = dots / na[...].astype(f32)

        g_query, g_latent, g_key, g_value, g_out, g_na = call(
            final_pack_body,
            (
                sds((n_d, R * q_c), f32),
                sds((n_d, LG * LAT), f32),
                sds((LG, n_l, 2 * q_c), f32),
                sds((LG, n_l, 2 * q_c), f32),
                sds((R * q_c, n_d), f32),
                row,
            ),
            [VMEM] * R + [LOAD] * 2 + [VMEM],
            name="fpack",
            after=(t_hid, t_out, t_tok),
        )(*sum_p, w_query, w_latent, norm_attn.reshape(1, n_d))
        return (
            output,
            grad_tokens,
            g_na.reshape(n_d),
            g_query,
            g_latent,
            g_key,
            g_value,
            g_out,
            g_nf.reshape(n_d),
            g_gate_w,
            g_up_w,
            g_down,
        )

    return layer


def make_layer(mesh):
    aligned = (LAT // mesh.shape["shard"]) % 16 == 0
    return make_fast(mesh) if aligned else make_plain(mesh)


def solution(mesh):
    return jax.shard_map(
        make_layer(mesh),
        mesh=mesh,
        in_specs=(
            P(("rep", "shard"), None),
            P("shard"),
            P("shard", None),
            P("shard", None),
            P(None, "shard", None),
            P(None, "shard", None),
            P(None, "shard"),
            P("shard"),
            P("shard", None),
            P("shard", None),
            P("shard", None),
            P(("rep", "shard"), None),
        ),
        out_specs=(
            P(("rep", "shard"), None),
            P(("rep", "shard"), None),
            P("shard"),
            P("shard", None),
            P("shard", None),
            P(None, "shard", None),
            P(None, "shard", None),
            P(None, "shard"),
            P("shard"),
            P("shard", None),
            P("shard", None),
            P("shard", None),
        ),
        check_vma=False,
    )
```
